128 devices in a mesh: frame: 8 (over z, y_hi), spatial: 4 (over x), dp: 4 (over y_lo, core).
Axes of the slice: x: 4, y: 4 (y_hi: 2, y_lo: 2; y = y_hi * 2 + y_lo), z: 4, core: 2. Of those that a mesh axis runs over, the one named last changes fastest.
Arguments:
- tokens: bfloat16 [4, 8, 48, 80, 3072], P('dp', 'frame', 'spatial'), may hold values from -6 to 6
- xz_weight: bfloat16 [3072, 3072], P(('spatial', 'dp')), may hold values from -0.109375 to 0.109375
- state_weight: bfloat16 [3072, 256], P(('spatial', 'dp')), may hold values from -0.109375 to 0.109375
- step_weight: bfloat16 [3072, 24], P(('spatial', 'dp')), may hold values from -0.109375 to 0.109375
- step_bias: float32 [24], replicated, may hold values from -1 to 1
- decay_rate: float32 [2, 24], replicated, may hold values from 0 to 1, as said below
- skip: float32 [2, 24], replicated, may hold values from 0.5 to 1.5
- norm_gain: float32 [1536], replicated, may hold values from 0.5 to 1.5
Outputs:
- mixed: bfloat16 [4, 8, 48, 80, 1536], P('dp', 'frame', 'spatial')
The draws below stay inside these ranges and needn't reach their ends.
Inputs may be any that keep to these rules, and one draw needn't show every extreme that they name: `decay_rate`: positive decay rates, one per direction and head.
All inputs are finite; a program needn't handle non-finite values.
Results may differ from the reference program's by a relative error of at most 0.0013.
Values may be sent and summed in bfloat16 or wider, within the bound.
A program may use at most 256 MiB of HBM per device.

```python
import jax
import jax.numpy as jnp
from jax import lax

D = 3072
HEADS = 24
HEAD_DIM = 64
STATE = 128
ROWS = 48
COLS = 80
INNER = 1536
VIDEOS = 4
FRAMES = 8


def draw_decay_rate(key, part):
    key = jax.random.fold_in(key, 7)
    pick_key, slow_key, fast_key = jax.random.split(key, 3)
    length = FRAMES * ROWS * COLS
    share = 0.5
    slow = jax.random.uniform(pick_key, (2, HEADS), jnp.float32) < share
    slow_rate = jnp.exp(jax.random.uniform(slow_key, (2, HEADS), jnp.float32, jnp.log(0.1 / length), jnp.log(2.0 / length)))
    fast_rate = jnp.exp(jax.random.uniform(fast_key, (2, HEADS), jnp.float32, jnp.log(1.0 / 40.0), jnp.log(1.0 / 15.0)))
    return jnp.where(slow, slow_rate, fast_rate).astype(jnp.float32)


def level_of(stream_key, extent, cuts, least, high):
    loudness = 1.0
    for position, parts in cuts:
        draws = jax.random.uniform(jax.random.fold_in(jax.random.fold_in(stream_key, 6), position), (parts,), jnp.float32, least / len(cuts), high / len(cuts))
        loudness = loudness * jnp.repeat(jnp.exp(draws), extent[position] // parts).reshape((-1,) + (1,) * (len(extent) - 1 - position))
    return loudness


def normal_values(own_key, dims, spread, most, cuts=(), dtype=jnp.bfloat16):
    drawn = jax.random.normal(own_key, dims, jnp.float32) * spread
    if len(cuts) > 0:
        drawn = level_of(own_key, dims, cuts, -0.22, 0.18) * drawn
    return jnp.clip(drawn, min=-most, max=most).astype(dtype)


def setup_inputs(seed: int = 0) -> dict:
    keys = jax.random.split(jax.random.key(seed), 9)
    return {
        "tokens": normal_values(keys[0], (VIDEOS, FRAMES, ROWS, COLS, D), 1.0, 6.0, ((0, 4), (1, 8), (2, 4))),
        "xz_weight": normal_values(keys[1], (D, 2 * INNER), D ** -0.5, 0.109375, ((0, 16),)),
        "state_weight": normal_values(keys[2], (D, 2 * STATE), D ** -0.5, 0.109375, ((0, 16),)),
        "step_weight": normal_values(keys[3], (D, HEADS), D ** -0.5, 0.109375, ((0, 16),)),
        "step_bias": jnp.clip(jax.random.uniform(keys[4], (HEADS,), jnp.float32, -1.0, 1.0), -1.0, 1.0),
        "decay_rate": draw_decay_rate(jax.random.fold_in(keys[8], 71), 0),
        "skip": jnp.clip(jax.random.uniform(keys[6], (2, HEADS), jnp.float32, 0.5, 1.5), 0.5, 1.5),
        "norm_gain": jnp.clip(1.0 + 0.1 * jax.random.normal(keys[7], (INNER,), jnp.float32), 0.5, 1.5),
    }


HIGHEST = lax.Precision.HIGHEST

def block_number(length):
    number = 1
    while length // number > 512 and length % (number * 2) == 0:
        number = number * 2
    return number

def block_step(memory, pieces, decay_rate):
    value_rows, key_rows, query_rows, step_rows = pieces
    logs_block = -step_rows * decay_rate[None, :]
    running = jnp.cumsum(logs_block, axis=0)
    positions = jnp.arange(value_rows.shape[0])
    causal = positions[:, None] >= positions[None, :]
    between = running[:, None, :] - running[None, :, :]
    decays = jnp.exp(jnp.where(causal[:, :, None], between, -jnp.inf))
    scores = jnp.dot(query_rows, key_rows.T, precision=HIGHEST, preferred_element_type=jnp.float32)
    scaled = value_rows * step_rows[:, :, None]
    within = jnp.einsum('tsh,shp->thp', decays * scores[:, :, None], scaled, precision=HIGHEST)
    carried = jnp.einsum('tn,hpn->thp', query_rows, memory, precision=HIGHEST) * jnp.exp(running)[:, :, None]
    final_log = running[-1]
    weighted = scaled * jnp.exp(final_log[None, :] - running)[:, :, None]
    new_memory = jnp.exp(final_log)[:, None, None] * memory + jnp.einsum('shp,sn->hpn', weighted, key_rows, precision=HIGHEST)
    return (new_memory, within + carried)

def run_sequence(value_rows, key_rows, query_rows, step_rows, decay_rate, memory):
    length = value_rows.shape[0]
    number = block_number(length)

    def blocked(source):
        return source.reshape((number, length // number) + source.shape[1:])

    def advance(previous, pieces):
        return block_step(previous, pieces, decay_rate)
    memory, outputs = lax.scan(advance, memory, (blocked(value_rows), blocked(key_rows), blocked(query_rows), blocked(step_rows)))
    return (outputs.reshape((length,) + outputs.shape[2:]), memory)

def to_columns(source, frames, rows_grid, cols_grid):
    shaped = source.reshape((frames, rows_grid, cols_grid) + source.shape[1:])
    return jnp.swapaxes(shaped, 1, 2).reshape(source.shape)[::-1]

def from_columns(source, frames, rows_grid, cols_grid):
    shaped = source[::-1].reshape((frames, cols_grid, rows_grid) + source.shape[1:])
    return jnp.swapaxes(shaped, 1, 2).reshape(source.shape)

def reference(tokens, xz_weight, state_weight, step_weight, step_bias, decay_rate, skip, norm_gain):

    def one_video(clip_tokens):
        flattened = clip_tokens.reshape(-1, D)
        projected = jnp.dot(flattened, xz_weight, preferred_element_type=jnp.float32)
        gate_rows = projected[:, :INNER]
        value_rows = projected[:, INNER:].reshape(-1, HEADS, HEAD_DIM)
        state_rows = jnp.dot(flattened, state_weight, preferred_element_type=jnp.float32)
        key_rows = state_rows[:, :STATE]
        query_rows = state_rows[:, STATE:]
        step_rows = jax.nn.softplus(jnp.dot(flattened, step_weight, preferred_element_type=jnp.float32) + step_bias)
        empty_state = jnp.zeros((HEADS, HEAD_DIM, STATE), jnp.float32)
        forward_out, forward_memory = run_sequence(value_rows, key_rows, query_rows, step_rows, decay_rate[0], empty_state)
        forward_out = forward_out + skip[0][None, :, None] * value_rows

        def reorder(source):
            return to_columns(source, FRAMES, ROWS, COLS)
        backward_out, backward_memory = run_sequence(reorder(value_rows), reorder(key_rows), reorder(query_rows), reorder(step_rows), decay_rate[1], empty_state)
        backward_out = from_columns(backward_out, FRAMES, ROWS, COLS) + skip[1][None, :, None] * value_rows
        combined = forward_out + backward_out
        gated = combined * jax.nn.silu(gate_rows).reshape(-1, HEADS, HEAD_DIM)
        inverse_rms = lax.rsqrt(lax.optimization_barrier(jnp.mean(gated * gated, axis=-1, keepdims=True)) + 1e-05)
        normed = (gated * inverse_rms).reshape(-1, INNER) * norm_gain
        return normed.astype(jnp.bfloat16).reshape(FRAMES, ROWS, COLS, INNER)
    return lax.map(one_video, tokens)
```

```python
import functools

import jax
import jax.numpy as jnp
from jax import lax
from jax.experimental import pallas as pl
from jax.experimental.pallas import tpu as pltpu
from jax.sharding import PartitionSpec as P

F32 = jnp.float32
BF16 = jnp.bfloat16
LANES = 128
GROUP = 4
VMEM_BYTES = 56 * 1024 * 1024


def split(value):
    high = value.astype(BF16)
    return high, (value - high.astype(F32)).astype(BF16)


def dot(a, b):
    return lax.dot_general(a, b, (((1,), (0,)), ((), ())), preferred_element_type=F32)


def rows_iota(shape):
    return lax.broadcasted_iota(jnp.int32, shape, 0)


def lanes_iota(shape):
    return lax.broadcasted_iota(jnp.int32, shape, 1)


def spread(columns, pair, head_size):
    first, second = columns[:, 2 * pair : 2 * pair + 1], columns[:, 2 * pair + 1 : 2 * pair + 2]
    shape = (columns.shape[0], LANES)
    return jnp.where(lanes_iota(shape) < head_size, first, second)


def params(semantics=("arbitrary",)):
    return pltpu.CompilerParams(vmem_limit_bytes=VMEM_BYTES, dimension_semantics=semantics)


def regroup_kernel(inner, state_columns, source_ref, bias_ref, mid_ref, steps_ref):
    step_lanes = pl.ds(inner + state_columns, LANES)
    raw = source_ref[:, step_lanes] + bias_ref[...]
    steps = jnp.maximum(raw, 0.0) + jnp.log1p(jnp.exp(-jnp.abs(raw)))
    steps_ref[...] = steps
    col_total = source_ref.shape[0] // 2
    wide = inner + state_columns

    def move(lower, upper, at, lanes):
        low = rows_iota(lower.shape) < GROUP
        mid_ref[2 * at, :, lanes] = jnp.where(low, lower, pltpu.roll(upper, GROUP, 0))
        mid_ref[2 * at + 1, :, lanes] = jnp.where(low, pltpu.roll(lower, GROUP, 0), upper)

    for at in range(col_total // 8):
        lower, upper = pl.ds(8 * at, 8), pl.ds(col_total + 8 * at, 8)
        move(source_ref[lower, :wide], source_ref[upper, :wide], at, pl.ds(0, wide))
        move(
            steps[8 * at : 8 * at + 8],
            steps[col_total + 8 * at : col_total + 8 * at + 8],
            at,
            step_lanes,
        )


def regroup(projected, bias, row_part, col_total, inner, state_columns):
    width = projected.shape[1]
    tokens = row_part * col_total
    groups = col_total // GROUP
    block = 2 * col_total
    return pl.pallas_call(
        functools.partial(regroup_kernel, inner, state_columns),
        grid=(row_part // 2,),
        in_specs=[
            pl.BlockSpec((block, width), lambda m: (m, 0)),
            pl.BlockSpec((1, LANES), lambda m: (0, 0)),
        ],
        out_specs=[
            pl.BlockSpec((groups, 2 * GROUP, width), lambda m: (0, m, 0)),
            pl.BlockSpec((block, LANES), lambda m: (m, 0)),
        ],
        out_shape=[
            jax.ShapeDtypeStruct((groups, row_part * GROUP, width), F32),
            jax.ShapeDtypeStruct((tokens, LANES), F32),
        ],
        compiler_params=params(),
    )(projected, bias)


def earlier_mask(size, column_rows):
    shape = (size, size)
    t, s = rows_iota(shape), lanes_iota(shape)
    if column_rows:

        def place(index):
            return size - 1 - (lax.rem(index, GROUP) * column_rows + index // GROUP)

        t, s = place(t), place(s)
    return s <= t


def running_logs(steps, rate, earlier):
    logs = -steps * rate
    high, rest = split(logs)
    middle = logs - high.astype(F32)
    middle, low = split(middle)
    before = jnp.where(earlier, 1.0, 0.0).astype(BF16)
    running = dot(before, high) + dot(before, middle) + dot(before, low)
    return running, jnp.sum(logs, axis=0, keepdims=True)


def advance(memory, keys_t, weighted, decay):
    keys_high, keys_low = keys_t
    high, low = split(weighted)
    both = dot(keys_high, jnp.concatenate([high, low], axis=1))
    added = both[:, :LANES] + both[:, LANES:] + dot(keys_low, high)
    return memory * decay + added


def state_kernel(
    column_rows, head_size, values_ref, keys_ref, steps_ref, rate_ref, memory_ref, decay_ref
):
    size = values_ref.shape[0] * values_ref.shape[1]
    pairs = values_ref.shape[2] // LANES

    @pl.when(pl.program_id(0) == 0)
    def _():
        memory_ref[...] = jnp.zeros_like(memory_ref)
        decay_ref[...] = jnp.ones_like(decay_ref)

    steps = steps_ref[...].reshape(size, LANES)
    keys_t = split(jnp.transpose(keys_ref[...].reshape(size, LANES)))
    running, total = running_logs(steps, rate_ref[...], earlier_mask(size, column_rows))
    coefficient = steps * jnp.exp(jnp.minimum(total - running, 0.0))
    decay = jnp.exp(total)
    for pair in range(pairs):
        lanes = pl.ds(pair * LANES, LANES)
        weighted = values_ref[:, :, lanes].reshape(size, LANES) * spread(coefficient, pair, head_size)
        pair_decay = spread(decay, pair, head_size)
        memory_ref[:, lanes] = advance(memory_ref[:, lanes], keys_t, weighted, pair_decay)
        decay_ref[pl.ds(pair, 1), :] = decay_ref[pl.ds(pair, 1), :] * pair_decay


def output_kernel(
    column_rows,
    head_size,
    values_ref,
    keys_ref,
    queries_ref,
    steps_ref,
    rate_ref,
    skip_ref,
    entering_ref,
    out_ref,
    memory_ref,
):
    size = values_ref.shape[0] * values_ref.shape[1]
    pairs = values_ref.shape[2] // LANES

    @pl.when(pl.program_id(0) == 0)
    def _():
        memory_ref[...] = entering_ref[...]

    steps = steps_ref[...].reshape(size, LANES)
    keys = keys_ref[...].reshape(size, LANES)
    keys_t = split(jnp.transpose(keys))
    queries_high, queries_low = split(queries_ref[...].reshape(size, LANES))
    earlier = earlier_mask(size, column_rows)
    running, total = running_logs(steps, rate_ref[...], earlier)
    across = jnp.transpose(running)
    scores = dot(queries_high, keys_t[0]) + dot(queries_high, keys_t[1]) + dot(queries_low, keys_t[0])
    scores = jnp.where(earlier, scores, 0.0)
    arrived = jnp.exp(running)
    leaving = jnp.exp(jnp.minimum(total - running, 0.0))
    decay = jnp.exp(total)
    first_half = lanes_iota((size, LANES)) < head_size
    for pair in range(pairs):
        lanes = pl.ds(pair * LANES, LANES)
        values = values_ref[:, :, lanes].reshape(size, LANES)
        scaled = values * spread(steps, pair, head_size)
        high, low = split(scaled)
        both = jnp.concatenate([high, low], axis=1)
        halves = []
        for head in (2 * pair, 2 * pair + 1):
            between = jnp.minimum(running[:, head : head + 1] - across[head : head + 1, :], 0.0)
            kernel_high, kernel_low = split(jnp.exp(between) * scores)
            part = dot(kernel_high, both)
            halves.append(part[:, :LANES] + part[:, LANES:] + dot(kernel_low, high))
        memory = memory_ref[:, lanes]
        memory_high, memory_low = split(memory)
        part = dot(queries_high, jnp.concatenate([memory_high, memory_low], axis=1))
        carried = part[:, :LANES] + part[:, LANES:] + dot(queries_low, memory_high)
        result = jnp.where(first_half, halves[0], halves[1])
        result = result + carried * spread(arrived, pair, head_size)
        if skip_ref is not None:
            result = result + values * skip_ref[:, lanes]
        out_ref[:, :, lanes] = result.reshape(out_ref.shape[0], out_ref.shape[1], LANES)
        weighted = scaled * spread(leaving, pair, head_size)
        memory_ref[:, lanes] = advance(memory, keys_t, weighted, spread(decay, pair, head_size))


def plain_output_kernel(column_rows, head_size, values_ref, keys_ref, queries_ref, steps_ref, rate_ref, *rest):
    output_kernel(
        column_rows, head_size, values_ref, keys_ref, queries_ref, steps_ref, rate_ref, None, *rest
    )


def chunk_specs(source, steps, inner, size, backward):
    pieces, length = source.shape[0], source.shape[1]
    part = size // pieces
    count = length // part

    def spec(lane_count, lane_block):
        def index(j):
            return (0, count - 1 - j if backward else j, lane_block)

        return pl.BlockSpec((pieces, part, lane_count), index)

    first = inner // LANES
    step_spec = spec(LANES, first + 2 if steps is None else 0)
    return count, spec(inner, 0), spec(LANES, first), spec(LANES, first + 1), step_spec


def whole(shape):
    return pl.BlockSpec(shape, lambda j: (0,) * len(shape))


def local_state(source, steps, rate, inner, size, column_rows, head_size):
    count, values, keys, _, step_spec = chunk_specs(source, steps, inner, size, column_rows > 0)
    pad = 16
    return pl.pallas_call(
        functools.partial(state_kernel, column_rows, head_size),
        grid=(count,),
        in_specs=[values, keys, step_spec, whole((1, LANES))],
        out_specs=[whole((LANES, inner)), whole((pad, LANES))],
        out_shape=[
            jax.ShapeDtypeStruct((LANES, inner), F32),
            jax.ShapeDtypeStruct((pad, LANES), F32),
        ],
        compiler_params=params(),
    )(source, source, source if steps is None else steps, rate)


def local_output(source, steps, rate, skip, entering, inner, size, column_rows, head_size):
    count, values, keys, queries, step_spec = chunk_specs(
        source, steps, inner, size, column_rows > 0
    )
    body = plain_output_kernel if skip is None else output_kernel
    skip_specs = [] if skip is None else [whole((1, inner))]
    skip_args = [] if skip is None else [skip]
    return pl.pallas_call(
        functools.partial(body, column_rows, head_size),
        grid=(count,),
        in_specs=[values, keys, queries, step_spec, whole((1, LANES))]
        + skip_specs
        + [whole((LANES, inner))],
        out_specs=values,
        out_shape=jax.ShapeDtypeStruct(source.shape[:2] + (inner,), F32),
        scratch_shapes=[pltpu.VMEM((LANES, inner), F32)],
        compiler_params=params(),
    )(source, source, source, source if steps is None else steps, rate, *skip_args, entering)


def prefix_kernel(reverse, rows, pairs, source_ref, out_ref):
    count = source_ref.shape[0]
    entering = jnp.zeros((rows, LANES), F32)
    for k in range(count):
        at = count - 1 - k if reverse else k
        out_ref[at] = entering
        decay = source_ref[at, pl.ds(rows, pairs), :]
        decay = jnp.concatenate([decay] * (rows // pairs), axis=0)
        entering = entering * decay + source_ref[at, pl.ds(0, rows), :]


def entering_state(memory, decay, axes, reverse):
    count = 1
    for axis in axes:
        count = count * lax.axis_size(axis)
    pairs = memory.shape[1] // LANES
    rows = memory.shape[0] * pairs // count
    sent = jnp.concatenate(
        [
            memory.reshape(count, rows, LANES),
            jnp.broadcast_to(decay[None], (count,) + decay.shape),
        ],
        axis=1,
    )
    received = lax.all_to_all(sent, axes, 0, 0, tiled=True)
    found = pl.pallas_call(
        functools.partial(prefix_kernel, reverse, rows, pairs),
        out_shape=jax.ShapeDtypeStruct((count, rows, LANES), F32),
        compiler_params=pltpu.CompilerParams(vmem_limit_bytes=VMEM_BYTES),
    )(received)
    returned = lax.all_to_all(found, axes, 0, 0, tiled=True)
    return returned.reshape(memory.shape)


def finish_kernel(head_size, forward_ref, backward_ref, gate_ref, gain_ref, out_ref, moved_ref):
    col_total = forward_ref.shape[0] // 2
    for at in range(col_total // 8):
        even, odd = backward_ref[2 * at], backward_ref[2 * at + 1]
        low = rows_iota(even.shape) < GROUP
        moved_ref[pl.ds(8 * at, 8), :] = jnp.where(low, even, pltpu.roll(odd, GROUP, 0))
        moved_ref[pl.ds(col_total + 8 * at, 8), :] = jnp.where(low, pltpu.roll(even, GROUP, 0), odd)
    wide = 2 * LANES
    same = rows_iota((wide, wide)) // head_size == lanes_iota((wide, wide)) // head_size
    ones = jnp.where(same, 1.0, 0.0).astype(BF16)
    for block in range(forward_ref.shape[1] // wide):
        lanes = pl.ds(block * wide, wide)
        gate = gate_ref[:, lanes]
        combined = forward_ref[:, lanes] + moved_ref[:, lanes]
        gated = combined * (gate / (1.0 + jnp.exp(-gate)))
        high, low = split(gated * gated)
        mean = (dot(high, ones) + dot(low, ones)) * (1.0 / head_size)
        normed = gated * lax.rsqrt(mean + 1e-5) * gain_ref[:, lanes]
        out_ref[:, lanes] = normed.astype(out_ref.dtype)


def finish(forward, backward, gate, gain, row_part, col_total, head_size):
    tokens, inner = forward.shape
    groups = col_total // GROUP
    block = 2 * col_total
    flat = pl.BlockSpec((block, inner), lambda m: (m, 0))
    return pl.pallas_call(
        functools.partial(finish_kernel, head_size),
        grid=(row_part // 2,),
        in_specs=[
            flat,
            pl.BlockSpec((groups, 2 * GROUP, inner), lambda m: (0, m, 0)),
            flat,
            pl.BlockSpec((1, inner), lambda m: (0, 0)),
        ],
        out_specs=flat,
        out_shape=jax.ShapeDtypeStruct((tokens, inner), BF16),
        scratch_shapes=[pltpu.VMEM((block, inner), F32)],
        compiler_params=params(),
    )(forward, backward, gate, gain)


def pad_lanes(source):
    return jnp.pad(source, ((0, 0), (0, LANES - source.shape[1])))


def local(tokens, xz_weight, state_weight, step_weight, step_bias, decay_rate, skip, norm_gain):
    videos, frame_count, row_part, col_total, width = tokens.shape
    flattened = tokens.reshape(-1, width)
    inner = xz_weight.shape[1] // 2
    state_columns = state_weight.shape[1]
    heads = step_weight.shape[1]
    head_size = inner // heads
    spatial = lax.axis_size("spatial")
    column_rows = row_part * spatial
    size = column_rows * GROUP

    first_part = jnp.concatenate([xz_weight[:, inner:], state_weight, pad_lanes(step_weight)], axis=1)
    first_weight = lax.all_gather(first_part, ("spatial", "dp"), axis=0, tiled=True)
    gate_weight = lax.all_gather(xz_weight[:, :inner], ("spatial", "dp"), axis=0, tiled=True)
    projected = jnp.dot(flattened, first_weight, preferred_element_type=F32)
    gate_rows = jnp.dot(flattened, gate_weight, preferred_element_type=F32)
    rates = pad_lanes(decay_rate)
    skips = jnp.repeat(skip[0] + skip[1], head_size)[None]

    mid, steps = regroup(
        projected, pad_lanes(step_bias[None]), row_part, col_total, inner, state_columns
    )
    full = projected.shape[1]
    columns = lax.all_to_all(
        mid.reshape(spatial, -1, full), "spatial", 0, 0, tiled=True
    )
    source = projected[None]
    steps = steps[None]
    axes = ("frame", "spatial")

    memory, decay = local_state(source, steps, rates[0:1], inner, size, 0, head_size)
    entering = entering_state(memory, decay, axes, False)
    forward = local_output(source, steps, rates[0:1], skips, entering, inner, size, 0, head_size)

    memory, decay = local_state(columns, None, rates[1:2], inner, size, column_rows, head_size)
    entering = entering_state(memory, decay, axes, True)
    backward = local_output(
        columns, None, rates[1:2], None, entering, inner, size, column_rows, head_size
    )
    returned = lax.all_to_all(backward, "spatial", 0, 0, tiled=True)
    returned = returned.reshape(col_total // GROUP, row_part * GROUP, inner)
    normed = finish(
        forward[0], returned, gate_rows, norm_gain[None], row_part, col_total, head_size
    )
    return normed.reshape(videos, frame_count, row_part, col_total, inner)


def solution(mesh):
    in_specs = (
        P("dp", "frame", "spatial", None, None),
        P(("spatial", "dp"), None),
        P(("spatial", "dp"), None),
        P(("spatial", "dp"), None),
        P(),
        P(),
        P(),
        P(),
    )
    out_specs = P("dp", "frame", "spatial", None, None)
    return jax.shard_map(local, mesh=mesh, in_specs=in_specs, out_specs=out_specs, check_vma=False)
```

```python
import functools

import jax
import jax.numpy as jnp
from jax import lax
from jax.experimental import pallas as pl
from jax.experimental.pallas import tpu as pltpu
from jax.sharding import PartitionSpec as P

F32 = jnp.float32
BF16 = jnp.bfloat16
LANES = 128
GROUP = 4
POWER = 17
CODE_TOP = 128.0
STEP_LANES = 24
MESH = pl.DeviceIdType.MESH
VMEM_BYTES = 56 * 1024 * 1024


def split(value):
    high = value.astype(BF16)
    return high, (value - high.astype(F32)).astype(BF16)


def dot(a, b):
    return lax.dot_general(a, b, (((1,), (0,)), ((), ())), preferred_element_type=F32)


def rows_iota(shape):
    return lax.broadcasted_iota(jnp.int32, shape, 0)


def lanes_iota(shape):
    return lax.broadcasted_iota(jnp.int32, shape, 1)


def spread(columns, pair, head_size):
    first, second = columns[:, 2 * pair : 2 * pair + 1], columns[:, 2 * pair + 1 : 2 * pair + 2]
    shape = (columns.shape[0], LANES)
    return jnp.where(lanes_iota(shape) < head_size, first, second)


def params(semantics=("arbitrary",)):
    return pltpu.CompilerParams(vmem_limit_bytes=VMEM_BYTES, dimension_semantics=semantics)


def encode(scaled):
    square = scaled * scaled
    fourth = square * square
    eighth = fourth * fourth
    return (eighth * eighth * scaled).astype(BF16)


def decode(coded):
    coded = coded.astype(F32)
    size = jnp.exp2(jnp.log2(jnp.abs(coded)) * (1.0 / POWER))
    return jnp.where(coded < 0.0, -size, size)


def code_scale(largest):
    scale = jnp.maximum(largest, 1e-30).astype(BF16)
    return scale, CODE_TOP / scale.astype(F32)


def column_groups(first, second):
    low = rows_iota(first.shape) < GROUP
    even = jnp.where(low, first, pltpu.roll(second, GROUP, 0))
    odd = jnp.where(low, pltpu.roll(first, GROUP, 0), second)
    return even, odd


def project_kernel(
    geometry,
    tokens_ref,
    state_ref,
    bias_ref,
    xz_ref,
    values_ref,
    keys_ref,
    columns_ref,
    weight,
    product,
    middle,
    own_sem,
    x_send,
    x_recv,
    y_send,
    y_recv,
    core_send,
    core_recv,
    move_send,
    move_recv,
    move_own,
    out_sem,
):
    row_part, col_total, inner, depth, blocks = geometry
    half = depth // 2
    frame, place, part = lax.axis_index("frame"), lax.axis_index("spatial"), lax.axis_index("dp")
    core, y = part % 2, (frame % 2) * 2 + part // 2
    right, left, across = (place + 1) % 4, (place + 3) % 4, (place + 2) % 4

    def y_device(other):
        return ((frame // 2) * 2 + other // 2, place, (other % 2) * 2 + core)

    x_right, x_left, x_across = (frame, right, part), (frame, left, part), (frame, across, part)
    y_up, y_down = y_device((y + 1) % 4), y_device((y + 3) % 4)
    partner = (frame, place, (part // 2) * 2 + 1 - core)

    barrier = pltpu.get_barrier_semaphore()
    peers = (x_right, x_left, x_across, y_up, y_down, partner)
    for peer in peers:
        pl.semaphore_signal(barrier, inc=1, device_id=peer, device_id_type=MESH)
    pl.semaphore_wait(barrier, len(peers))

    def slot(where, other_core, other_part):
        return where * 4 + other_part * 2 + other_core

    same, opposite = part // 2, 1 - part // 2
    sources = (place, left, right, across)

    def rows(index, first, count):
        return pl.ds(pl.multiple_of(index * depth + first, 16), count)

    def view(block, index, first, count):
        return weight.at[block, rows(index, first, count), pl.ds(0, blocks[block][1])]

    def own(block, first, count):
        start, width = blocks[block]
        if block == 0:
            return state_ref.at[pl.ds(first, count), :]
        return xz_ref.at[pl.ds(first, count), pl.ds(inner + start, width)]

    pending = []

    def send(source, target, send_sem, recv_sem, device):
        copy = pltpu.make_async_remote_copy(
            src_ref=source,
            dst_ref=target,
            send_sem=send_sem,
            recv_sem=recv_sem,
            device_id=device,
            device_id_type=MESH,
        )
        copy.start()
        pending.append(copy)

    def arrived(target, send_sem, recv_sem):
        pltpu.make_async_remote_copy(
            src_ref=target,
            dst_ref=target,
            send_sem=send_sem,
            recv_sem=recv_sem,
            device_id=x_right,
            device_id_type=MESH,
        ).wait_recv()

    def send_y(block, which, source_of):
        index = slot(sources[which], core, same)
        for part_at, device in ((0, y_up), (1, y_down)):
            first = part_at * half
            send(
                source_of(first),
                view(block, index, first, half),
                y_send.at[block, which, part_at],
                y_recv.at[block, which, part_at],
                device,
            )

    def send_core(block, at, index, source):
        send(
            source,
            view(block, index, 0, depth),
            core_send.at[block, at],
            core_recv.at[block, at],
            partner,
        )

    def send_own(block):
        index = slot(place, core, same)
        target = view(block, index, 0, depth)
        source = own(block, 0, depth)
        send(source, target, x_send.at[block, 0], x_recv.at[block, 0], x_right)
        send(source, target, x_send.at[block, 1], x_recv.at[block, 1], x_left)
        send_y(block, 0, lambda first: own(block, first, half))
        send_core(block, 0, index, source)
        copy = pltpu.make_async_copy(source, target, own_sem.at[block])
        copy.start()

    def relay(block):
        from_left, from_right = slot(left, core, same), slot(right, core, same)
        far = slot(across, core, same)
        for which, index in ((1, from_left), (2, from_right)):
            arrived(
                view(block, index, 0, depth),
                x_send.at[block, which - 1],
                x_recv.at[block, which - 1],
            )
            part_at = which - 1
            send(
                view(block, index, part_at * half, half),
                view(block, index, part_at * half, half),
                x_send.at[block, 2 + part_at],
                x_recv.at[block, 2 + part_at],
                (x_right, x_left)[part_at],
            )
            send_y(block, which, lambda first: view(block, index, first, half))
            send_core(block, which, index, view(block, index, 0, depth))
        for part_at in (0, 1):
            arrived(
                view(block, far, part_at * half, half),
                x_send.at[block, 2 + part_at],
                x_recv.at[block, 2 + part_at],
            )
        send_y(block, 3, lambda first: view(block, far, first, half))
        send_core(block, 3, far, view(block, far, 0, depth))

    def pass_on(block):
        for which in range(4):
            index = slot(sources[which], core, opposite)
            for part_at in (0, 1):
                arrived(
                    view(block, index, part_at * half, half),
                    y_send.at[block, which, part_at],
                    y_recv.at[block, which, part_at],
                )
            send_core(block, 4 + which, index, view(block, index, 0, depth))

    def gathered(block):
        for at in range(8):
            index = slot(sources[at % 4], 1 - core, same if at < 4 else opposite)
            arrived(
                view(block, index, 0, depth), core_send.at[block, at], core_recv.at[block, at]
            )
        index = slot(place, core, same)
        target = view(block, index, 0, depth)
        pltpu.make_async_copy(own(block, 0, depth), target, own_sem.at[block]).wait()

    tokens = row_part * col_total
    tile = tokens // 5
    groups = col_total // GROUP // 4
    piece_rows = groups * row_part * GROUP
    outs = {}

    def compute(block):
        start, width = blocks[block]
        lanes = pl.ds(0, width)
        buffer = block % 2
        if block - 2 in outs:
            outs.pop(block - 2).wait()

        def one_tile(i, largest):
            at = pl.ds(pl.multiple_of(i * tile, tile), tile)
            result = dot(tokens_ref[at, :], weight[block, :, lanes])
            if block == 0:
                raw = result[:, width - LANES :] + bias_ref[...]
                steps = jnp.maximum(raw, 0.0) + jnp.log1p(jnp.exp(-jnp.abs(raw)))
                result = jnp.concatenate([result[:, : width - LANES], steps], axis=1)
            product[buffer, at, lanes] = result
            return jnp.maximum(largest, jnp.max(jnp.abs(result), axis=0, keepdims=True))

        largest = lax.fori_loop(0, 5, one_tile, jnp.zeros((1, width), F32))
        if block == 0:
            out = keys_ref
        else:
            out = values_ref.at[:, pl.ds(start, width)]
        copy = pltpu.make_async_copy(product.at[buffer, :, lanes], out, out_sem.at[block])
        copy.start()
        outs[block] = copy

        scale, factor = code_scale(largest)

        def code(value):
            coded = encode(value * factor)
            if block == 0:
                exact = value[:, width - LANES :]
                high = exact.astype(BF16)
                rest = exact - high.astype(F32)
                second = rest.astype(BF16)
                third = (rest - second.astype(F32)).astype(BF16)
                lane = lanes_iota(exact.shape)
                heads = STEP_LANES
                parts = jnp.where(
                    lane < heads,
                    high.astype(F32),
                    jnp.where(lane < 2 * heads, second.astype(F32), third.astype(F32)),
                )
                coded = jnp.concatenate([coded[:, : width - LANES], parts.astype(BF16)], axis=1)
            return coded

        for quad in range(row_part // 4):

            def one_group(at, carry):
                both = []
                for pair in (2 * quad, 2 * quad + 1):
                    first = product[buffer, pl.ds(pl.multiple_of(2 * pair * col_total + 8 * at, 8), 8), lanes]
                    second = product[
                        buffer, pl.ds(pl.multiple_of((2 * pair + 1) * col_total + 8 * at, 8), 8), lanes
                    ]
                    both.append(column_groups(first, second))
                for odd in (0, 1):
                    group = 2 * at + odd
                    piece = group // groups
                    row = pl.multiple_of((group % groups) * row_part * GROUP + 16 * quad, 16)
                    value = jnp.concatenate([both[0][odd], both[1][odd]], axis=0)
                    middle[block, piece, pl.ds(row, 16), lanes] = code(value)
                return carry

            lax.fori_loop(0, col_total // 8, one_group, 0)
        for piece in range(4):
            middle[block, piece, pl.ds(piece_rows, 16), lanes] = jnp.broadcast_to(scale, (16, width))
        into = columns_ref.at[place, :, pl.ds(inner if block == 0 else start, width)]
        for at, (where, device) in enumerate(((right, x_right), (left, x_left), (across, x_across))):
            send(
                middle.at[block, where, :, lanes],
                into,
                move_send.at[block, at],
                move_recv.at[block, at],
                device,
            )
        pltpu.make_async_copy(middle.at[block, place, :, lanes], into, move_own.at[block]).start()

    count = len(blocks)
    send_own(0)
    send_own(1)
    relay(0)
    for block in range(count):
        if block + 2 < count:
            send_own(block + 2)
        if block + 1 < count:
            relay(block + 1)
        pass_on(block)
        gathered(block)
        compute(block)
    for block in range(count):
        start, width = blocks[block]
        lanes = pl.ds(0, width)
        for at, where in enumerate((left, right, across)):
            into = columns_ref.at[where, :, pl.ds(inner if block == 0 else start, width)]
            arrived(into, move_send.at[block, at], move_recv.at[block, at])
        into = columns_ref.at[place, :, pl.ds(inner if block == 0 else start, width)]
        pltpu.make_async_copy(middle.at[block, place, :, lanes], into, move_own.at[block]).wait()
    for copy in outs.values():
        copy.wait()
    for copy in pending:
        copy.wait_send()


def project(tokens, state_weight, bias, xz_weight, row_part, col_total, inner, block_width):
    depth, state_width = state_weight.shape
    count = inner // block_width + 1
    blocks = ((0, state_width),) + tuple((k * block_width, block_width) for k in range(count - 1))
    width = max(block_width, state_width)
    total = tokens.shape[0]
    piece_rows = total // 4 + 16
    vmem, hbm = pl.BlockSpec(memory_space=pltpu.VMEM), pl.BlockSpec(memory_space=pl.ANY)
    dma = pltpu.SemaphoreType.DMA
    return pl.pallas_call(
        functools.partial(project_kernel, (row_part, col_total, inner, depth, blocks)),
        in_specs=[vmem, vmem, vmem, hbm],
        out_specs=[hbm, hbm, hbm],
        out_shape=[
            jax.ShapeDtypeStruct((total, inner), F32),
            jax.ShapeDtypeStruct((total, state_width), F32),
            jax.ShapeDtypeStruct((4, piece_rows, inner + state_width), BF16),
        ],
        scratch_shapes=[
            pltpu.VMEM((count, tokens.shape[1], width), BF16),
            pltpu.VMEM((2, total, width), F32),
            pltpu.VMEM((count, 4, piece_rows, width), BF16),
            dma((count,)),
            dma((count, 4)),
            dma((count, 4)),
            dma((count, 4, 2)),
            dma((count, 4, 2)),
            dma((count, 8)),
            dma((count, 8)),
            dma((count, 3)),
            dma((count, 3)),
            dma((count,)),
            dma((count,)),
        ],
        compiler_params=pltpu.CompilerParams(
            collective_id=0, has_side_effects=True, vmem_limit_bytes=VMEM_BYTES
        ),
    )(tokens, state_weight, bias, xz_weight)


def earlier_mask(size, column_rows):
    shape = (size, size)
    t, s = rows_iota(shape), lanes_iota(shape)
    if column_rows:

        def place(index):
            return size - 1 - (lax.rem(index, GROUP) * column_rows + index // GROUP)

        t, s = place(t), place(s)
    return s <= t


def running_logs(steps, rate, earlier):
    logs = -steps * rate
    high, rest = split(logs)
    middle = logs - high.astype(F32)
    middle, low = split(middle)
    before = jnp.where(earlier, 1.0, 0.0).astype(BF16)
    running = dot(before, high) + dot(before, middle) + dot(before, low)
    return running, jnp.sum(logs, axis=0, keepdims=True)


def advance(memory, keys_t, weighted, decay):
    keys_high, keys_low = keys_t
    high, low = split(weighted)
    both = dot(keys_high, jnp.concatenate([high, low], axis=1))
    added = both[:, :LANES] + both[:, LANES:] + dot(keys_low, high)
    return memory * decay + added


class Chunk:
    def __init__(self, column_rows, values_ref, keys_ref, steps_ref, scale_ref):
        self.size = values_ref.shape[0] * values_ref.shape[1]
        self.inner = values_ref.shape[2]
        self.pairs = self.inner // LANES
        self.column_rows, self.values_ref, self.scale_ref = column_rows, values_ref, scale_ref
        self.keys_ref, self.steps_ref = keys_ref, steps_ref
        if column_rows:
            self.scales = [scale_ref[k, pl.ds(0, 16), :].astype(F32)[0:1] for k in range(4)]

    def read(self, ref, lanes, scale_lane):
        block = ref[:, :, lanes]
        if not self.column_rows:
            return block.reshape(self.size, LANES)
        block = decode(block)
        parts = [
            block[k] * (self.scales[k][:, scale_lane : scale_lane + LANES] * (1.0 / CODE_TOP))
            for k in range(4)
        ]
        return jnp.concatenate(parts, axis=0)

    def values(self, pair):
        return self.read(self.values_ref, pl.ds(pair * LANES, LANES), pair * LANES)

    def keys(self):
        return self.read(self.keys_ref, pl.ds(0, LANES), self.inner)

    def queries(self, ref):
        return self.read(ref, pl.ds(0, LANES), self.inner + LANES)

    def steps(self):
        block = self.steps_ref[...].reshape(self.size, LANES)
        if not self.column_rows:
            return block
        shape = (LANES, LANES)
        part, head = rows_iota(shape), lanes_iota(shape)
        fold = (lax.rem(part, STEP_LANES) == head) & (part < 3 * STEP_LANES)
        return dot(block, jnp.where(fold, 1.0, 0.0).astype(BF16))

    def earlier(self):
        return earlier_mask(self.size, self.column_rows)


def state_kernel(column_rows, head_size, values_ref, keys_ref, steps_ref, *rest):
    scale_ref = rest[0] if column_rows else None
    rate_ref, memory_ref, decay_ref = rest[-3:]
    chunk = Chunk(column_rows, values_ref, keys_ref, steps_ref, scale_ref)

    @pl.when(pl.program_id(0) == 0)
    def _():
        memory_ref[...] = jnp.zeros_like(memory_ref)
        decay_ref[...] = jnp.ones_like(decay_ref)

    steps = chunk.steps()
    keys_t = split(jnp.transpose(chunk.keys()))
    running, total = running_logs(steps, rate_ref[...], chunk.earlier())
    coefficient = steps * jnp.exp(jnp.minimum(total - running, 0.0))
    decay = jnp.exp(total)
    for pair in range(chunk.pairs):
        lanes = pl.ds(pair * LANES, LANES)
        weighted = chunk.values(pair) * spread(coefficient, pair, head_size)
        pair_decay = spread(decay, pair, head_size)
        memory_ref[:, lanes] = advance(memory_ref[:, lanes], keys_t, weighted, pair_decay)
        decay_ref[pl.ds(pair, 1), :] = decay_ref[pl.ds(pair, 1), :] * pair_decay


def output_kernel(column_rows, head_size, values_ref, keys_ref, steps_ref, *rest):
    if column_rows:
        scale_ref, queries_ref, rate_ref, entering_ref, out_ref, memory_ref, scales_ref = rest
        skip_ref = None
    else:
        queries_ref, rate_ref, entering_ref, skip_ref, out_ref, memory_ref = rest
        scale_ref = None
    chunk = Chunk(column_rows, values_ref, keys_ref, steps_ref, scale_ref)
    size = chunk.size

    @pl.when(pl.program_id(0) == 0)
    def _():
        memory_ref[...] = entering_ref[...]
        if column_rows:
            scales_ref[...] = jnp.zeros_like(scales_ref)

    steps = chunk.steps()
    keys_t = split(jnp.transpose(chunk.keys()))
    queries_high, queries_low = split(chunk.queries(queries_ref))
    earlier = chunk.earlier()
    running, total = running_logs(steps, rate_ref[...], earlier)
    across = jnp.transpose(running)
    scores = dot(queries_high, keys_t[0]) + dot(queries_high, keys_t[1]) + dot(queries_low, keys_t[0])
    scores = jnp.where(earlier, scores, 0.0)
    arrived = jnp.exp(running)
    leaving = jnp.exp(jnp.minimum(total - running, 0.0))
    decay = jnp.exp(total)
    first_half = lanes_iota((size, LANES)) < head_size
    at = pl.num_programs(0) - 1 - pl.program_id(0)
    for pair in range(chunk.pairs):
        lanes = pl.ds(pair * LANES, LANES)
        values = chunk.values(pair)
        scaled = values * spread(steps, pair, head_size)
        high, low = split(scaled)
        both = jnp.concatenate([high, low], axis=1)
        halves = []
        for head in (2 * pair, 2 * pair + 1):
            between = jnp.minimum(running[:, head : head + 1] - across[head : head + 1, :], 0.0)
            kernel_high, kernel_low = split(jnp.exp(between) * scores)
            part = dot(kernel_high, both)
            halves.append(part[:, :LANES] + part[:, LANES:] + dot(kernel_low, high))
        memory = memory_ref[:, lanes]
        memory_high, memory_low = split(memory)
        part = dot(queries_high, jnp.concatenate([memory_high, memory_low], axis=1))
        carried = part[:, :LANES] + part[:, LANES:] + dot(queries_low, memory_high)
        result = jnp.where(first_half, halves[0], halves[1])
        result = result + carried * spread(arrived, pair, head_size)
        if column_rows:
            scale, factor = code_scale(jnp.max(jnp.abs(result), axis=0, keepdims=True))
            coded = encode(result * factor).reshape(4, size // 4, LANES)
            first = pl.multiple_of(at * (size // 4), 16)
            out_ref[:, pl.ds(first, size // 4), lanes] = coded
            here = rows_iota((16, LANES)) == at
            scales_ref[:, lanes] = jnp.where(here, scale.astype(F32), scales_ref[:, lanes])
        else:
            result = result + values * skip_ref[:, lanes]
            out_ref[:, :, lanes] = result.reshape(1, size, LANES)
        weighted = scaled * spread(leaving, pair, head_size)
        memory_ref[:, lanes] = advance(memory, keys_t, weighted, spread(decay, pair, head_size))

    if column_rows:

        @pl.when(pl.program_id(0) == pl.num_programs(0) - 1)
        def _():
            scales = scales_ref[...].astype(BF16)
            for k in range(4):
                out_ref[k, pl.ds(out_ref.shape[1] - 16, 16), :] = scales


def chunk_specs(sources, inner, size, column_rows):
    pieces = 4 if column_rows else 1
    part = size // pieces
    count = sources[0].shape[1] // part
    first = inner // LANES if column_rows else 0

    def spec(lane_count, lane_block):
        def index(j):
            return (0, count - 1 - j if column_rows else j, lane_block)

        return pl.BlockSpec((pieces, part, lane_count), index)

    specs = [spec(inner, 0), spec(LANES, first), spec(LANES, first + 2)]
    arrays = [sources[0], sources[-1], sources[-1]]
    if column_rows:
        last = sources[0].shape[1] // 16 - 1
        specs.append(pl.BlockSpec((pieces, 16, sources[0].shape[2]), lambda j: (0, last, 0)))
        arrays.append(sources[0])
    return count, specs, arrays, spec(LANES, first + 1)


def whole(shape):
    return pl.BlockSpec(shape, lambda j: (0,) * len(shape))


def estimate(tokens, inner, passes, transfers):
    return pl.CostEstimate(
        flops=2 * tokens * inner * 192 * passes, bytes_accessed=transfers, transcendentals=0
    )


def local_state(sources, rate, inner, size, column_rows, head_size):
    count, specs, arrays, _ = chunk_specs(sources, inner, size, column_rows)
    return pl.pallas_call(
        functools.partial(state_kernel, column_rows, head_size),
        grid=(count,),
        in_specs=specs + [whole((1, LANES))],
        out_specs=[whole((LANES, inner)), whole((16, LANES))],
        out_shape=[
            jax.ShapeDtypeStruct((LANES, inner), F32),
            jax.ShapeDtypeStruct((16, LANES), F32),
        ],
        cost_estimate=estimate(count * size, inner, 10, 16 << 20),
        compiler_params=params(),
    )(*arrays, rate)


def local_output(sources, rate, entering, skip, inner, size, column_rows, head_size):
    count, specs, arrays, queries = chunk_specs(sources, inner, size, column_rows)
    shape = sources[0].shape[:2] + (inner,)
    extra = [] if column_rows else [skip]
    scratch = [pltpu.VMEM((LANES, inner), F32)]
    if column_rows:
        scratch.append(pltpu.VMEM((16, inner), F32))
    return pl.pallas_call(
        functools.partial(output_kernel, column_rows, head_size),
        grid=(count,),
        in_specs=specs
        + [queries, whole((1, LANES)), whole((LANES, inner))]
        + [whole((1, inner)) for _ in extra],
        out_specs=whole(shape) if column_rows else specs[0],
        out_shape=jax.ShapeDtypeStruct(shape, BF16 if column_rows else F32),
        scratch_shapes=scratch,
        cost_estimate=estimate(count * size, inner, 30, 32 << 20),
        compiler_params=params(),
    )(*arrays, sources[-1], rate, entering, *extra)


def prefix_kernel(reverse, rows, pairs, source_ref, out_ref):
    count = source_ref.shape[0]
    entering = jnp.zeros((rows, LANES), F32)
    for k in range(count):
        at = count - 1 - k if reverse else k
        out_ref[at] = entering
        decay = source_ref[at, pl.ds(rows, pairs), :]
        decay = jnp.concatenate([decay] * (rows // pairs), axis=0)
        entering = entering * decay + source_ref[at, pl.ds(0, rows), :]


def entering_state(memory, decay, axes, reverse):
    count = 1
    for axis in axes:
        count = count * lax.axis_size(axis)
    pairs = memory.shape[1] // LANES
    rows = memory.shape[0] * pairs // count
    sent = jnp.concatenate(
        [
            memory.reshape(count, rows, LANES),
            jnp.broadcast_to(decay[None], (count,) + decay.shape),
        ],
        axis=1,
    )
    received = lax.all_to_all(sent, axes, 0, 0, tiled=True)
    found = pl.pallas_call(
        functools.partial(prefix_kernel, reverse, rows, pairs),
        out_shape=jax.ShapeDtypeStruct((count, rows, LANES), F32),
        compiler_params=pltpu.CompilerParams(vmem_limit_bytes=VMEM_BYTES),
    )(received)
    returned = lax.all_to_all(found, axes, 0, 0, tiled=True)
    return returned.reshape(memory.shape)


def finish_kernel(head_size, groups, part, forward_ref, backward_ref, gate_ref, gain_ref, out_ref, moved_ref):
    col_total = forward_ref.shape[0] // 4
    quad = pl.program_id(0)
    last = backward_ref.shape[1] - 16
    scales = [backward_ref[k, pl.ds(last, 16), :].astype(F32) * (1.0 / CODE_TOP) for k in range(4)]

    def group_rows(group):
        piece, within = group // groups, group % groups
        first = pl.multiple_of(within * part + 16 * quad, 16)
        coded = backward_ref[piece, pl.ds(first, 16), :]
        return decode(coded) * scales[piece][within : within + 1, :]

    for at in range(col_total // 8):
        even, odd = group_rows(2 * at), group_rows(2 * at + 1)
        for k in (0, 1):
            low_half, high_half = even[8 * k : 8 * k + 8], odd[8 * k : 8 * k + 8]
            first, second = column_groups(low_half, high_half)
            moved_ref[pl.ds(2 * k * col_total + 8 * at, 8), :] = first
            moved_ref[pl.ds((2 * k + 1) * col_total + 8 * at, 8), :] = second
    wide = 2 * LANES
    same = rows_iota((wide, wide)) // head_size == lanes_iota((wide, wide)) // head_size
    ones = jnp.where(same, 1.0, 0.0).astype(BF16)
    for block in range(forward_ref.shape[1] // wide):
        lanes = pl.ds(block * wide, wide)
        gate = gate_ref[:, lanes]
        combined = forward_ref[:, lanes] + moved_ref[:, lanes]
        gated = combined * (gate / (1.0 + jnp.exp(-gate)))
        high, low = split(gated * gated)
        mean = (dot(high, ones) + dot(low, ones)) * (1.0 / head_size)
        normed = gated * lax.rsqrt(mean + 1e-5) * gain_ref[:, lanes]
        out_ref[:, lanes] = normed.astype(out_ref.dtype)


def finish(forward, backward, gate, gain, row_part, col_total, head_size):
    tokens, inner = forward.shape
    groups = col_total // GROUP // 4
    block = 4 * col_total
    flat = pl.BlockSpec((block, inner), lambda m: (m, 0))
    return pl.pallas_call(
        functools.partial(finish_kernel, head_size, groups, row_part * GROUP),
        grid=(row_part // 4,),
        in_specs=[flat, whole(backward.shape), flat, whole((1, inner))],
        out_specs=flat,
        out_shape=jax.ShapeDtypeStruct((tokens, inner), BF16),
        scratch_shapes=[pltpu.VMEM((block, inner), F32)],
        compiler_params=params(),
    )(forward, backward, gate, gain)


def pad_lanes(source):
    return jnp.pad(source, ((0, 0), (0, LANES - source.shape[1])))


def local(tokens, xz_weight, state_weight, step_weight, step_bias, decay_rate, skip, norm_gain):
    videos, frame_count, row_part, col_total, width = tokens.shape
    flattened = tokens.reshape(-1, width)
    inner = xz_weight.shape[1] // 2
    heads = step_weight.shape[1]
    head_size = inner // heads
    column_rows = row_part * lax.axis_size("spatial")
    size = column_rows * GROUP
    axes = ("frame", "spatial")

    thrice = pad_lanes(jnp.concatenate([step_weight] * 3, axis=1))
    bias = pad_lanes(jnp.concatenate([step_bias] * 3)[None])
    first_weight = jnp.concatenate([state_weight, thrice], axis=1)
    gate_weight = lax.all_gather(xz_weight[:, :inner], ("spatial", "dp"), axis=0, tiled=True)
    rates = pad_lanes(decay_rate)
    skips = jnp.repeat(skip[0] + skip[1], head_size)[None]

    values, keys, columns = project(
        flattened, first_weight, bias, xz_weight, row_part, col_total, inner, 512
    )
    rowwise = (values[None], keys[None])
    columnwise = (columns,)

    memory, decay = local_state(columnwise, rates[1:2], inner, size, column_rows, head_size)
    entering = entering_state(memory, decay, axes, True)
    forward_memory, forward_decay = local_state(rowwise, rates[0:1], inner, size, 0, head_size)
    forward_entering = entering_state(forward_memory, forward_decay, axes, False)
    backward = local_output(
        columnwise, rates[1:2], entering, None, inner, size, column_rows, head_size
    )
    returned = lax.all_to_all(backward, "spatial", 0, 0, tiled=True)
    forward = local_output(
        rowwise, rates[0:1], forward_entering, skips, inner, size, 0, head_size
    )
    gate_rows = jnp.dot(flattened, gate_weight, preferred_element_type=F32)
    normed = finish(
        forward[0], returned, gate_rows, norm_gain[None], row_part, col_total, head_size
    )
    return normed.reshape(videos, frame_count, row_part, col_total, inner)


def solution(mesh):
    in_specs = (
        P("dp", "frame", "spatial", None, None),
        P(("spatial", "dp"), None),
        P(("spatial", "dp"), None),
        P(("spatial", "dp"), None),
        P(),
        P(),
        P(),
        P(),
    )
    out_specs = P("dp", "frame", "spatial", None, None)
    return jax.shard_map(local, mesh=mesh, in_specs=in_specs, out_specs=out_specs, check_vma=False)
```

```python
import functools

import jax
import jax.numpy as jnp
from jax import lax
from jax.experimental import pallas as pl
from jax.experimental.pallas import tpu as pltpu
from jax.sharding import PartitionSpec as P

F32 = jnp.float32
BF16 = jnp.bfloat16
LANES = 128
GROUP = 4
POWER = 17
CODE_TOP = 128.0
STEP_LANES = 24
MESH = pl.DeviceIdType.MESH
VMEM_BYTES = 56 * 1024 * 1024


def split(value):
    high = value.astype(BF16)
    return high, (value - high.astype(F32)).astype(BF16)


def dot(a, b):
    return lax.dot_general(a, b, (((1,), (0,)), ((), ())), preferred_element_type=F32)


def rows_iota(shape):
    return lax.broadcasted_iota(jnp.int32, shape, 0)


def lanes_iota(shape):
    return lax.broadcasted_iota(jnp.int32, shape, 1)


def spread(columns, pair, head_size):
    first, second = columns[:, 2 * pair : 2 * pair + 1], columns[:, 2 * pair + 1 : 2 * pair + 2]
    shape = (columns.shape[0], LANES)
    return jnp.where(lanes_iota(shape) < head_size, first, second)


def params(semantics=("arbitrary",)):
    return pltpu.CompilerParams(vmem_limit_bytes=VMEM_BYTES, dimension_semantics=semantics)


def encode(scaled):
    square = scaled * scaled
    fourth = square * square
    eighth = fourth * fourth
    return (eighth * eighth * scaled).astype(BF16)


def decode(coded):
    coded = coded.astype(F32)
    size = jnp.exp2(jnp.log2(jnp.abs(coded)) * (1.0 / POWER))
    return jnp.where(coded < 0.0, -size, size)


def code_scale(largest):
    scale = jnp.maximum(largest, 1e-30).astype(BF16)
    return scale, CODE_TOP / scale.astype(F32)


def column_groups(first, second):
    low = rows_iota(first.shape) < GROUP
    even = jnp.where(low, first, pltpu.roll(second, GROUP, 0))
    odd = jnp.where(low, pltpu.roll(first, GROUP, 0), second)
    return even, odd


def earlier_mask(size, column_rows):
    shape = (size, size)
    t, s = rows_iota(shape), lanes_iota(shape)
    if column_rows:

        def place(index):
            return size - 1 - (lax.rem(index, GROUP) * column_rows + index // GROUP)

        t, s = place(t), place(s)
    return s <= t


def running_logs(steps, rate, earlier):
    logs = -steps * rate
    high, rest = split(logs)
    middle = logs - high.astype(F32)
    middle, low = split(middle)
    before = jnp.where(earlier, 1.0, 0.0).astype(BF16)
    running = dot(before, high) + dot(before, middle) + dot(before, low)
    return running, jnp.sum(logs, axis=0, keepdims=True)


def advance(memory, keys_t, weighted, decay):
    keys_high, keys_low = keys_t
    high, low = split(weighted)
    both = dot(keys_high, jnp.concatenate([high, low], axis=1))
    added = both[:, :LANES] + both[:, LANES:] + dot(keys_low, high)
    return memory * decay + added


def fold_chunk(values, keys, steps, rate, earlier, head_size, memory_ref, total_ref):
    keys_t = split(jnp.transpose(keys))
    running, total = running_logs(steps, rate, earlier)
    coefficient = steps * jnp.exp(jnp.minimum(total - running, 0.0))
    decay = jnp.exp(total)
    for pair in range(memory_ref.shape[1] // LANES):
        lanes = pl.ds(pair * LANES, LANES)
        weighted = values(pair) * spread(coefficient, pair, head_size)
        memory_ref[:, lanes] = advance(
            memory_ref[:, lanes], keys_t, weighted, spread(decay, pair, head_size)
        )
    total_ref[...] = total_ref[...] + total


def project_kernel(
    geometry,
    tokens_ref,
    state_ref,
    bias_ref,
    rate_ref,
    xz_ref,
    values_ref,
    keys_ref,
    columns_ref,
    memory_ref,
    total_ref,
    weight,
    product,
    middle,
    own_sem,
    x_send,
    x_recv,
    y_send,
    y_recv,
    core_send,
    core_recv,
    move_send,
    move_recv,
    move_own,
    out_sem,
):
    row_part, col_total, inner, depth, blocks, head_size = geometry
    half = depth // 2
    frame, place, part = lax.axis_index("frame"), lax.axis_index("spatial"), lax.axis_index("dp")
    core, y = part % 2, (frame % 2) * 2 + part // 2
    right, left, across = (place + 1) % 4, (place + 3) % 4, (place + 2) % 4

    def y_device(other):
        return ((frame // 2) * 2 + other // 2, place, (other % 2) * 2 + core)

    x_right, x_left, x_across = (frame, right, part), (frame, left, part), (frame, across, part)
    y_up, y_down = y_device((y + 1) % 4), y_device((y + 3) % 4)
    partner = (frame, place, (part // 2) * 2 + 1 - core)

    barrier = pltpu.get_barrier_semaphore()
    peers = (x_right, x_left, x_across, y_up, y_down, partner)
    for peer in peers:
        pl.semaphore_signal(barrier, inc=1, device_id=peer, device_id_type=MESH)
    pl.semaphore_wait(barrier, len(peers))

    def slot(where, other_core, other_part):
        return where * 4 + other_part * 2 + other_core

    same, opposite = part // 2, 1 - part // 2
    sources = (place, left, right, across)

    def rows(index, first, count):
        return pl.ds(pl.multiple_of(index * depth + first, 16), count)

    def view(block, index, first, count):
        return weight.at[block, rows(index, first, count), pl.ds(0, blocks[block][1])]

    def own(block, first, count):
        start, width = blocks[block]
        if block == 0:
            return state_ref.at[pl.ds(first, count), :]
        return xz_ref.at[pl.ds(first, count), pl.ds(inner + start, width)]

    pending = []

    def send(source, target, send_sem, recv_sem, device):
        copy = pltpu.make_async_remote_copy(
            src_ref=source,
            dst_ref=target,
            send_sem=send_sem,
            recv_sem=recv_sem,
            device_id=device,
            device_id_type=MESH,
        )
        copy.start()
        pending.append(copy)

    def arrived(target, send_sem, recv_sem):
        pltpu.make_async_remote_copy(
            src_ref=target,
            dst_ref=target,
            send_sem=send_sem,
            recv_sem=recv_sem,
            device_id=x_right,
            device_id_type=MESH,
        ).wait_recv()

    def send_y(block, which, source_of):
        index = slot(sources[which], core, same)
        for part_at, device in ((0, y_up), (1, y_down)):
            first = part_at * half
            send(
                source_of(first),
                view(block, index, first, half),
                y_send.at[block, which, part_at],
                y_recv.at[block, which, part_at],
                device,
            )

    def send_core(block, at, index, source):
        send(
            source,
            view(block, index, 0, depth),
            core_send.at[block, at],
            core_recv.at[block, at],
            partner,
        )

    def send_own(block):
        index = slot(place, core, same)
        target = view(block, index, 0, depth)
        source = own(block, 0, depth)
        send(source, target, x_send.at[block, 0], x_recv.at[block, 0], x_right)
        send(source, target, x_send.at[block, 1], x_recv.at[block, 1], x_left)
        send_y(block, 0, lambda first: own(block, first, half))
        send_core(block, 0, index, source)
        copy = pltpu.make_async_copy(source, target, own_sem.at[block])
        copy.start()

    def relay(block):
        from_left, from_right = slot(left, core, same), slot(right, core, same)
        for which, index in ((1, from_left), (2, from_right)):
            arrived(
                view(block, index, 0, depth),
                x_send.at[block, which - 1],
                x_recv.at[block, which - 1],
            )
            part_at = which - 1
            send(
                view(block, index, part_at * half, half),
                view(block, index, part_at * half, half),
                x_send.at[block, 2 + part_at],
                x_recv.at[block, 2 + part_at],
                (x_right, x_left)[part_at],
            )
            send_y(block, which, lambda first: view(block, index, first, half))
            send_core(block, which, index, view(block, index, 0, depth))
    def relay_far(block):
        far = slot(across, core, same)
        for part_at in (0, 1):
            arrived(
                view(block, far, part_at * half, half),
                x_send.at[block, 2 + part_at],
                x_recv.at[block, 2 + part_at],
            )
        send_y(block, 3, lambda first: view(block, far, first, half))
        send_core(block, 3, far, view(block, far, 0, depth))

    def pass_on(block):
        for which in range(4):
            index = slot(sources[which], core, opposite)
            for part_at in (0, 1):
                arrived(
                    view(block, index, part_at * half, half),
                    y_send.at[block, which, part_at],
                    y_recv.at[block, which, part_at],
                )
            send_core(block, 4 + which, index, view(block, index, 0, depth))

    def gathered(block):
        for at in range(8):
            index = slot(sources[at % 4], 1 - core, same if at < 4 else opposite)
            arrived(
                view(block, index, 0, depth), core_send.at[block, at], core_recv.at[block, at]
            )
        index = slot(place, core, same)
        target = view(block, index, 0, depth)
        pltpu.make_async_copy(own(block, 0, depth), target, own_sem.at[block]).wait()

    tokens = row_part * col_total
    tile = tokens // 5
    groups = col_total // GROUP // 4
    piece_rows = groups * row_part * GROUP
    outs = {}

    def compute(block):
        start, width = blocks[block]
        lanes = pl.ds(0, width)
        buffer = block

        def one_tile(i, largest):
            at = pl.ds(pl.multiple_of(i * tile, tile), tile)
            result = dot(tokens_ref[at, :], weight[block, :, lanes])
            if block == 0:
                raw = result[:, width - LANES :] + bias_ref[...]
                steps = jnp.maximum(raw, 0.0) + jnp.log1p(jnp.exp(-jnp.abs(raw)))
                result = jnp.concatenate([result[:, : width - LANES], steps], axis=1)
            product[buffer, at, lanes] = result
            return jnp.maximum(largest, jnp.max(jnp.abs(result), axis=0, keepdims=True))

        largest = lax.fori_loop(0, 5, one_tile, jnp.zeros((1, width), F32))
        if block == 0:
            out = keys_ref
        else:
            out = values_ref.at[:, pl.ds(start, width)]
        copy = pltpu.make_async_copy(product.at[buffer, :, lanes], out, out_sem.at[block])
        copy.start()
        outs[block] = copy

        scale, factor = code_scale(largest)

        def code(value):
            coded = encode(value * factor)
            if block == 0:
                exact = value[:, width - LANES :]
                high = exact.astype(BF16)
                rest = exact - high.astype(F32)
                second = rest.astype(BF16)
                third = (rest - second.astype(F32)).astype(BF16)
                lane = lanes_iota(exact.shape)
                heads = STEP_LANES
                parts = jnp.where(
                    lane < heads,
                    high.astype(F32),
                    jnp.where(lane < 2 * heads, second.astype(F32), third.astype(F32)),
                )
                coded = jnp.concatenate([coded[:, : width - LANES], parts.astype(BF16)], axis=1)
            return coded

        for quad in range(row_part // 4):

            def one_group(at, carry):
                both = []
                for pair in (2 * quad, 2 * quad + 1):
                    first = product[buffer, pl.ds(pl.multiple_of(2 * pair * col_total + 8 * at, 8), 8), lanes]
                    second = product[
                        buffer, pl.ds(pl.multiple_of((2 * pair + 1) * col_total + 8 * at, 8), 8), lanes
                    ]
                    both.append(column_groups(first, second))
                for odd in (0, 1):
                    group = 2 * at + odd
                    piece = group // groups
                    row = pl.multiple_of((group % groups) * row_part * GROUP + 16 * quad, 16)
                    value = jnp.concatenate([both[0][odd], both[1][odd]], axis=0)
                    middle[block, piece, pl.ds(row, 16), lanes] = code(value)
                return carry

            lax.fori_loop(0, col_total // 8, one_group, 0)
        for piece in range(4):
            middle[block, piece, pl.ds(piece_rows, 16), lanes] = jnp.broadcast_to(scale, (16, width))
        into = columns_ref.at[place, :, pl.ds(inner if block == 0 else start, width)]
        for at, (where, device) in enumerate(((right, x_right), (left, x_left), (across, x_across))):
            send(
                middle.at[block, where, :, lanes],
                into,
                move_send.at[block, at],
                move_recv.at[block, at],
                device,
            )
        pltpu.make_async_copy(middle.at[block, place, :, lanes], into, move_own.at[block]).start()

    count = len(blocks)
    for block in range(count):
        send_own(block)
    relay(0)
    relay(1)
    relay_far(0)
    for block in range(count):
        if block + 2 < count:
            relay(block + 2)
        if block + 1 < count:
            relay_far(block + 1)
        pass_on(block)
        gathered(block)
        compute(block)

    memory_ref[...] = jnp.zeros_like(memory_ref)
    total_ref[...] = jnp.zeros_like(total_ref)

    def fold_rows(step, carry):
        at = pl.ds(pl.multiple_of(step * tile, 16), tile)
        block_pairs = blocks[1][1] // LANES

        def values(pair):
            return product[1 + pair // block_pairs, at, pl.ds(pair % block_pairs * LANES, LANES)]

        fold_chunk(
            values,
            product[0, at, pl.ds(0, LANES)],
            product[0, at, pl.ds(2 * LANES, LANES)],
            rate_ref[...],
            earlier_mask(tile, 0),
            head_size,
            memory_ref,
            total_ref,
        )
        return carry

    lax.fori_loop(0, 5, fold_rows, 0)
    for block in range(count):
        start, width = blocks[block]
        lanes = pl.ds(0, width)
        for at, where in enumerate((left, right, across)):
            into = columns_ref.at[where, :, pl.ds(inner if block == 0 else start, width)]
            arrived(into, move_send.at[block, at], move_recv.at[block, at])
        into = columns_ref.at[place, :, pl.ds(inner if block == 0 else start, width)]
        pltpu.make_async_copy(middle.at[block, place, :, lanes], into, move_own.at[block]).wait()
    for copy in outs.values():
        copy.wait()
    for copy in pending:
        copy.wait_send()


def project(tokens, state_weight, bias, rate, xz_weight, row_part, col_total, inner, head_size, block_width):
    depth, state_width = state_weight.shape
    count = inner // block_width + 1
    blocks = ((0, state_width),) + tuple((k * block_width, block_width) for k in range(count - 1))
    width = max(block_width, state_width)
    total = tokens.shape[0]
    piece_rows = total // 4 + 16
    vmem, hbm = pl.BlockSpec(memory_space=pltpu.VMEM), pl.BlockSpec(memory_space=pl.ANY)
    dma = pltpu.SemaphoreType.DMA
    return pl.pallas_call(
        functools.partial(project_kernel, (row_part, col_total, inner, depth, blocks, head_size)),
        in_specs=[vmem, vmem, vmem, vmem, hbm],
        out_specs=[hbm, hbm, hbm, vmem, vmem],
        out_shape=[
            jax.ShapeDtypeStruct((total, inner), F32),
            jax.ShapeDtypeStruct((total, state_width), F32),
            jax.ShapeDtypeStruct((4, piece_rows, inner + state_width), BF16),
            jax.ShapeDtypeStruct((LANES, inner), F32),
            jax.ShapeDtypeStruct((8, LANES), F32),
        ],
        scratch_shapes=[
            pltpu.VMEM((count, tokens.shape[1], width), BF16),
            pltpu.VMEM((count, total, width), F32),
            pltpu.VMEM((count, 4, piece_rows, width), BF16),
            dma((count,)),
            dma((count, 4)),
            dma((count, 4)),
            dma((count, 4, 2)),
            dma((count, 4, 2)),
            dma((count, 8)),
            dma((count, 8)),
            dma((count, 3)),
            dma((count, 3)),
            dma((count,)),
            dma((count,)),
        ],
        compiler_params=pltpu.CompilerParams(
            collective_id=0, has_side_effects=True, vmem_limit_bytes=VMEM_BYTES
        ),
    )(tokens, state_weight, bias, rate, xz_weight)


class Chunk:
    def __init__(self, column_rows, values_ref, keys_ref, steps_ref, scale_ref):
        self.size = values_ref.shape[0] * values_ref.shape[1]
        self.inner = values_ref.shape[2]
        self.pairs = self.inner // LANES
        self.column_rows, self.values_ref, self.scale_ref = column_rows, values_ref, scale_ref
        self.keys_ref, self.steps_ref = keys_ref, steps_ref
        if column_rows:
            self.scales = [scale_ref[k, pl.ds(0, 16), :].astype(F32)[0:1] for k in range(4)]

    def read(self, ref, lanes, scale_lane):
        block = ref[:, :, lanes]
        if not self.column_rows:
            return block.reshape(self.size, LANES)
        block = decode(block)
        parts = [
            block[k] * (self.scales[k][:, scale_lane : scale_lane + LANES] * (1.0 / CODE_TOP))
            for k in range(4)
        ]
        return jnp.concatenate(parts, axis=0)

    def values(self, pair):
        return self.read(self.values_ref, pl.ds(pair * LANES, LANES), pair * LANES)

    def keys(self):
        return self.read(self.keys_ref, pl.ds(0, LANES), self.inner)

    def queries(self, ref):
        return self.read(ref, pl.ds(0, LANES), self.inner + LANES)

    def steps(self):
        block = self.steps_ref[...].reshape(self.size, LANES)
        if not self.column_rows:
            return block
        shape = (LANES, LANES)
        part, head = rows_iota(shape), lanes_iota(shape)
        fold = (lax.rem(part, STEP_LANES) == head) & (part < 3 * STEP_LANES)
        return dot(block, jnp.where(fold, 1.0, 0.0).astype(BF16))

    def earlier(self):
        return earlier_mask(self.size, self.column_rows)


def output_kernel(column_rows, head_size, values_ref, keys_ref, steps_ref, *rest):
    if column_rows:
        scale_ref, queries_ref, rate_ref, entering_ref, out_ref, memory_ref, scales_ref = rest
        skip_ref = None
    else:
        queries_ref, rate_ref, entering_ref, skip_ref, out_ref, memory_ref = rest
        scale_ref = None
    chunk = Chunk(column_rows, values_ref, keys_ref, steps_ref, scale_ref)
    size = chunk.size

    @pl.when(pl.program_id(0) == 0)
    def _():
        memory_ref[...] = entering_ref[...]
        if column_rows:
            scales_ref[...] = jnp.zeros_like(scales_ref)

    steps = chunk.steps()
    keys_t = split(jnp.transpose(chunk.keys()))
    queries_high, queries_low = split(chunk.queries(queries_ref))
    earlier = chunk.earlier()
    running, total = running_logs(steps, rate_ref[...], earlier)
    across = jnp.transpose(running)
    scores = dot(queries_high, keys_t[0]) + dot(queries_high, keys_t[1]) + dot(queries_low, keys_t[0])
    scores = jnp.where(earlier, scores, 0.0)
    arrived = jnp.exp(running)
    leaving = jnp.exp(jnp.minimum(total - running, 0.0))
    decay = jnp.exp(total)
    first_half = lanes_iota((size, LANES)) < head_size
    at = pl.num_programs(0) - 1 - pl.program_id(0)
    for pair in range(chunk.pairs):
        lanes = pl.ds(pair * LANES, LANES)
        values = chunk.values(pair)
        scaled = values * spread(steps, pair, head_size)
        high, low = split(scaled)
        both = jnp.concatenate([high, low], axis=1)
        halves = []
        for head in (2 * pair, 2 * pair + 1):
            between = jnp.minimum(running[:, head : head + 1] - across[head : head + 1, :], 0.0)
            kernel_high, kernel_low = split(jnp.exp(between) * scores)
            part = dot(kernel_high, both)
            halves.append(part[:, :LANES] + part[:, LANES:] + dot(kernel_low, high))
        memory = memory_ref[:, lanes]
        memory_high, memory_low = split(memory)
        part = dot(queries_high, jnp.concatenate([memory_high, memory_low], axis=1))
        carried = part[:, :LANES] + part[:, LANES:] + dot(queries_low, memory_high)
        result = jnp.where(first_half, halves[0], halves[1])
        result = result + carried * spread(arrived, pair, head_size)
        if column_rows:
            scale, factor = code_scale(jnp.max(jnp.abs(result), axis=0, keepdims=True))
            coded = encode(result * factor).reshape(4, size // 4, LANES)
            first = pl.multiple_of(at * (size // 4), 16)
            out_ref[:, pl.ds(first, size // 4), lanes] = coded
            here = rows_iota((16, LANES)) == at
            scales_ref[:, lanes] = jnp.where(here, scale.astype(F32), scales_ref[:, lanes])
        else:
            result = result + values * skip_ref[:, lanes]
            out_ref[:, :, lanes] = result.reshape(1, size, LANES)
        weighted = scaled * spread(leaving, pair, head_size)
        memory_ref[:, lanes] = advance(memory, keys_t, weighted, spread(decay, pair, head_size))

    if column_rows:

        @pl.when(pl.program_id(0) == pl.num_programs(0) - 1)
        def _():
            scales = scales_ref[...].astype(BF16)
            for k in range(4):
                out_ref[k, pl.ds(out_ref.shape[1] - 16, 16), :] = scales


def chunk_specs(sources, inner, size, column_rows):
    pieces = 4 if column_rows else 1
    part = size // pieces
    count = sources[0].shape[1] // part
    first = inner // LANES if column_rows else 0

    def spec(lane_count, lane_block):
        def index(j):
            return (0, count - 1 - j if column_rows else j, lane_block)

        return pl.BlockSpec((pieces, part, lane_count), index)

    specs = [spec(inner, 0), spec(LANES, first), spec(LANES, first + 2)]
    arrays = [sources[0], sources[-1], sources[-1]]
    if column_rows:
        last = sources[0].shape[1] // 16 - 1
        specs.append(pl.BlockSpec((pieces, 16, sources[0].shape[2]), lambda j: (0, last, 0)))
        arrays.append(sources[0])
    return count, specs, arrays, spec(LANES, first + 1)


def whole(shape):
    return pl.BlockSpec(shape, lambda j: (0,) * len(shape))


def estimate(tokens, inner, passes, transfers):
    return pl.CostEstimate(
        flops=2 * tokens * inner * 192 * passes, bytes_accessed=transfers, transcendentals=0
    )


def local_output(sources, rate, entering, skip, inner, size, column_rows, head_size):
    count, specs, arrays, queries = chunk_specs(sources, inner, size, column_rows)
    shape = sources[0].shape[:2] + (inner,)
    extra = [] if column_rows else [skip]
    scratch = [pltpu.VMEM((LANES, inner), F32)]
    if column_rows:
        scratch.append(pltpu.VMEM((16, inner), F32))
    return pl.pallas_call(
        functools.partial(output_kernel, column_rows, head_size),
        grid=(count,),
        in_specs=specs
        + [queries, whole((1, LANES)), whole((LANES, inner))]
        + [whole((1, inner)) for _ in extra],
        out_specs=whole(shape) if column_rows else specs[0],
        out_shape=jax.ShapeDtypeStruct(shape, BF16 if column_rows else F32),
        scratch_shapes=scratch,
        cost_estimate=estimate(count * size, inner, 30, 32 << 20),
        compiler_params=params(),
    )(*arrays, sources[-1], rate, entering, *extra)


def states_kernel(
    geometry,
    columns_ref,
    rate_ref,
    forward_ref,
    forward_total_ref,
    entering_forward_ref,
    entering_backward_ref,
    memory,
    total,
    sent,
    received,
    found,
    out_send,
    out_recv,
    back_send,
    back_recv,
    own_sem,
):
    inner, size, column_rows, head_size, count, spatial = geometry
    slices = count // 2
    rows, wide = LANES // slices, inner // 2
    pairs = wide // LANES
    frame, place, part = lax.axis_index("frame"), lax.axis_index("spatial"), lax.axis_index("dp")
    me = frame * spatial + place

    def device(index):
        return (index // spatial, index % spatial, part)

    barrier = pltpu.get_barrier_semaphore()

    def greet(k, carry):
        peer = device((me + k) % count)
        pl.semaphore_signal(barrier, inc=1, device_id=peer, device_id_type=MESH)
        return carry

    lax.fori_loop(1, count, greet, 0)
    pl.semaphore_wait(barrier, count - 1)

    def send_slices(way, memory_ref, total_ref):
        totals = total_ref[...]
        shifted = pltpu.roll(totals, LANES - 2 * pairs, 1)
        for index in range(count):
            first, lane = rows * (index // 2), wide * (index % 2)
            sent[way, index, :, pl.ds(0, wide)] = memory_ref[pl.ds(first, rows), pl.ds(lane, wide)]
            sent[way, index, :, pl.ds(wide, LANES)] = shifted if index % 2 else totals

        def one(k, carry):
            to = (me + k) % count
            pltpu.make_async_remote_copy(
                src_ref=sent.at[way, to],
                dst_ref=received.at[way, me],
                send_sem=out_send.at[way, k],
                recv_sem=out_recv.at[way, k],
                device_id=device(to),
                device_id_type=MESH,
            ).start()
            return carry

        lax.fori_loop(1, count, one, 0)
        received[way, me] = sent[way, me]

    def scan(way, reverse, entering_ref):
        def arrive(k, carry):
            source = (me + count - k) % count
            pltpu.make_async_remote_copy(
                src_ref=received.at[way, source],
                dst_ref=received.at[way, source],
                send_sem=out_send.at[way, k],
                recv_sem=out_recv.at[way, k],
                device_id=device(source),
                device_id_type=MESH,
            ).wait_recv()
            return carry

        lax.fori_loop(1, count, arrive, 0)
        entering = jnp.zeros((rows, wide), F32)
        for k in range(count):
            at = count - 1 - k if reverse else k
            found[way, at] = entering
            decay = jnp.exp(received[way, at, :, pl.ds(wide, LANES)])
            spreads = [spread(decay, pair, head_size) for pair in range(pairs)]
            decay = jnp.concatenate(spreads, axis=1)
            entering = entering * decay + received[way, at, :, pl.ds(0, wide)]

        def one(k, carry):
            to = (me + k) % count
            pltpu.make_async_remote_copy(
                src_ref=found.at[way, to],
                dst_ref=place_of(entering_ref, me),
                send_sem=back_send.at[way, k],
                recv_sem=back_recv.at[way, k],
                device_id=device(to),
                device_id_type=MESH,
            ).start()
            return carry

        lax.fori_loop(1, count, one, 0)
        copy = pltpu.make_async_copy(found.at[way, me], place_of(entering_ref, me), own_sem.at[way])
        copy.start()

    def place_of(entering_ref, index):
        first = pl.multiple_of(rows * (index // 2), rows)
        lane = pl.multiple_of(wide * (index % 2), LANES)
        return entering_ref.at[pl.ds(first, rows), pl.ds(lane, wide)]

    def finish_way(way, entering_ref):
        def arrive(k, carry):
            source = (me + count - k) % count
            to = (me + k) % count
            pltpu.make_async_remote_copy(
                src_ref=found.at[way, source],
                dst_ref=place_of(entering_ref, source),
                send_sem=back_send.at[way, k],
                recv_sem=back_recv.at[way, k],
                device_id=device(to),
                device_id_type=MESH,
            ).wait()
            pltpu.make_async_remote_copy(
                src_ref=sent.at[way, to],
                dst_ref=received.at[way, me],
                send_sem=out_send.at[way, k],
                recv_sem=out_recv.at[way, k],
                device_id=device(to),
                device_id_type=MESH,
            ).wait_send()
            return carry

        lax.fori_loop(1, count, arrive, 0)
        pltpu.make_async_copy(
            found.at[way, me], place_of(entering_ref, me), own_sem.at[way]
        ).wait()

    send_slices(0, forward_ref, forward_total_ref)
    memory[...] = jnp.zeros_like(memory)
    total[...] = jnp.zeros_like(total)
    chunks = (columns_ref.shape[1] - 16) // (size // 4)
    last = columns_ref.shape[1] - 16

    def fold_columns(step, carry):
        at = pl.ds(pl.multiple_of((chunks - 1 - step) * (size // 4), 16), size // 4)
        chunk = Chunk(
            column_rows,
            columns_ref.at[:, at, pl.ds(0, inner)],
            columns_ref.at[:, at, pl.ds(inner, LANES)],
            columns_ref.at[:, at, pl.ds(inner + 2 * LANES, LANES)],
            columns_ref.at[:, pl.ds(last, 16), :],
        )
        fold_chunk(
            chunk.values,
            chunk.keys(),
            chunk.steps(),
            rate_ref[...],
            chunk.earlier(),
            head_size,
            memory,
            total,
        )
        return carry

    lax.fori_loop(0, chunks, fold_columns, 0)
    send_slices(1, memory, total)
    scan(0, False, entering_forward_ref)
    scan(1, True, entering_backward_ref)
    finish_way(0, entering_forward_ref)
    finish_way(1, entering_backward_ref)


def entering_states(columns, rate, memory, total, inner, size, column_rows, head_size):
    spatial = lax.axis_size("spatial")
    count = lax.axis_size("frame") * spatial
    rows, wide = LANES * 2 // count, inner // 2
    vmem, hbm = pl.BlockSpec(memory_space=pltpu.VMEM), pl.BlockSpec(memory_space=pl.ANY)
    dma = pltpu.SemaphoreType.DMA
    state = jax.ShapeDtypeStruct((LANES, inner), F32)
    geometry = (inner, size, column_rows, head_size, count, spatial)
    return pl.pallas_call(
        functools.partial(states_kernel, geometry),
        in_specs=[vmem] * 4,
        out_specs=[hbm, hbm],
        out_shape=[state, state],
        scratch_shapes=[
            pltpu.VMEM((LANES, inner), F32),
            pltpu.VMEM((8, LANES), F32),
            pltpu.VMEM((2, count, rows, wide + LANES), F32),
            pltpu.VMEM((2, count, rows, wide + LANES), F32),
            pltpu.VMEM((2, count, rows, wide), F32),
            dma((2, count)),
            dma((2, count)),
            dma((2, count)),
            dma((2, count)),
            dma((2,)),
        ],
        compiler_params=pltpu.CompilerParams(
            collective_id=1, has_side_effects=True, vmem_limit_bytes=VMEM_BYTES
        ),
    )(columns, rate, memory, total)


def finish_kernel(head_size, groups, part, forward_ref, backward_ref, gate_ref, gain_ref, out_ref, moved_ref):
    col_total = forward_ref.shape[0] // 4
    quad = pl.program_id(0)
    last = backward_ref.shape[1] - 16
    scales = [backward_ref[k, pl.ds(last, 16), :].astype(F32) * (1.0 / CODE_TOP) for k in range(4)]

    def group_rows(group):
        piece, within = group // groups, group % groups
        first = pl.multiple_of(within * part + 16 * quad, 16)
        coded = backward_ref[piece, pl.ds(first, 16), :]
        return decode(coded) * scales[piece][within : within + 1, :]

    for at in range(col_total // 8):
        even, odd = group_rows(2 * at), group_rows(2 * at + 1)
        for k in (0, 1):
            low_half, high_half = even[8 * k : 8 * k + 8], odd[8 * k : 8 * k + 8]
            first, second = column_groups(low_half, high_half)
            moved_ref[pl.ds(2 * k * col_total + 8 * at, 8), :] = first
            moved_ref[pl.ds((2 * k + 1) * col_total + 8 * at, 8), :] = second
    wide = 2 * LANES
    same = rows_iota((wide, wide)) // head_size == lanes_iota((wide, wide)) // head_size
    ones = jnp.where(same, 1.0, 0.0).astype(BF16)
    for block in range(forward_ref.shape[1] // wide):
        lanes = pl.ds(block * wide, wide)
        gate = gate_ref[:, lanes]
        combined = forward_ref[:, lanes] + moved_ref[:, lanes]
        gated = combined * (gate / (1.0 + jnp.exp(-gate)))
        high, low = split(gated * gated)
        mean = (dot(high, ones) + dot(low, ones)) * (1.0 / head_size)
        normed = gated * lax.rsqrt(mean + 1e-5) * gain_ref[:, lanes]
        out_ref[:, lanes] = normed.astype(out_ref.dtype)


def finish(forward, backward, gate, gain, row_part, col_total, head_size):
    tokens, inner = forward.shape
    groups = col_total // GROUP // 4
    block = 4 * col_total
    flat = pl.BlockSpec((block, inner), lambda m: (m, 0))
    return pl.pallas_call(
        functools.partial(finish_kernel, head_size, groups, row_part * GROUP),
        grid=(row_part // 4,),
        in_specs=[flat, whole(backward.shape), flat, whole((1, inner))],
        out_specs=flat,
        out_shape=jax.ShapeDtypeStruct((tokens, inner), BF16),
        scratch_shapes=[pltpu.VMEM((block, inner), F32)],
        compiler_params=params(),
    )(forward, backward, gate, gain)


def pad_lanes(source):
    return jnp.pad(source, ((0, 0), (0, LANES - source.shape[1])))


def local(tokens, xz_weight, state_weight, step_weight, step_bias, decay_rate, skip, norm_gain):
    videos, frame_count, row_part, col_total, width = tokens.shape
    flattened = tokens.reshape(-1, width)
    inner = xz_weight.shape[1] // 2
    heads = step_weight.shape[1]
    head_size = inner // heads
    column_rows = row_part * lax.axis_size("spatial")
    size = column_rows * GROUP
    axes = ("frame", "spatial")

    thrice = pad_lanes(jnp.concatenate([step_weight] * 3, axis=1))
    bias = pad_lanes(jnp.concatenate([step_bias] * 3)[None])
    first_weight = jnp.concatenate([state_weight, thrice], axis=1)
    rates = pad_lanes(decay_rate)
    skips = jnp.repeat(skip[0] + skip[1], head_size)[None]

    values, keys, columns, memory, total = project(
        flattened,
        first_weight,
        bias,
        rates[0:1],
        xz_weight,
        row_part,
        col_total,
        inner,
        head_size,
        512,
    )
    gate_part, total = lax.optimization_barrier((xz_weight[:, :inner], total))
    gate_weight = lax.all_gather(gate_part, ("spatial", "dp"), axis=0, tiled=True)
    rowwise = (values[None], keys[None])
    columnwise = (columns,)
    forward_entering, entering = entering_states(
        columns, rates[1:2], memory, total, inner, size, column_rows, head_size
    )
    backward = local_output(
        columnwise, rates[1:2], entering, None, inner, size, column_rows, head_size
    )
    returned = lax.all_to_all(backward, "spatial", 0, 0, tiled=True)
    forward = local_output(
        rowwise, rates[0:1], forward_entering, skips, inner, size, 0, head_size
    )
    gate_rows = jnp.dot(flattened, gate_weight, preferred_element_type=F32)
    normed = finish(
        forward[0], returned, gate_rows, norm_gain[None], row_part, col_total, head_size
    )
    return normed.reshape(videos, frame_count, row_part, col_total, inner)


def solution(mesh):
    in_specs = (
        P("dp", "frame", "spatial", None, None),
        P(("spatial", "dp"), None),
        P(("spatial", "dp"), None),
        P(("spatial", "dp"), None),
        P(),
        P(),
        P(),
        P(),
    )
    out_specs = P("dp", "frame", "spatial", None, None)
    return jax.shard_map(local, mesh=mesh, in_specs=in_specs, out_specs=out_specs, check_vma=False)
```

```python
import functools

import jax
import jax.numpy as jnp
from jax import lax
from jax.experimental import pallas as pl
from jax.experimental.pallas import tpu as pltpu
from jax.sharding import PartitionSpec as P

F32 = jnp.float32
BF16 = jnp.bfloat16
LANES = 128
GROUP = 4
POWER = 17
CODE_TOP = 128.0
STEP_LANES = 24
MESH = pl.DeviceIdType.MESH
VMEM_BYTES = 56 * 1024 * 1024


def split(value):
    high = value.astype(BF16)
    return high, (value - high.astype(F32)).astype(BF16)


def dot(a, b):
    return lax.dot_general(a, b, (((1,), (0,)), ((), ())), preferred_element_type=F32)


def rows_iota(shape):
    return lax.broadcasted_iota(jnp.int32, shape, 0)


def lanes_iota(shape):
    return lax.broadcasted_iota(jnp.int32, shape, 1)


def spread(columns, pair, head_size):
    first, second = columns[:, 2 * pair : 2 * pair + 1], columns[:, 2 * pair + 1 : 2 * pair + 2]
    shape = (columns.shape[0], LANES)
    return jnp.where(lanes_iota(shape) < head_size, first, second)


def params(semantics=("arbitrary",)):
    return pltpu.CompilerParams(vmem_limit_bytes=VMEM_BYTES, dimension_semantics=semantics)


def encode(scaled):
    square = scaled * scaled
    fourth = square * square
    eighth = fourth * fourth
    return (eighth * eighth * scaled).astype(BF16)


def decode(coded):
    coded = coded.astype(F32)
    size = jnp.exp2(jnp.log2(jnp.abs(coded)) * (1.0 / POWER))
    return jnp.where(coded < 0.0, -size, size)


def code_scale(largest):
    scale = jnp.maximum(largest, 1e-30).astype(BF16)
    return scale, CODE_TOP / scale.astype(F32)


def column_groups(first, second):
    low = rows_iota(first.shape) < GROUP
    even = jnp.where(low, first, pltpu.roll(second, GROUP, 0))
    odd = jnp.where(low, pltpu.roll(first, GROUP, 0), second)
    return even, odd


def earlier_mask(size, column_rows):
    shape = (size, size)
    t, s = rows_iota(shape), lanes_iota(shape)
    if column_rows:

        def place(index):
            return size - 1 - (lax.rem(index, GROUP) * column_rows + index // GROUP)

        t, s = place(t), place(s)
    return s <= t


def running_logs(steps, rate, earlier):
    logs = -steps * rate
    high, rest = split(logs)
    middle = logs - high.astype(F32)
    middle, low = split(middle)
    before = jnp.where(earlier, 1.0, 0.0).astype(BF16)
    running = dot(before, high) + dot(before, middle) + dot(before, low)
    return running, jnp.sum(logs, axis=0, keepdims=True)


def advance(memory, keys_t, weighted, decay):
    keys_high, keys_low = keys_t
    high, low = split(weighted)
    both = dot(keys_high, jnp.concatenate([high, low], axis=1))
    added = both[:, :LANES] + both[:, LANES:] + dot(keys_low, high)
    return memory * decay + added


def fold_chunk(values, keys, steps, rate, earlier, head_size, memory_ref, total_ref):
    keys_t = split(jnp.transpose(keys))
    running, total = running_logs(steps, rate, earlier)
    coefficient = steps * jnp.exp(jnp.minimum(total - running, 0.0))
    decay = jnp.exp(total)
    for pair in range(memory_ref.shape[1] // LANES):
        lanes = pl.ds(pair * LANES, LANES)
        weighted = values(pair) * spread(coefficient, pair, head_size)
        memory_ref[:, lanes] = advance(
            memory_ref[:, lanes], keys_t, weighted, spread(decay, pair, head_size)
        )
    total_ref[...] = total_ref[...] + total


def in_order(ref, depth):
    parts = []
    for row in range(16):
        where, part, core = row // 4, (row // 2) % 2, row % 2
        parts.append(ref[pl.ds((core * 8 + part * 4 + where) * depth, depth), :])
    return jnp.concatenate(parts, axis=0)


def gate_kernel(depth, tokens_ref, weight_ref, gate_ref):
    width = weight_ref.shape[2]
    for quarter in range(0, 4, 2):
        weight = jnp.concatenate(
            [in_order(weight_ref.at[quarter + k], depth) for k in range(2)], axis=1
        )
        gate_ref[:, pl.ds(quarter * width, 2 * width)] = dot(tokens_ref[...], weight)


def gate_rows_of(tokens, weight, depth):
    total, model = tokens.shape
    inner = 4 * weight.shape[2]
    tile = total // 5
    return pl.pallas_call(
        functools.partial(gate_kernel, depth),
        grid=(5,),
        in_specs=[pl.BlockSpec((tile, model), lambda m: (m, 0)), whole(weight.shape)],
        out_specs=pl.BlockSpec((tile, inner), lambda m: (m, 0)),
        out_shape=jax.ShapeDtypeStruct((total, inner), F32),
        cost_estimate=pl.CostEstimate(
            flops=2 * total * model * inner, bytes_accessed=20 << 20, transcendentals=0
        ),
        compiler_params=params(),
    )(tokens, weight)


def project_kernel(
    geometry,
    tokens_ref,
    state_ref,
    bias_ref,
    rate_ref,
    xz_ref,
    values_ref,
    keys_ref,
    columns_ref,
    memory_ref,
    total_ref,
    gate_ref,
    weight,
    gate_weight,
    product,
    middle,
    own_sem,
    x_send,
    x_recv,
    y_send,
    y_recv,
    core_send,
    core_recv,
    move_send,
    move_recv,
    move_own,
    out_sem,
    gate_send,
    gate_recv,
    gate_out,
):
    row_part, col_total, inner, depth, blocks, head_size = geometry
    half = depth // 2
    frame, place, part = lax.axis_index("frame"), lax.axis_index("spatial"), lax.axis_index("dp")
    core, y = part % 2, (frame % 2) * 2 + part // 2
    right, left, across = (place + 1) % 4, (place + 3) % 4, (place + 2) % 4

    z = frame // 2

    def z_device(other):
        return (other * 2 + frame % 2, place, part)

    def y_device(other):
        return ((frame // 2) * 2 + other // 2, place, (other % 2) * 2 + core)

    x_right, x_left, x_across = (frame, right, part), (frame, left, part), (frame, across, part)
    y_up, y_down = y_device((y + 1) % 4), y_device((y + 3) % 4)
    partner = (frame, place, (part // 2) * 2 + 1 - core)

    barrier = pltpu.get_barrier_semaphore()
    z_up, z_down = z_device((z + 1) % 4), z_device((z + 3) % 4)
    peers = (x_right, x_left, x_across, y_up, y_down, z_up, z_down, partner)
    for peer in peers:
        pl.semaphore_signal(barrier, inc=1, device_id=peer, device_id_type=MESH)
    pl.semaphore_wait(barrier, len(peers))

    def slot(where, other_core, other_part):
        return other_core * 8 + other_part * 4 + where

    same, opposite = part // 2, 1 - part // 2
    sources = (place, left, right, across)

    def rows(index, first, count):
        return pl.ds(pl.multiple_of(index * depth + first, 16), count)

    def view(block, index, first, count):
        return weight.at[block, rows(index, first, count), pl.ds(0, blocks[block][1])]

    def own(block, first, count):
        start, width = blocks[block]
        if block == 0:
            return state_ref.at[pl.ds(first, count), :]
        return xz_ref.at[pl.ds(first, count), pl.ds(inner + start, width)]

    pending = []

    def send(source, target, send_sem, recv_sem, device):
        copy = pltpu.make_async_remote_copy(
            src_ref=source,
            dst_ref=target,
            send_sem=send_sem,
            recv_sem=recv_sem,
            device_id=device,
            device_id_type=MESH,
        )
        copy.start()
        pending.append(copy)

    def arrived(target, send_sem, recv_sem):
        pltpu.make_async_remote_copy(
            src_ref=target,
            dst_ref=target,
            send_sem=send_sem,
            recv_sem=recv_sem,
            device_id=x_right,
            device_id_type=MESH,
        ).wait_recv()

    def send_y(block, which, source_of):
        index = slot(sources[which], core, same)
        for part_at, device in ((0, y_up), (1, y_down)):
            first = part_at * half
            send(
                source_of(first),
                view(block, index, first, half),
                y_send.at[block, which, part_at],
                y_recv.at[block, which, part_at],
                device,
            )

    def send_core(block, at, index, source):
        send(
            source,
            view(block, index, 0, depth),
            core_send.at[block, at],
            core_recv.at[block, at],
            partner,
        )

    def send_own(block):
        index = slot(place, core, same)
        target = view(block, index, 0, depth)
        source = own(block, 0, depth)
        send(source, target, x_send.at[block, 0], x_recv.at[block, 0], x_right)
        send(source, target, x_send.at[block, 1], x_recv.at[block, 1], x_left)
        send_y(block, 0, lambda first: own(block, first, half))
        send_core(block, 0, index, source)
        copy = pltpu.make_async_copy(source, target, own_sem.at[block])
        copy.start()

    def relay(block):
        from_left, from_right = slot(left, core, same), slot(right, core, same)
        for which, index in ((1, from_left), (2, from_right)):
            arrived(
                view(block, index, 0, depth),
                x_send.at[block, which - 1],
                x_recv.at[block, which - 1],
            )
            part_at = which - 1
            send(
                view(block, index, part_at * half, half),
                view(block, index, part_at * half, half),
                x_send.at[block, 2 + part_at],
                x_recv.at[block, 2 + part_at],
                (x_right, x_left)[part_at],
            )
            send_y(block, which, lambda first: view(block, index, first, half))
            send_core(block, which, index, view(block, index, 0, depth))
    def relay_far(block):
        far = slot(across, core, same)
        for part_at in (0, 1):
            arrived(
                view(block, far, part_at * half, half),
                x_send.at[block, 2 + part_at],
                x_recv.at[block, 2 + part_at],
            )
        send_y(block, 3, lambda first: view(block, far, first, half))
        send_core(block, 3, far, view(block, far, 0, depth))

    def pass_on(block):
        for which in range(4):
            index = slot(sources[which], core, opposite)
            for part_at in (0, 1):
                arrived(
                    view(block, index, part_at * half, half),
                    y_send.at[block, which, part_at],
                    y_recv.at[block, which, part_at],
                )
            send_core(block, 4 + which, index, view(block, index, 0, depth))

    def gathered(block):
        for at in range(8):
            index = slot(sources[at % 4], 1 - core, same if at < 4 else opposite)
            arrived(
                view(block, index, 0, depth), core_send.at[block, at], core_recv.at[block, at]
            )
        index = slot(place, core, same)
        target = view(block, index, 0, depth)
        pltpu.make_async_copy(own(block, 0, depth), target, own_sem.at[block]).wait()


    quarter_width = gate_weight.shape[2]
    many, core_rows = 4 * depth, 8 * depth

    def gate_view(quarter, first, rows_count):
        return gate_weight.at[quarter, pl.ds(pl.multiple_of(first, 16), rows_count), :]

    def gate_copy(source, at, device):
        send(source, source, gate_send.at[at], gate_recv.at[at], device)

    def gate_arrived(target, at):
        arrived(target, gate_send.at[at], gate_recv.at[at])

    def gate_own():
        first = pl.multiple_of(z * quarter_width, LANES)
        return xz_ref.at[:, pl.ds(first, quarter_width)]

    def gate_start():
        target = gate_view(z, slot(place, core, same) * depth, depth)
        send(gate_own(), target, gate_send.at[0], gate_recv.at[0], x_right)
        send(gate_own(), target, gate_send.at[1], gate_recv.at[1], x_left)
        pltpu.make_async_copy(gate_own(), target, own_sem.at[len(blocks)]).start()

    def gate_x():
        for at, index in ((0, slot(left, core, same)), (1, slot(right, core, same))):
            gate_arrived(gate_view(z, index * depth, depth), at)
            gate_copy(gate_view(z, index * depth + at * half, half), 2 + at, (x_right, x_left)[at])

    def gate_y():
        far = slot(across, core, same) * depth
        for at in (0, 1):
            gate_arrived(gate_view(z, far + at * half, half), 2 + at)
        target = gate_view(z, slot(place, core, same) * depth, depth)
        pltpu.make_async_copy(gate_own(), target, own_sem.at[len(blocks)]).wait()
        first = slot(0, core, same) * depth
        for at, device in ((0, y_up), (1, y_down)):
            gate_copy(gate_view(z, first + at * (many // 2), many // 2), 4 + at, device)

    def gate_z():
        first = slot(0, core, opposite) * depth
        for at in (0, 1):
            gate_arrived(gate_view(z, first + at * (many // 2), many // 2), 4 + at)
        mine = gate_view(z, core * core_rows, core_rows)
        gate_copy(mine, 6, z_up)
        gate_copy(mine, 7, z_down)
        gate_copy(mine, 10, partner)

    def gate_pass():
        for at, quarter in ((0, (z + 3) % 4), (1, (z + 1) % 4)):
            mine = gate_view(quarter, core * core_rows, core_rows)
            gate_arrived(mine, 6 + at)
            part_rows = gate_view(quarter, core * core_rows + at * many, many)
            gate_copy(part_rows, 8 + at, (z_up, z_down)[at])
            gate_copy(mine, 11 + at, partner)

    def gate_end():
        quarter = (z + 2) % 4
        for at in (0, 1):
            gate_arrived(gate_view(quarter, core * core_rows + at * many, many), 8 + at)
        gate_copy(gate_view(quarter, core * core_rows, core_rows), 13, partner)
        for at, quarter in enumerate((z, (z + 3) % 4, (z + 1) % 4, (z + 2) % 4)):
            gate_arrived(gate_view(quarter, (1 - core) * core_rows, core_rows), 10 + at)

    tokens = row_part * col_total
    tile = tokens // 5
    groups = col_total // GROUP // 4
    piece_rows = groups * row_part * GROUP
    outs = {}

    def compute(block):
        start, width = blocks[block]
        lanes = pl.ds(0, width)
        buffer = block

        def one_tile(i, largest):
            at = pl.ds(pl.multiple_of(i * tile, tile), tile)
            result = dot(tokens_ref[at, :], in_order(weight.at[block, :, lanes], depth))
            if block == 0:
                raw = result[:, width - LANES :] + bias_ref[...]
                steps = jnp.maximum(raw, 0.0) + jnp.log1p(jnp.exp(-jnp.abs(raw)))
                result = jnp.concatenate([result[:, : width - LANES], steps], axis=1)
            product[buffer, at, lanes] = result
            return jnp.maximum(largest, jnp.max(jnp.abs(result), axis=0, keepdims=True))

        largest = lax.fori_loop(0, 5, one_tile, jnp.zeros((1, width), F32))
        if block == 0:
            out = keys_ref
        else:
            out = values_ref.at[:, pl.ds(start, width)]
        copy = pltpu.make_async_copy(product.at[buffer, :, lanes], out, out_sem.at[block])
        copy.start()
        outs[block] = copy

        scale, factor = code_scale(largest)

        def code(value):
            coded = encode(value * factor)
            if block == 0:
                exact = value[:, width - LANES :]
                high = exact.astype(BF16)
                rest = exact - high.astype(F32)
                second = rest.astype(BF16)
                third = (rest - second.astype(F32)).astype(BF16)
                lane = lanes_iota(exact.shape)
                heads = STEP_LANES
                parts = jnp.where(
                    lane < heads,
                    high.astype(F32),
                    jnp.where(lane < 2 * heads, second.astype(F32), third.astype(F32)),
                )
                coded = jnp.concatenate([coded[:, : width - LANES], parts.astype(BF16)], axis=1)
            return coded

        for quad in range(row_part // 4):

            def one_group(at, carry):
                both = []
                for pair in (2 * quad, 2 * quad + 1):
                    first = product[buffer, pl.ds(pl.multiple_of(2 * pair * col_total + 8 * at, 8), 8), lanes]
                    second = product[
                        buffer, pl.ds(pl.multiple_of((2 * pair + 1) * col_total + 8 * at, 8), 8), lanes
                    ]
                    both.append(column_groups(first, second))
                for odd in (0, 1):
                    group = 2 * at + odd
                    piece = group // groups
                    row = pl.multiple_of((group % groups) * row_part * GROUP + 16 * quad, 16)
                    value = jnp.concatenate([both[0][odd], both[1][odd]], axis=0)
                    middle[block, piece, pl.ds(row, 16), lanes] = code(value)
                return carry

            lax.fori_loop(0, col_total // 8, one_group, 0)
        for piece in range(4):
            middle[block, piece, pl.ds(piece_rows, 16), lanes] = jnp.broadcast_to(scale, (16, width))
        into = columns_ref.at[place, :, pl.ds(inner if block == 0 else start, width)]
        for at, (where, device) in enumerate(((right, x_right), (left, x_left), (across, x_across))):
            send(
                middle.at[block, where, :, lanes],
                into,
                move_send.at[block, at],
                move_recv.at[block, at],
                device,
            )
        pltpu.make_async_copy(middle.at[block, place, :, lanes], into, move_own.at[block]).start()

    count = len(blocks)
    for block in range(count):
        send_own(block)
    gate_start()
    relay(0)
    relay(1)
    gate_x()
    relay_far(0)
    for block in range(count):
        if block + 2 < count:
            relay(block + 2)
        if block + 1 < count:
            relay_far(block + 1)
        if block < 2:
            (gate_y, gate_z)[block]()
        pass_on(block)
        gathered(block)
        compute(block)

    gate_pass()
    memory_ref[...] = jnp.zeros_like(memory_ref)
    total_ref[...] = jnp.zeros_like(total_ref)

    def fold_rows(step, carry):
        at = pl.ds(pl.multiple_of(step * tile, 16), tile)
        block_pairs = blocks[1][1] // LANES

        def values(pair):
            return product[1 + pair // block_pairs, at, pl.ds(pair % block_pairs * LANES, LANES)]

        fold_chunk(
            values,
            product[0, at, pl.ds(0, LANES)],
            product[0, at, pl.ds(2 * LANES, LANES)],
            rate_ref[...],
            earlier_mask(tile, 0),
            head_size,
            memory_ref,
            total_ref,
        )
        return carry

    lax.fori_loop(0, 5, fold_rows, 0)
    gate_end()
    gate_copies = [
        pltpu.make_async_copy(gate_weight.at[quarter], gate_ref.at[quarter], gate_out.at[quarter])
        for quarter in range(4)
    ]
    for copy in gate_copies:
        copy.start()
    for block in range(count):
        start, width = blocks[block]
        lanes = pl.ds(0, width)
        for at, where in enumerate((left, right, across)):
            into = columns_ref.at[where, :, pl.ds(inner if block == 0 else start, width)]
            arrived(into, move_send.at[block, at], move_recv.at[block, at])
        into = columns_ref.at[place, :, pl.ds(inner if block == 0 else start, width)]
        pltpu.make_async_copy(middle.at[block, place, :, lanes], into, move_own.at[block]).wait()
    for copy in list(outs.values()) + gate_copies:
        copy.wait()
    for copy in pending:
        copy.wait_send()


def project(tokens, state_weight, bias, rate, xz_weight, row_part, col_total, inner, head_size, block_width):
    depth, state_width = state_weight.shape
    count = inner // block_width + 1
    blocks = ((0, state_width),) + tuple((k * block_width, block_width) for k in range(count - 1))
    width = max(block_width, state_width)
    total = tokens.shape[0]
    piece_rows = total // 4 + 16
    vmem, hbm = pl.BlockSpec(memory_space=pltpu.VMEM), pl.BlockSpec(memory_space=pl.ANY)
    dma = pltpu.SemaphoreType.DMA
    return pl.pallas_call(
        functools.partial(project_kernel, (row_part, col_total, inner, depth, blocks, head_size)),
        in_specs=[vmem, vmem, vmem, vmem, hbm],
        out_specs=[hbm, hbm, hbm, vmem, vmem, hbm],
        out_shape=[
            jax.ShapeDtypeStruct((total, inner), F32),
            jax.ShapeDtypeStruct((total, state_width), F32),
            jax.ShapeDtypeStruct((4, piece_rows, inner + state_width), BF16),
            jax.ShapeDtypeStruct((LANES, inner), F32),
            jax.ShapeDtypeStruct((8, LANES), F32),
            jax.ShapeDtypeStruct((4, tokens.shape[1], inner // 4), BF16),
        ],
        scratch_shapes=[
            pltpu.VMEM((count, tokens.shape[1], width), BF16),
            pltpu.VMEM((4, tokens.shape[1], inner // 4), BF16),
            pltpu.VMEM((count, total, width), F32),
            pltpu.VMEM((count, 4, piece_rows, width), BF16),
            dma((count + 1,)),
            dma((count, 4)),
            dma((count, 4)),
            dma((count, 4, 2)),
            dma((count, 4, 2)),
            dma((count, 8)),
            dma((count, 8)),
            dma((count, 3)),
            dma((count, 3)),
            dma((count,)),
            dma((count,)),
            dma((14,)),
            dma((14,)),
            dma((4,)),
        ],
        compiler_params=pltpu.CompilerParams(
            collective_id=0, has_side_effects=True, vmem_limit_bytes=VMEM_BYTES
        ),
    )(tokens, state_weight, bias, rate, xz_weight)


class Chunk:
    def __init__(self, column_rows, values_ref, keys_ref, steps_ref, scale_ref):
        self.size = values_ref.shape[0] * values_ref.shape[1]
        self.inner = values_ref.shape[2]
        self.pairs = self.inner // LANES
        self.column_rows, self.values_ref, self.scale_ref = column_rows, values_ref, scale_ref
        self.keys_ref, self.steps_ref = keys_ref, steps_ref
        if column_rows:
            self.scales = [scale_ref[k, pl.ds(0, 16), :].astype(F32)[0:1] for k in range(4)]

    def read(self, ref, lanes, scale_lane):
        block = ref[:, :, lanes]
        if not self.column_rows:
            return block.reshape(self.size, LANES)
        block = decode(block)
        parts = [
            block[k] * (self.scales[k][:, scale_lane : scale_lane + LANES] * (1.0 / CODE_TOP))
            for k in range(4)
        ]
        return jnp.concatenate(parts, axis=0)

    def values(self, pair):
        return self.read(self.values_ref, pl.ds(pair * LANES, LANES), pair * LANES)

    def keys(self):
        return self.read(self.keys_ref, pl.ds(0, LANES), self.inner)

    def queries(self, ref):
        return self.read(ref, pl.ds(0, LANES), self.inner + LANES)

    def steps(self):
        block = self.steps_ref[...].reshape(self.size, LANES)
        if not self.column_rows:
            return block
        shape = (LANES, LANES)
        part, head = rows_iota(shape), lanes_iota(shape)
        fold = (lax.rem(part, STEP_LANES) == head) & (part < 3 * STEP_LANES)
        return dot(block, jnp.where(fold, 1.0, 0.0).astype(BF16))

    def earlier(self):
        return earlier_mask(self.size, self.column_rows)


def output_kernel(column_rows, head_size, values_ref, keys_ref, steps_ref, *rest):
    if column_rows:
        scale_ref, queries_ref, rate_ref, entering_ref, out_ref, memory_ref, scales_ref = rest
        skip_ref = None
    else:
        queries_ref, rate_ref, entering_ref, skip_ref, out_ref, memory_ref = rest
        scale_ref = None
    chunk = Chunk(column_rows, values_ref, keys_ref, steps_ref, scale_ref)
    size = chunk.size

    @pl.when(pl.program_id(0) == 0)
    def _():
        memory_ref[...] = entering_ref[...]
        if column_rows:
            scales_ref[...] = jnp.zeros_like(scales_ref)

    steps = chunk.steps()
    keys_t = split(jnp.transpose(chunk.keys()))
    queries_high, queries_low = split(chunk.queries(queries_ref))
    earlier = chunk.earlier()
    running, total = running_logs(steps, rate_ref[...], earlier)
    across = jnp.transpose(running)
    scores = dot(queries_high, keys_t[0]) + dot(queries_high, keys_t[1]) + dot(queries_low, keys_t[0])
    scores = jnp.where(earlier, scores, 0.0)
    arrived = jnp.exp(running)
    leaving = jnp.exp(jnp.minimum(total - running, 0.0))
    decay = jnp.exp(total)
    first_half = lanes_iota((size, LANES)) < head_size
    at = pl.num_programs(0) - 1 - pl.program_id(0)
    for pair in range(chunk.pairs):
        lanes = pl.ds(pair * LANES, LANES)
        values = chunk.values(pair)
        scaled = values * spread(steps, pair, head_size)
        high, low = split(scaled)
        both = jnp.concatenate([high, low], axis=1)
        halves = []
        for head in (2 * pair, 2 * pair + 1):
            between = jnp.minimum(running[:, head : head + 1] - across[head : head + 1, :], 0.0)
            kernel_high, kernel_low = split(jnp.exp(between) * scores)
            part = dot(kernel_high, both)
            halves.append(part[:, :LANES] + part[:, LANES:] + dot(kernel_low, high))
        memory = memory_ref[:, lanes]
        memory_high, memory_low = split(memory)
        part = dot(queries_high, jnp.concatenate([memory_high, memory_low], axis=1))
        carried = part[:, :LANES] + part[:, LANES:] + dot(queries_low, memory_high)
        result = jnp.where(first_half, halves[0], halves[1])
        result = result + carried * spread(arrived, pair, head_size)
        if column_rows:
            scale, factor = code_scale(jnp.max(jnp.abs(result), axis=0, keepdims=True))
            coded = encode(result * factor).reshape(4, size // 4, LANES)
            first = pl.multiple_of(at * (size // 4), 16)
            out_ref[:, pl.ds(first, size // 4), lanes] = coded
            here = rows_iota((16, LANES)) == at
            scales_ref[:, lanes] = jnp.where(here, scale.astype(F32), scales_ref[:, lanes])
        else:
            result = result + values * skip_ref[:, lanes]
            out_ref[:, :, lanes] = result.reshape(1, size, LANES)
        weighted = scaled * spread(leaving, pair, head_size)
        memory_ref[:, lanes] = advance(memory, keys_t, weighted, spread(decay, pair, head_size))

    if column_rows:

        @pl.when(pl.program_id(0) == pl.num_programs(0) - 1)
        def _():
            scales = scales_ref[...].astype(BF16)
            for k in range(4):
                out_ref[k, pl.ds(out_ref.shape[1] - 16, 16), :] = scales


def chunk_specs(sources, inner, size, column_rows):
    pieces = 4 if column_rows else 1
    part = size // pieces
    count = sources[0].shape[1] // part
    first = inner // LANES if column_rows else 0

    def spec(lane_count, lane_block):
        def index(j):
            return (0, count - 1 - j if column_rows else j, lane_block)

        return pl.BlockSpec((pieces, part, lane_count), index)

    specs = [spec(inner, 0), spec(LANES, first), spec(LANES, first + 2)]
    arrays = [sources[0], sources[-1], sources[-1]]
    if column_rows:
        last = sources[0].shape[1] // 16 - 1
        specs.append(pl.BlockSpec((pieces, 16, sources[0].shape[2]), lambda j: (0, last, 0)))
        arrays.append(sources[0])
    return count, specs, arrays, spec(LANES, first + 1)


def whole(shape):
    return pl.BlockSpec(shape, lambda j: (0,) * len(shape))


def estimate(tokens, inner, passes, transfers):
    return pl.CostEstimate(
        flops=2 * tokens * inner * 192 * passes, bytes_accessed=transfers, transcendentals=0
    )


def local_output(sources, rate, entering, skip, inner, size, column_rows, head_size):
    count, specs, arrays, queries = chunk_specs(sources, inner, size, column_rows)
    shape = sources[0].shape[:2] + (inner,)
    extra = [] if column_rows else [skip]
    scratch = [pltpu.VMEM((LANES, inner), F32)]
    if column_rows:
        scratch.append(pltpu.VMEM((16, inner), F32))
    return pl.pallas_call(
        functools.partial(output_kernel, column_rows, head_size),
        grid=(count,),
        in_specs=specs
        + [queries, whole((1, LANES)), whole((LANES, inner))]
        + [whole((1, inner)) for _ in extra],
        out_specs=whole(shape) if column_rows else specs[0],
        out_shape=jax.ShapeDtypeStruct(shape, BF16 if column_rows else F32),
        scratch_shapes=scratch,
        cost_estimate=estimate(count * size, inner, 30, 32 << 20),
        compiler_params=params(),
    )(*arrays, sources[-1], rate, entering, *extra)


def states_kernel(
    geometry,
    columns_ref,
    rate_ref,
    forward_ref,
    forward_total_ref,
    entering_forward_ref,
    entering_backward_ref,
    memory,
    total,
    sent,
    received,
    found,
    out_send,
    out_recv,
    back_send,
    back_recv,
    own_sem,
):
    inner, size, column_rows, head_size, count, spatial = geometry
    slices = count // 2
    rows, wide = LANES // slices, inner // 2
    pairs = wide // LANES
    frame, place, part = lax.axis_index("frame"), lax.axis_index("spatial"), lax.axis_index("dp")
    me = frame * spatial + place

    def device(index):
        return (index // spatial, index % spatial, part)

    barrier = pltpu.get_barrier_semaphore()

    def greet(k, carry):
        peer = device((me + k) % count)
        pl.semaphore_signal(barrier, inc=1, device_id=peer, device_id_type=MESH)
        return carry

    lax.fori_loop(1, count, greet, 0)
    pl.semaphore_wait(barrier, count - 1)

    def send_slices(way, memory_ref, total_ref):
        totals = total_ref[...]
        shifted = pltpu.roll(totals, LANES - 2 * pairs, 1)
        for index in range(count):
            first, lane = rows * (index // 2), wide * (index % 2)
            sent[way, index, :, pl.ds(0, wide)] = memory_ref[pl.ds(first, rows), pl.ds(lane, wide)]
            sent[way, index, :, pl.ds(wide, LANES)] = shifted if index % 2 else totals

        def one(k, carry):
            to = (me + k) % count
            pltpu.make_async_remote_copy(
                src_ref=sent.at[way, to],
                dst_ref=received.at[way, me],
                send_sem=out_send.at[way, k],
                recv_sem=out_recv.at[way, k],
                device_id=device(to),
                device_id_type=MESH,
            ).start()
            return carry

        lax.fori_loop(1, count, one, 0)
        received[way, me] = sent[way, me]

    def scan(way, reverse, entering_ref):
        def arrive(k, carry):
            source = (me + count - k) % count
            pltpu.make_async_remote_copy(
                src_ref=received.at[way, source],
                dst_ref=received.at[way, source],
                send_sem=out_send.at[way, k],
                recv_sem=out_recv.at[way, k],
                device_id=device(source),
                device_id_type=MESH,
            ).wait_recv()
            return carry

        lax.fori_loop(1, count, arrive, 0)
        entering = jnp.zeros((rows, wide), F32)
        for k in range(count):
            at = count - 1 - k if reverse else k
            found[way, at] = entering
            decay = jnp.exp(received[way, at, :, pl.ds(wide, LANES)])
            spreads = [spread(decay, pair, head_size) for pair in range(pairs)]
            decay = jnp.concatenate(spreads, axis=1)
            entering = entering * decay + received[way, at, :, pl.ds(0, wide)]

        def one(k, carry):
            to = (me + k) % count
            pltpu.make_async_remote_copy(
                src_ref=found.at[way, to],
                dst_ref=place_of(entering_ref, me),
                send_sem=back_send.at[way, k],
                recv_sem=back_recv.at[way, k],
                device_id=device(to),
                device_id_type=MESH,
            ).start()
            return carry

        lax.fori_loop(1, count, one, 0)
        copy = pltpu.make_async_copy(found.at[way, me], place_of(entering_ref, me), own_sem.at[way])
        copy.start()

    def place_of(entering_ref, index):
        first = pl.multiple_of(rows * (index // 2), rows)
        lane = pl.multiple_of(wide * (index % 2), LANES)
        return entering_ref.at[pl.ds(first, rows), pl.ds(lane, wide)]

    def finish_way(way, entering_ref):
        def arrive(k, carry):
            source = (me + count - k) % count
            to = (me + k) % count
            pltpu.make_async_remote_copy(
                src_ref=found.at[way, source],
                dst_ref=place_of(entering_ref, source),
                send_sem=back_send.at[way, k],
                recv_sem=back_recv.at[way, k],
                device_id=device(to),
                device_id_type=MESH,
            ).wait()
            pltpu.make_async_remote_copy(
                src_ref=sent.at[way, to],
                dst_ref=received.at[way, me],
                send_sem=out_send.at[way, k],
                recv_sem=out_recv.at[way, k],
                device_id=device(to),
                device_id_type=MESH,
            ).wait_send()
            return carry

        lax.fori_loop(1, count, arrive, 0)
        pltpu.make_async_copy(
            found.at[way, me], place_of(entering_ref, me), own_sem.at[way]
        ).wait()

    send_slices(0, forward_ref, forward_total_ref)
    memory[...] = jnp.zeros_like(memory)
    total[...] = jnp.zeros_like(total)
    chunks = (columns_ref.shape[1] - 16) // (size // 4)
    last = columns_ref.shape[1] - 16

    def fold_columns(step, carry):
        at = pl.ds(pl.multiple_of((chunks - 1 - step) * (size // 4), 16), size // 4)
        chunk = Chunk(
            column_rows,
            columns_ref.at[:, at, pl.ds(0, inner)],
            columns_ref.at[:, at, pl.ds(inner, LANES)],
            columns_ref.at[:, at, pl.ds(inner + 2 * LANES, LANES)],
            columns_ref.at[:, pl.ds(last, 16), :],
        )
        fold_chunk(
            chunk.values,
            chunk.keys(),
            chunk.steps(),
            rate_ref[...],
            chunk.earlier(),
            head_size,
            memory,
            total,
        )
        return carry

    lax.fori_loop(0, chunks, fold_columns, 0)
    send_slices(1, memory, total)
    scan(0, False, entering_forward_ref)
    scan(1, True, entering_backward_ref)
    finish_way(0, entering_forward_ref)
    finish_way(1, entering_backward_ref)


def entering_states(columns, rate, memory, total, inner, size, column_rows, head_size):
    spatial = lax.axis_size("spatial")
    count = lax.axis_size("frame") * spatial
    rows, wide = LANES * 2 // count, inner // 2
    vmem, hbm = pl.BlockSpec(memory_space=pltpu.VMEM), pl.BlockSpec(memory_space=pl.ANY)
    dma = pltpu.SemaphoreType.DMA
    state = jax.ShapeDtypeStruct((LANES, inner), F32)
    geometry = (inner, size, column_rows, head_size, count, spatial)
    return pl.pallas_call(
        functools.partial(states_kernel, geometry),
        in_specs=[vmem] * 4,
        out_specs=[hbm, hbm],
        out_shape=[state, state],
        scratch_shapes=[
            pltpu.VMEM((LANES, inner), F32),
            pltpu.VMEM((8, LANES), F32),
            pltpu.VMEM((2, count, rows, wide + LANES), F32),
            pltpu.VMEM((2, count, rows, wide + LANES), F32),
            pltpu.VMEM((2, count, rows, wide), F32),
            dma((2, count)),
            dma((2, count)),
            dma((2, count)),
            dma((2, count)),
            dma((2,)),
        ],
        compiler_params=pltpu.CompilerParams(
            collective_id=1, has_side_effects=True, vmem_limit_bytes=VMEM_BYTES
        ),
    )(columns, rate, memory, total)


def finish_kernel(head_size, groups, part, forward_ref, backward_ref, gate_ref, gain_ref, out_ref, moved_ref):
    col_total = forward_ref.shape[0] // 4
    quad = pl.program_id(0)
    last = backward_ref.shape[1] - 16
    scales = [backward_ref[k, pl.ds(last, 16), :].astype(F32) * (1.0 / CODE_TOP) for k in range(4)]

    def group_rows(group):
        piece, within = group // groups, group % groups
        first = pl.multiple_of(within * part + 16 * quad, 16)
        coded = backward_ref[piece, pl.ds(first, 16), :]
        return decode(coded) * scales[piece][within : within + 1, :]

    for at in range(col_total // 8):
        even, odd = group_rows(2 * at), group_rows(2 * at + 1)
        for k in (0, 1):
            low_half, high_half = even[8 * k : 8 * k + 8], odd[8 * k : 8 * k + 8]
            first, second = column_groups(low_half, high_half)
            moved_ref[pl.ds(2 * k * col_total + 8 * at, 8), :] = first
            moved_ref[pl.ds((2 * k + 1) * col_total + 8 * at, 8), :] = second
    wide = 2 * LANES
    same = rows_iota((wide, wide)) // head_size == lanes_iota((wide, wide)) // head_size
    ones = jnp.where(same, 1.0, 0.0).astype(BF16)
    for block in range(forward_ref.shape[1] // wide):
        lanes = pl.ds(block * wide, wide)
        gate = gate_ref[:, lanes]
        combined = forward_ref[:, lanes] + moved_ref[:, lanes]
        gated = combined * (gate / (1.0 + jnp.exp(-gate)))
        high, low = split(gated * gated)
        mean = (dot(high, ones) + dot(low, ones)) * (1.0 / head_size)
        normed = gated * lax.rsqrt(mean + 1e-5) * gain_ref[:, lanes]
        out_ref[:, lanes] = normed.astype(out_ref.dtype)


def finish(forward, backward, gate, gain, row_part, col_total, head_size):
    tokens, inner = forward.shape
    groups = col_total // GROUP // 4
    block = 4 * col_total
    flat = pl.BlockSpec((block, inner), lambda m: (m, 0))
    return pl.pallas_call(
        functools.partial(finish_kernel, head_size, groups, row_part * GROUP),
        grid=(row_part // 4,),
        in_specs=[flat, whole(backward.shape), flat, whole((1, inner))],
        out_specs=flat,
        out_shape=jax.ShapeDtypeStruct((tokens, inner), BF16),
        scratch_shapes=[pltpu.VMEM((block, inner), F32)],
        compiler_params=params(),
    )(forward, backward, gate, gain)


def pad_lanes(source):
    return jnp.pad(source, ((0, 0), (0, LANES - source.shape[1])))


def local(tokens, xz_weight, state_weight, step_weight, step_bias, decay_rate, skip, norm_gain):
    videos, frame_count, row_part, col_total, width = tokens.shape
    flattened = tokens.reshape(-1, width)
    inner = xz_weight.shape[1] // 2
    heads = step_weight.shape[1]
    head_size = inner // heads
    column_rows = row_part * lax.axis_size("spatial")
    size = column_rows * GROUP
    axes = ("frame", "spatial")

    thrice = pad_lanes(jnp.concatenate([step_weight] * 3, axis=1))
    bias = pad_lanes(jnp.concatenate([step_bias] * 3)[None])
    first_weight = jnp.concatenate([state_weight, thrice], axis=1)
    rates = pad_lanes(decay_rate)
    skips = jnp.repeat(skip[0] + skip[1], head_size)[None]

    values, keys, columns, memory, total, gate_weight = project(
        flattened,
        first_weight,
        bias,
        rates[0:1],
        xz_weight,
        row_part,
        col_total,
        inner,
        head_size,
        512,
    )
    rowwise = (values[None], keys[None])
    columnwise = (columns,)
    forward_entering, entering = entering_states(
        columns, rates[1:2], memory, total, inner, size, column_rows, head_size
    )
    backward = local_output(
        columnwise, rates[1:2], entering, None, inner, size, column_rows, head_size
    )
    returned = lax.all_to_all(backward, "spatial", 0, 0, tiled=True)
    forward = local_output(
        rowwise, rates[0:1], forward_entering, skips, inner, size, 0, head_size
    )
    gate_weight, forward = lax.optimization_barrier((gate_weight, forward))
    gate_rows = gate_rows_of(flattened, gate_weight, xz_weight.shape[0])
    normed = finish(
        forward[0], returned, gate_rows, norm_gain[None], row_part, col_total, head_size
    )
    return normed.reshape(videos, frame_count, row_part, col_total, inner)


def solution(mesh):
    in_specs = (
        P("dp", "frame", "spatial", None, None),
        P(("spatial", "dp"), None),
        P(("spatial", "dp"), None),
        P(("spatial", "dp"), None),
        P(),
        P(),
        P(),
        P(),
    )
    out_specs = P("dp", "frame", "spatial", None, None)
    return jax.shard_map(local, mesh=mesh, in_specs=in_specs, out_specs=out_specs, check_vma=False)
```

```python
import functools

import jax
import jax.numpy as jnp
from jax import lax
from jax.experimental import pallas as pl
from jax.experimental.pallas import tpu as pltpu
from jax.sharding import PartitionSpec as P

F32 = jnp.float32
BF16 = jnp.bfloat16
LANES = 128
GROUP = 4
POWER = 17
CODE_TOP = 128.0
STEP_LANES = 24
MESH = pl.DeviceIdType.MESH
VMEM_BYTES = 56 * 1024 * 1024


def split(value):
    high = value.astype(BF16)
    return high, (value - high.astype(F32)).astype(BF16)


def dot(a, b):
    return lax.dot_general(a, b, (((1,), (0,)), ((), ())), preferred_element_type=F32)


def rows_iota(shape):
    return lax.broadcasted_iota(jnp.int32, shape, 0)


def lanes_iota(shape):
    return lax.broadcasted_iota(jnp.int32, shape, 1)


def spread(columns, pair, head_size):
    first, second = columns[:, 2 * pair : 2 * pair + 1], columns[:, 2 * pair + 1 : 2 * pair + 2]
    shape = (columns.shape[0], LANES)
    return jnp.where(lanes_iota(shape) < head_size, first, second)


def params(semantics=("arbitrary",)):
    return pltpu.CompilerParams(vmem_limit_bytes=VMEM_BYTES, dimension_semantics=semantics)


def encode(scaled):
    square = scaled * scaled
    fourth = square * square
    eighth = fourth * fourth
    return (eighth * eighth * scaled).astype(BF16)


def decode(coded):
    coded = coded.astype(F32)
    size = jnp.exp2(jnp.log2(jnp.abs(coded)) * (1.0 / POWER))
    return jnp.where(coded < 0.0, -size, size)


def code_scale(largest):
    scale = jnp.maximum(largest, 1e-30).astype(BF16)
    return scale, CODE_TOP / scale.astype(F32)


def column_groups(first, second):
    low = rows_iota(first.shape) < GROUP
    even = jnp.where(low, first, pltpu.roll(second, GROUP, 0))
    odd = jnp.where(low, pltpu.roll(first, GROUP, 0), second)
    return even, odd


def earlier_mask(size, column_rows):
    shape = (size, size)
    t, s = rows_iota(shape), lanes_iota(shape)
    if column_rows:

        def place(index):
            return size - 1 - (lax.rem(index, GROUP) * column_rows + index // GROUP)

        t, s = place(t), place(s)
    return s <= t


def running_logs(steps, rate, earlier):
    logs = -steps * rate
    high, rest = split(logs)
    middle = logs - high.astype(F32)
    middle, low = split(middle)
    before = jnp.where(earlier, 1.0, 0.0).astype(BF16)
    running = dot(before, high) + dot(before, middle) + dot(before, low)
    return running, jnp.sum(logs, axis=0, keepdims=True)


def advance(memory, keys_t, weighted, decay):
    keys_high, keys_low = keys_t
    high, low = split(weighted)
    both = dot(keys_high, jnp.concatenate([high, low], axis=1))
    added = both[:, :LANES] + both[:, LANES:] + dot(keys_low, high)
    return memory * decay + added


def fold_chunk(values, keys, steps, rate, earlier, head_size, memory_ref, total_ref):
    keys_t = split(jnp.transpose(keys))
    running, total = running_logs(steps, rate, earlier)
    coefficient = steps * jnp.exp(jnp.minimum(total - running, 0.0))
    decay = jnp.exp(total)
    for pair in range(memory_ref.shape[1] // LANES):
        lanes = pl.ds(pair * LANES, LANES)
        weighted = values(pair) * spread(coefficient, pair, head_size)
        memory_ref[:, lanes] = advance(
            memory_ref[:, lanes], keys_t, weighted, spread(decay, pair, head_size)
        )
    total_ref[...] = total_ref[...] + total


def in_order(ref, depth):
    parts = []
    for row in range(16):
        where, part, core = row // 4, (row // 2) % 2, row % 2
        parts.append(ref[pl.ds((core * 8 + part * 4 + where) * depth, depth), :])
    return jnp.concatenate(parts, axis=0)


def gate_kernel(depth, tokens_ref, weight_ref, gate_ref):
    width = weight_ref.shape[2]
    for quarter in range(0, 4, 2):
        weight = jnp.concatenate(
            [in_order(weight_ref.at[quarter + k], depth) for k in range(2)], axis=1
        )
        gate_ref[:, pl.ds(quarter * width, 2 * width)] = dot(tokens_ref[...], weight)


def gate_rows_of(tokens, weight, depth):
    total, model = tokens.shape
    inner = 4 * weight.shape[2]
    tile = total // 5
    return pl.pallas_call(
        functools.partial(gate_kernel, depth),
        grid=(5,),
        in_specs=[pl.BlockSpec((tile, model), lambda m: (m, 0)), whole(weight.shape)],
        out_specs=pl.BlockSpec((tile, inner), lambda m: (m, 0)),
        out_shape=jax.ShapeDtypeStruct((total, inner), F32),
        cost_estimate=pl.CostEstimate(
            flops=2 * total * model * inner, bytes_accessed=20 << 20, transcendentals=0
        ),
        compiler_params=params(),
    )(tokens, weight)


def project_kernel(
    geometry,
    tokens_ref,
    state_ref,
    bias_ref,
    rate_ref,
    xz_ref,
    values_ref,
    keys_ref,
    columns_ref,
    memory_ref,
    total_ref,
    gate_ref,
    weight,
    gate_weight,
    product,
    middle,
    own_sem,
    x_send,
    x_recv,
    y_send,
    y_recv,
    core_send,
    core_recv,
    move_send,
    move_recv,
    move_own,
    out_sem,
    gate_send,
    gate_recv,
    gate_out,
):
    row_part, col_total, inner, depth, blocks, head_size = geometry
    half = depth // 2
    frame, place, part = lax.axis_index("frame"), lax.axis_index("spatial"), lax.axis_index("dp")
    core, y = part % 2, (frame % 2) * 2 + part // 2
    right, left, across = (place + 1) % 4, (place + 3) % 4, (place + 2) % 4

    z = frame // 2

    def z_device(other):
        return (other * 2 + frame % 2, place, part)

    def y_device(other):
        return ((frame // 2) * 2 + other // 2, place, (other % 2) * 2 + core)

    x_right, x_left, x_across = (frame, right, part), (frame, left, part), (frame, across, part)
    y_up, y_down = y_device((y + 1) % 4), y_device((y + 3) % 4)
    partner = (frame, place, (part // 2) * 2 + 1 - core)

    barrier = pltpu.get_barrier_semaphore()
    z_up, z_down = z_device((z + 1) % 4), z_device((z + 3) % 4)
    peers = (x_right, x_left, x_across, y_up, y_down, z_up, z_down, partner)
    for peer in peers:
        pl.semaphore_signal(barrier, inc=1, device_id=peer, device_id_type=MESH)
    pl.semaphore_wait(barrier, len(peers))

    def slot(where, other_core, other_part):
        return other_core * 8 + other_part * 4 + where

    same, opposite = part // 2, 1 - part // 2
    sources = (place, left, right, across)

    def rows(index, first, count):
        return pl.ds(pl.multiple_of(index * depth + first, 16), count)

    def view(block, index, first, count):
        return weight.at[block, rows(index, first, count), pl.ds(0, blocks[block][1])]

    def own(block, first, count):
        start, width = blocks[block]
        if block == 0:
            return state_ref.at[pl.ds(first, count), :]
        return xz_ref.at[pl.ds(first, count), pl.ds(inner + start, width)]

    pending = []

    def send(source, target, send_sem, recv_sem, device):
        copy = pltpu.make_async_remote_copy(
            src_ref=source,
            dst_ref=target,
            send_sem=send_sem,
            recv_sem=recv_sem,
            device_id=device,
            device_id_type=MESH,
        )
        copy.start()
        pending.append(copy)

    def arrived(target, send_sem, recv_sem):
        pltpu.make_async_remote_copy(
            src_ref=target,
            dst_ref=target,
            send_sem=send_sem,
            recv_sem=recv_sem,
            device_id=x_right,
            device_id_type=MESH,
        ).wait_recv()

    def send_y(block, which, source_of):
        index = slot(sources[which], core, same)
        for part_at, device in ((0, y_up), (1, y_down)):
            first = part_at * half
            send(
                source_of(first),
                view(block, index, first, half),
                y_send.at[block, which, part_at],
                y_recv.at[block, which, part_at],
                device,
            )

    def send_core(block, at, index, source):
        send(
            source,
            view(block, index, 0, depth),
            core_send.at[block, at],
            core_recv.at[block, at],
            partner,
        )

    def send_own(block):
        index = slot(place, core, same)
        target = view(block, index, 0, depth)
        source = own(block, 0, depth)
        send(source, target, x_send.at[block, 0], x_recv.at[block, 0], x_right)
        send(source, target, x_send.at[block, 1], x_recv.at[block, 1], x_left)
        send_y(block, 0, lambda first: own(block, first, half))
        send_core(block, 0, index, source)
        copy = pltpu.make_async_copy(source, target, own_sem.at[block])
        copy.start()

    def relay(block):
        from_left, from_right = slot(left, core, same), slot(right, core, same)
        for which, index in ((1, from_left), (2, from_right)):
            arrived(
                view(block, index, 0, depth),
                x_send.at[block, which - 1],
                x_recv.at[block, which - 1],
            )
            part_at = which - 1
            send(
                view(block, index, part_at * half, half),
                view(block, index, part_at * half, half),
                x_send.at[block, 2 + part_at],
                x_recv.at[block, 2 + part_at],
                (x_right, x_left)[part_at],
            )
            send_y(block, which, lambda first: view(block, index, first, half))
            send_core(block, which, index, view(block, index, 0, depth))
    def relay_far(block):
        far = slot(across, core, same)
        for part_at in (0, 1):
            arrived(
                view(block, far, part_at * half, half),
                x_send.at[block, 2 + part_at],
                x_recv.at[block, 2 + part_at],
            )
        send_y(block, 3, lambda first: view(block, far, first, half))
        send_core(block, 3, far, view(block, far, 0, depth))

    def pass_on(block):
        for which in range(4):
            index = slot(sources[which], core, opposite)
            for part_at in (0, 1):
                arrived(
                    view(block, index, part_at * half, half),
                    y_send.at[block, which, part_at],
                    y_recv.at[block, which, part_at],
                )
            send_core(block, 4 + which, index, view(block, index, 0, depth))

    def gathered(block):
        for at in range(8):
            index = slot(sources[at % 4], 1 - core, same if at < 4 else opposite)
            arrived(
                view(block, index, 0, depth), core_send.at[block, at], core_recv.at[block, at]
            )
        index = slot(place, core, same)
        target = view(block, index, 0, depth)
        pltpu.make_async_copy(own(block, 0, depth), target, own_sem.at[block]).wait()


    quarter_width = gate_weight.shape[2]
    many, core_rows = 4 * depth, 8 * depth

    def gate_view(quarter, first, rows_count):
        return gate_weight.at[quarter, pl.ds(pl.multiple_of(first, 16), rows_count), :]

    def gate_copy(source, at, device):
        send(source, source, gate_send.at[at], gate_recv.at[at], device)

    def gate_arrived(target, at):
        arrived(target, gate_send.at[at], gate_recv.at[at])

    def gate_own():
        first = pl.multiple_of(z * quarter_width, LANES)
        return xz_ref.at[:, pl.ds(first, quarter_width)]

    def gate_start():
        target = gate_view(z, slot(place, core, same) * depth, depth)
        send(gate_own(), target, gate_send.at[0], gate_recv.at[0], x_right)
        send(gate_own(), target, gate_send.at[1], gate_recv.at[1], x_left)
        pltpu.make_async_copy(gate_own(), target, own_sem.at[len(blocks)]).start()

    def gate_x():
        for at, index in ((0, slot(left, core, same)), (1, slot(right, core, same))):
            gate_arrived(gate_view(z, index * depth, depth), at)
            gate_copy(gate_view(z, index * depth + at * half, half), 2 + at, (x_right, x_left)[at])

    def gate_y():
        far = slot(across, core, same) * depth
        for at in (0, 1):
            gate_arrived(gate_view(z, far + at * half, half), 2 + at)
        target = gate_view(z, slot(place, core, same) * depth, depth)
        pltpu.make_async_copy(gate_own(), target, own_sem.at[len(blocks)]).wait()
        first = slot(0, core, same) * depth
        for at, device in ((0, y_up), (1, y_down)):
            gate_copy(gate_view(z, first + at * (many // 2), many // 2), 4 + at, device)

    def gate_z():
        first = slot(0, core, opposite) * depth
        for at in (0, 1):
            gate_arrived(gate_view(z, first + at * (many // 2), many // 2), 4 + at)
        mine = gate_view(z, core * core_rows, core_rows)
        gate_copy(mine, 6, z_up)
        gate_copy(mine, 7, z_down)
        gate_copy(mine, 10, partner)

    def gate_pass():
        for at, quarter in ((0, (z + 3) % 4), (1, (z + 1) % 4)):
            mine = gate_view(quarter, core * core_rows, core_rows)
            gate_arrived(mine, 6 + at)
            part_rows = gate_view(quarter, core * core_rows + at * many, many)
            gate_copy(part_rows, 8 + at, (z_up, z_down)[at])
            gate_copy(mine, 11 + at, partner)

    def gate_end():
        quarter = (z + 2) % 4
        for at in (0, 1):
            gate_arrived(gate_view(quarter, core * core_rows + at * many, many), 8 + at)
        gate_copy(gate_view(quarter, core * core_rows, core_rows), 13, partner)
        for at, quarter in enumerate((z, (z + 3) % 4, (z + 1) % 4, (z + 2) % 4)):
            gate_arrived(gate_view(quarter, (1 - core) * core_rows, core_rows), 10 + at)

    tokens = row_part * col_total
    tile = tokens // 5
    groups = col_total // GROUP // 4
    piece_rows = groups * row_part * GROUP
    outs = {}

    def compute(block):
        start, width = blocks[block]
        lanes = pl.ds(0, width)
        buffer = block

        def one_tile(i, largest):
            at = pl.ds(pl.multiple_of(i * tile, tile), tile)
            result = dot(tokens_ref[at, :], in_order(weight.at[block, :, lanes], depth))
            if block == 0:
                raw = result[:, width - LANES :] + bias_ref[...]
                steps = jnp.maximum(raw, 0.0) + jnp.log1p(jnp.exp(-jnp.abs(raw)))
                result = jnp.concatenate([result[:, : width - LANES], steps], axis=1)
            product[buffer, at, lanes] = result
            return jnp.maximum(largest, jnp.max(jnp.abs(result), axis=0, keepdims=True))

        largest = lax.fori_loop(0, 5, one_tile, jnp.zeros((1, width), F32))
        if block == 0:
            out = keys_ref
        else:
            out = values_ref.at[:, pl.ds(start, width)]
        copy = pltpu.make_async_copy(product.at[buffer, :, lanes], out, out_sem.at[block])
        copy.start()
        outs[block] = copy

        scale, factor = code_scale(largest)

        def code(value):
            coded = encode(value * factor)
            if block == 0:
                exact = value[:, width - LANES :]
                high = exact.astype(BF16)
                rest = exact - high.astype(F32)
                second = rest.astype(BF16)
                third = (rest - second.astype(F32)).astype(BF16)
                lane = lanes_iota(exact.shape)
                heads = STEP_LANES
                parts = jnp.where(
                    lane < heads,
                    high.astype(F32),
                    jnp.where(lane < 2 * heads, second.astype(F32), third.astype(F32)),
                )
                coded = jnp.concatenate([coded[:, : width - LANES], parts.astype(BF16)], axis=1)
            return coded

        for quad in range(row_part // 4):

            def one_group(at, carry):
                both = []
                for pair in (2 * quad, 2 * quad + 1):
                    first = product[buffer, pl.ds(pl.multiple_of(2 * pair * col_total + 8 * at, 8), 8), lanes]
                    second = product[
                        buffer, pl.ds(pl.multiple_of((2 * pair + 1) * col_total + 8 * at, 8), 8), lanes
                    ]
                    both.append(column_groups(first, second))
                for odd in (0, 1):
                    group = 2 * at + odd
                    piece = group // groups
                    row = pl.multiple_of((group % groups) * row_part * GROUP + 16 * quad, 16)
                    value = jnp.concatenate([both[0][odd], both[1][odd]], axis=0)
                    middle[block, piece, pl.ds(row, 16), lanes] = code(value)
                return carry

            lax.fori_loop(0, col_total // 8, one_group, 0)
        for piece in range(4):
            middle[block, piece, pl.ds(piece_rows, 16), lanes] = jnp.broadcast_to(scale, (16, width))
        into = columns_ref.at[place, :, pl.ds(inner if block == 0 else start, width)]
        for at, (where, device) in enumerate(((right, x_right), (left, x_left), (across, x_across))):
            send(
                middle.at[block, where, :, lanes],
                into,
                move_send.at[block, at],
                move_recv.at[block, at],
                device,
            )
        pltpu.make_async_copy(middle.at[block, place, :, lanes], into, move_own.at[block]).start()

    count = len(blocks)
    for block in range(count):
        send_own(block)
    gate_start()
    relay(0)
    relay(1)
    gate_x()
    relay_far(0)
    for block in range(count):
        if block + 2 < count:
            relay(block + 2)
        if block + 1 < count:
            relay_far(block + 1)
        if block < 2:
            (gate_y, gate_z)[block]()
        pass_on(block)
        gathered(block)
        compute(block)

    gate_pass()
    memory_ref[...] = jnp.zeros_like(memory_ref)
    total_ref[...] = jnp.zeros_like(total_ref)

    def fold_rows(step, carry):
        at = pl.ds(pl.multiple_of(step * tile, 16), tile)
        block_pairs = blocks[1][1] // LANES

        def values(pair):
            return product[1 + pair // block_pairs, at, pl.ds(pair % block_pairs * LANES, LANES)]

        fold_chunk(
            values,
            product[0, at, pl.ds(0, LANES)],
            product[0, at, pl.ds(2 * LANES, LANES)],
            rate_ref[...],
            earlier_mask(tile, 0),
            head_size,
            memory_ref,
            total_ref,
        )
        return carry

    lax.fori_loop(0, 5, fold_rows, 0)
    gate_end()
    gate_copies = [
        pltpu.make_async_copy(gate_weight.at[quarter], gate_ref.at[quarter], gate_out.at[quarter])
        for quarter in range(4)
    ]
    for copy in gate_copies:
        copy.start()
    for block in range(count):
        start, width = blocks[block]
        lanes = pl.ds(0, width)
        for at, where in enumerate((left, right, across)):
            into = columns_ref.at[where, :, pl.ds(inner if block == 0 else start, width)]
            arrived(into, move_send.at[block, at], move_recv.at[block, at])
        into = columns_ref.at[place, :, pl.ds(inner if block == 0 else start, width)]
        pltpu.make_async_copy(middle.at[block, place, :, lanes], into, move_own.at[block]).wait()
    for copy in list(outs.values()) + gate_copies:
        copy.wait()
    for copy in pending:
        copy.wait_send()


def project(tokens, state_weight, bias, rate, xz_weight, row_part, col_total, inner, head_size, block_width):
    depth, state_width = state_weight.shape
    count = inner // block_width + 1
    blocks = ((0, state_width),) + tuple((k * block_width, block_width) for k in range(count - 1))
    width = max(block_width, state_width)
    total = tokens.shape[0]
    piece_rows = total // 4 + 16
    vmem, hbm = pl.BlockSpec(memory_space=pltpu.VMEM), pl.BlockSpec(memory_space=pl.ANY)
    dma = pltpu.SemaphoreType.DMA
    return pl.pallas_call(
        functools.partial(project_kernel, (row_part, col_total, inner, depth, blocks, head_size)),
        in_specs=[vmem, vmem, vmem, vmem, hbm],
        out_specs=[hbm, hbm, hbm, vmem, vmem, hbm],
        out_shape=[
            jax.ShapeDtypeStruct((total, inner), F32),
            jax.ShapeDtypeStruct((total, state_width), F32),
            jax.ShapeDtypeStruct((4, piece_rows, inner + state_width), BF16),
            jax.ShapeDtypeStruct((LANES, inner), F32),
            jax.ShapeDtypeStruct((8, LANES), F32),
            jax.ShapeDtypeStruct((4, tokens.shape[1], inner // 4), BF16),
        ],
        scratch_shapes=[
            pltpu.VMEM((count, tokens.shape[1], width), BF16),
            pltpu.VMEM((4, tokens.shape[1], inner // 4), BF16),
            pltpu.VMEM((count, total, width), F32),
            pltpu.VMEM((count, 4, piece_rows, width), BF16),
            dma((count + 1,)),
            dma((count, 4)),
            dma((count, 4)),
            dma((count, 4, 2)),
            dma((count, 4, 2)),
            dma((count, 8)),
            dma((count, 8)),
            dma((count, 3)),
            dma((count, 3)),
            dma((count,)),
            dma((count,)),
            dma((14,)),
            dma((14,)),
            dma((4,)),
        ],
        compiler_params=pltpu.CompilerParams(
            collective_id=0, has_side_effects=True, vmem_limit_bytes=VMEM_BYTES
        ),
    )(tokens, state_weight, bias, rate, xz_weight)


class Chunk:
    def __init__(self, column_rows, values_ref, keys_ref, steps_ref, scale_ref):
        self.size = values_ref.shape[0] * values_ref.shape[1]
        self.inner = values_ref.shape[2]
        self.pairs = self.inner // LANES
        self.column_rows, self.values_ref, self.scale_ref = column_rows, values_ref, scale_ref
        self.keys_ref, self.steps_ref = keys_ref, steps_ref
        if column_rows:
            self.scales = [scale_ref[k, pl.ds(0, 16), :].astype(F32)[0:1] for k in range(4)]

    def read(self, ref, lanes, scale_lane):
        block = ref[:, :, lanes]
        if not self.column_rows:
            return block.reshape(self.size, LANES)
        block = decode(block)
        parts = [
            block[k] * (self.scales[k][:, scale_lane : scale_lane + LANES] * (1.0 / CODE_TOP))
            for k in range(4)
        ]
        return jnp.concatenate(parts, axis=0)

    def values(self, pair):
        return self.read(self.values_ref, pl.ds(pair * LANES, LANES), pair * LANES)

    def keys(self):
        return self.read(self.keys_ref, pl.ds(0, LANES), self.inner)

    def queries(self, ref):
        return self.read(ref, pl.ds(0, LANES), self.inner + LANES)

    def steps(self):
        block = self.steps_ref[...].reshape(self.size, LANES)
        if not self.column_rows:
            return block
        shape = (LANES, LANES)
        part, head = rows_iota(shape), lanes_iota(shape)
        fold = (lax.rem(part, STEP_LANES) == head) & (part < 3 * STEP_LANES)
        return dot(block, jnp.where(fold, 1.0, 0.0).astype(BF16))

    def earlier(self):
        return earlier_mask(self.size, self.column_rows)


def output_chunk(chunk, queries, rate, memory_ref, head_size, emit):
    size = chunk.size
    steps = chunk.steps()
    keys_t = split(jnp.transpose(chunk.keys()))
    queries_high, queries_low = queries
    earlier = chunk.earlier()
    running, total = running_logs(steps, rate, earlier)
    across = jnp.transpose(running)
    scores = dot(queries_high, keys_t[0]) + dot(queries_high, keys_t[1]) + dot(queries_low, keys_t[0])
    scores = jnp.where(earlier, scores, 0.0)
    arrived = jnp.exp(running)
    leaving = jnp.exp(jnp.minimum(total - running, 0.0))
    decay = jnp.exp(total)
    first_half = lanes_iota((size, LANES)) < head_size
    for pair in range(chunk.pairs):
        lanes = pl.ds(pair * LANES, LANES)
        values = chunk.values(pair)
        scaled = values * spread(steps, pair, head_size)
        high, low = split(scaled)
        both = jnp.concatenate([high, low], axis=1)
        halves = []
        for head in (2 * pair, 2 * pair + 1):
            between = jnp.minimum(running[:, head : head + 1] - across[head : head + 1, :], 0.0)
            kernel_high, kernel_low = split(jnp.exp(between) * scores)
            part = dot(kernel_high, both)
            halves.append(part[:, :LANES] + part[:, LANES:] + dot(kernel_low, high))
        memory = memory_ref[:, lanes]
        result = jnp.where(first_half, halves[0], halves[1])
        result = result + carried(queries, memory) * spread(arrived, pair, head_size)
        emit(pair, result, values)
        weighted = scaled * spread(leaving, pair, head_size)
        memory_ref[:, lanes] = advance(memory, keys_t, weighted, spread(decay, pair, head_size))
    return running, total


def carried(queries, memory):
    queries_high, queries_low = queries
    memory_high, memory_low = split(memory)
    part = dot(queries_high, jnp.concatenate([memory_high, memory_low], axis=1))
    return part[:, :LANES] + part[:, LANES:] + dot(queries_low, memory_high)


def output_kernel(
    head_size, values_ref, keys_ref, steps_ref, queries_ref, rate_ref, entering_ref, skip_ref, out_ref, memory_ref
):
    chunk = Chunk(0, values_ref, keys_ref, steps_ref, None)

    @pl.when(pl.program_id(0) == 0)
    def _():
        memory_ref[...] = entering_ref[...]

    def emit(pair, result, values):
        lanes = pl.ds(pair * LANES, LANES)
        result = result + values * skip_ref[:, lanes]
        out_ref[:, :, lanes] = result.reshape(1, chunk.size, LANES)

    output_chunk(chunk, split(chunk.queries(queries_ref)), rate_ref[...], memory_ref, head_size, emit)


def whole(shape):
    return pl.BlockSpec(shape, lambda j: (0,) * len(shape))


def estimate(tokens, inner, passes, transfers):
    return pl.CostEstimate(
        flops=2 * tokens * inner * 192 * passes, bytes_accessed=transfers, transcendentals=0
    )


def row_output(values, keys, rate, entering, skip, inner, size, head_size):
    count = values.shape[1] // size

    def spec(lane_count, lane_block):
        return pl.BlockSpec((1, size, lane_count), lambda j: (0, j, lane_block))

    return pl.pallas_call(
        functools.partial(output_kernel, head_size),
        grid=(count,),
        in_specs=[
            spec(inner, 0),
            spec(LANES, 0),
            spec(LANES, 2),
            spec(LANES, 1),
            whole((1, LANES)),
            whole((LANES, inner)),
            whole((1, inner)),
        ],
        out_specs=spec(inner, 0),
        out_shape=jax.ShapeDtypeStruct(values.shape, F32),
        scratch_shapes=[pltpu.VMEM((LANES, inner), F32)],
        cost_estimate=estimate(count * size, inner, 30, 32 << 20),
        compiler_params=params(),
    )(values, keys, keys, keys, rate, entering, skip)


def states_kernel(
    geometry,
    columns_ref,
    rate_ref,
    forward_ref,
    forward_total_ref,
    entering_forward_ref,
    out_ref,
    entering_backward_ref,
    outputs,
    logs,
    before,
    scales_ref,
    local_memory,
    memory,
    total,
    sent,
    received,
    found,
    out_send,
    out_recv,
    back_send,
    back_recv,
    own_sem,
):
    inner, size, column_rows, head_size, count, spatial = geometry
    slices = count // 2
    rows, wide = LANES // slices, inner // 2
    pairs = wide // LANES
    frame, place, part = lax.axis_index("frame"), lax.axis_index("spatial"), lax.axis_index("dp")
    me = frame * spatial + place

    def device(index):
        return (index // spatial, index % spatial, part)

    barrier = pltpu.get_barrier_semaphore()

    def greet(k, carry):
        peer = device((me + k) % count)
        pl.semaphore_signal(barrier, inc=1, device_id=peer, device_id_type=MESH)
        return carry

    lax.fori_loop(1, count, greet, 0)
    pl.semaphore_wait(barrier, count - 1)

    def send_slices(way, memory_ref, total_ref):
        totals = total_ref[...]
        shifted = pltpu.roll(totals, LANES - 2 * pairs, 1)
        for index in range(count):
            first, lane = rows * (index // 2), wide * (index % 2)
            sent[way, index, :, pl.ds(0, wide)] = memory_ref[pl.ds(first, rows), pl.ds(lane, wide)]
            sent[way, index, :, pl.ds(wide, LANES)] = shifted if index % 2 else totals

        def one(k, carry):
            to = (me + k) % count
            pltpu.make_async_remote_copy(
                src_ref=sent.at[way, to],
                dst_ref=received.at[way, me],
                send_sem=out_send.at[way, k],
                recv_sem=out_recv.at[way, k],
                device_id=device(to),
                device_id_type=MESH,
            ).start()
            return carry

        lax.fori_loop(1, count, one, 0)
        received[way, me] = sent[way, me]

    def scan(way, reverse, entering_ref):
        def arrive(k, carry):
            source = (me + count - k) % count
            pltpu.make_async_remote_copy(
                src_ref=received.at[way, source],
                dst_ref=received.at[way, source],
                send_sem=out_send.at[way, k],
                recv_sem=out_recv.at[way, k],
                device_id=device(source),
                device_id_type=MESH,
            ).wait_recv()
            return carry

        lax.fori_loop(1, count, arrive, 0)
        entering = jnp.zeros((rows, wide), F32)
        for k in range(count):
            at = count - 1 - k if reverse else k
            found[way, at] = entering
            decay = jnp.exp(received[way, at, :, pl.ds(wide, LANES)])
            spreads = [spread(decay, pair, head_size) for pair in range(pairs)]
            decay = jnp.concatenate(spreads, axis=1)
            entering = entering * decay + received[way, at, :, pl.ds(0, wide)]

        def one(k, carry):
            to = (me + k) % count
            pltpu.make_async_remote_copy(
                src_ref=found.at[way, to],
                dst_ref=place_of(entering_ref, me),
                send_sem=back_send.at[way, k],
                recv_sem=back_recv.at[way, k],
                device_id=device(to),
                device_id_type=MESH,
            ).start()
            return carry

        lax.fori_loop(1, count, one, 0)
        copy = pltpu.make_async_copy(found.at[way, me], place_of(entering_ref, me), own_sem.at[way])
        copy.start()

    def place_of(entering_ref, index):
        first = pl.multiple_of(rows * (index // 2), rows)
        lane = pl.multiple_of(wide * (index % 2), LANES)
        return entering_ref.at[pl.ds(first, rows), pl.ds(lane, wide)]

    def finish_way(way, entering_ref):
        def arrive(k, carry):
            source = (me + count - k) % count
            to = (me + k) % count
            pltpu.make_async_remote_copy(
                src_ref=found.at[way, source],
                dst_ref=place_of(entering_ref, source),
                send_sem=back_send.at[way, k],
                recv_sem=back_recv.at[way, k],
                device_id=device(to),
                device_id_type=MESH,
            ).wait()
            pltpu.make_async_remote_copy(
                src_ref=sent.at[way, to],
                dst_ref=received.at[way, me],
                send_sem=out_send.at[way, k],
                recv_sem=out_recv.at[way, k],
                device_id=device(to),
                device_id_type=MESH,
            ).wait_send()
            return carry

        lax.fori_loop(1, count, arrive, 0)
        pltpu.make_async_copy(
            found.at[way, me], place_of(entering_ref, me), own_sem.at[way]
        ).wait()

    send_slices(0, forward_ref, forward_total_ref)
    memory[...] = jnp.zeros_like(memory)
    total[...] = jnp.zeros_like(total)
    chunks = (columns_ref.shape[1] - 16) // (size // 4)
    last = columns_ref.shape[1] - 16

    part_rows = size // 4

    def chunk_at(step):
        at = pl.ds(pl.multiple_of((chunks - 1 - step) * part_rows, 16), part_rows)
        chunk = Chunk(
            column_rows,
            columns_ref.at[:, at, pl.ds(0, inner)],
            columns_ref.at[:, at, pl.ds(inner, LANES)],
            columns_ref.at[:, at, pl.ds(inner + 2 * LANES, LANES)],
            columns_ref.at[:, pl.ds(last, 16), :],
        )
        return chunk, split(chunk.queries(columns_ref.at[:, at, pl.ds(inner + LANES, LANES)]))

    def fold_columns(step, carry):
        chunk, _ = chunk_at(step)
        fold_chunk(
            chunk.values,
            chunk.keys(),
            chunk.steps(),
            rate_ref[...],
            chunk.earlier(),
            head_size,
            memory,
            total,
        )
        return carry

    def output_columns(step, carry):
        chunk, queries = chunk_at(step)

        def emit(pair, result, values):
            outputs[step, :, pl.ds(pair * LANES, LANES)] = result

        running, chunk_total = output_chunk(
            chunk, queries, rate_ref[...], local_memory, head_size, emit
        )
        logs[step] = before[0:1] + running
        before[...] = before[...] + chunk_total

        @pl.when(step == 1)
        def _():
            scan(0, False, entering_forward_ref)

        @pl.when(step == 2)
        def _():
            scan(1, True, entering_backward_ref)

        return carry

    def correct(step, carry):
        _, queries = chunk_at(step)
        arrived = jnp.exp(logs[step])
        first = pl.multiple_of((chunks - 1 - step) * part_rows, 16)
        here = rows_iota((16, LANES)) == chunks - 1 - step
        for pair in range(inner // LANES):
            lanes = pl.ds(pair * LANES, LANES)
            added = carried(queries, memory[:, lanes]) * spread(arrived, pair, head_size)
            result = outputs[step, :, lanes] + added
            scale, factor = code_scale(jnp.max(jnp.abs(result), axis=0, keepdims=True))
            out_ref[:, pl.ds(first, part_rows), lanes] = encode(result * factor).reshape(
                4, part_rows, LANES
            )
            scales_ref[:, lanes] = jnp.where(here, scale.astype(F32), scales_ref[:, lanes])
        return carry

    lax.fori_loop(0, chunks, fold_columns, 0)
    send_slices(1, memory, total)
    local_memory[...] = jnp.zeros_like(local_memory)
    before[...] = jnp.zeros_like(before)
    scales_ref[...] = jnp.zeros_like(scales_ref)
    lax.fori_loop(0, chunks, output_columns, 0)
    finish_way(1, entering_backward_ref)
    memory[...] = entering_backward_ref[...]
    lax.fori_loop(0, chunks, correct, 0)
    for k in range(4):
        out_ref[k, pl.ds(last, 16), :] = scales_ref[...].astype(BF16)
    finish_way(0, entering_forward_ref)


def column_output(columns, rate, memory, total, inner, size, column_rows, head_size):
    spatial = lax.axis_size("spatial")
    count = lax.axis_size("frame") * spatial
    rows, wide = LANES * 2 // count, inner // 2
    chunks = (columns.shape[1] - 16) * 4 // size
    vmem, hbm = pl.BlockSpec(memory_space=pltpu.VMEM), pl.BlockSpec(memory_space=pl.ANY)
    dma = pltpu.SemaphoreType.DMA
    geometry = (inner, size, column_rows, head_size, count, spatial)
    return pl.pallas_call(
        functools.partial(states_kernel, geometry),
        in_specs=[vmem] * 4,
        out_specs=[hbm, vmem],
        out_shape=[
            jax.ShapeDtypeStruct((LANES, inner), F32),
            jax.ShapeDtypeStruct(columns.shape[:2] + (inner,), BF16),
        ],
        scratch_shapes=[
            pltpu.VMEM((LANES, inner), F32),
            pltpu.VMEM((chunks, size, inner), F32),
            pltpu.VMEM((chunks, size, LANES), F32),
            pltpu.VMEM((8, LANES), F32),
            pltpu.VMEM((16, inner), F32),
            pltpu.VMEM((LANES, inner), F32),
            pltpu.VMEM((LANES, inner), F32),
            pltpu.VMEM((8, LANES), F32),
            pltpu.VMEM((2, count, rows, wide + LANES), F32),
            pltpu.VMEM((2, count, rows, wide + LANES), F32),
            pltpu.VMEM((2, count, rows, wide), F32),
            dma((2, count)),
            dma((2, count)),
            dma((2, count)),
            dma((2, count)),
            dma((2,)),
        ],
        compiler_params=pltpu.CompilerParams(
            collective_id=1, has_side_effects=True, vmem_limit_bytes=VMEM_BYTES
        ),
    )(columns, rate, memory, total)


def finish_kernel(head_size, groups, part, forward_ref, backward_ref, gate_ref, gain_ref, out_ref, moved_ref):
    col_total = forward_ref.shape[0] // 4
    quad = pl.program_id(0)
    last = backward_ref.shape[1] - 16
    scales = [backward_ref[k, pl.ds(last, 16), :].astype(F32) * (1.0 / CODE_TOP) for k in range(4)]

    def group_rows(group):
        piece, within = group // groups, group % groups
        first = pl.multiple_of(within * part + 16 * quad, 16)
        coded = backward_ref[piece, pl.ds(first, 16), :]
        return decode(coded) * scales[piece][within : within + 1, :]

    for at in range(col_total // 8):
        even, odd = group_rows(2 * at), group_rows(2 * at + 1)
        for k in (0, 1):
            low_half, high_half = even[8 * k : 8 * k + 8], odd[8 * k : 8 * k + 8]
            first, second = column_groups(low_half, high_half)
            moved_ref[pl.ds(2 * k * col_total + 8 * at, 8), :] = first
            moved_ref[pl.ds((2 * k + 1) * col_total + 8 * at, 8), :] = second
    wide = 2 * LANES
    same = rows_iota((wide, wide)) // head_size == lanes_iota((wide, wide)) // head_size
    ones = jnp.where(same, 1.0, 0.0).astype(BF16)
    for block in range(forward_ref.shape[1] // wide):
        lanes = pl.ds(block * wide, wide)
        gate = gate_ref[:, lanes]
        combined = forward_ref[:, lanes] + moved_ref[:, lanes]
        gated = combined * (gate / (1.0 + jnp.exp(-gate)))
        high, low = split(gated * gated)
        mean = (dot(high, ones) + dot(low, ones)) * (1.0 / head_size)
        normed = gated * lax.rsqrt(mean + 1e-5) * gain_ref[:, lanes]
        out_ref[:, lanes] = normed.astype(out_ref.dtype)


def finish(forward, backward, gate, gain, row_part, col_total, head_size):
    tokens, inner = forward.shape
    groups = col_total // GROUP // 4
    block = 4 * col_total
    flat = pl.BlockSpec((block, inner), lambda m: (m, 0))
    return pl.pallas_call(
        functools.partial(finish_kernel, head_size, groups, row_part * GROUP),
        grid=(row_part // 4,),
        in_specs=[flat, whole(backward.shape), flat, whole((1, inner))],
        out_specs=flat,
        out_shape=jax.ShapeDtypeStruct((tokens, inner), BF16),
        scratch_shapes=[pltpu.VMEM((block, inner), F32)],
        compiler_params=params(),
    )(forward, backward, gate, gain)


def pad_lanes(source):
    return jnp.pad(source, ((0, 0), (0, LANES - source.shape[1])))


def local(tokens, xz_weight, state_weight, step_weight, step_bias, decay_rate, skip, norm_gain):
    videos, frame_count, row_part, col_total, width = tokens.shape
    flattened = tokens.reshape(-1, width)
    inner = xz_weight.shape[1] // 2
    heads = step_weight.shape[1]
    head_size = inner // heads
    column_rows = row_part * lax.axis_size("spatial")
    size = column_rows * GROUP
    axes = ("frame", "spatial")

    thrice = pad_lanes(jnp.concatenate([step_weight] * 3, axis=1))
    bias = pad_lanes(jnp.concatenate([step_bias] * 3)[None])
    first_weight = jnp.concatenate([state_weight, thrice], axis=1)
    rates = pad_lanes(decay_rate)
    skips = jnp.repeat(skip[0] + skip[1], head_size)[None]

    values, keys, columns, memory, total, gate_weight = project(
        flattened,
        first_weight,
        bias,
        rates[0:1],
        xz_weight,
        row_part,
        col_total,
        inner,
        head_size,
        512,
    )
    entering, backward = column_output(
        columns, rates[1:2], memory, total, inner, size, column_rows, head_size
    )
    returned = lax.all_to_all(backward, "spatial", 0, 0, tiled=True)
    forward = row_output(
        values[None], keys[None], rates[0:1], entering, skips, inner, size, head_size
    )
    gate_weight, forward = lax.optimization_barrier((gate_weight, forward))
    gate_rows = gate_rows_of(flattened, gate_weight, xz_weight.shape[0])
    normed = finish(
        forward[0], returned, gate_rows, norm_gain[None], row_part, col_total, head_size
    )
    return normed.reshape(videos, frame_count, row_part, col_total, inner)


def solution(mesh):
    in_specs = (
        P("dp", "frame", "spatial", None, None),
        P(("spatial", "dp"), None),
        P(("spatial", "dp"), None),
        P(("spatial", "dp"), None),
        P(),
        P(),
        P(),
        P(),
    )
    out_specs = P("dp", "frame", "spatial", None, None)
    return jax.shard_map(local, mesh=mesh, in_specs=in_specs, out_specs=out_specs, check_vma=False)
```

```python
import functools

import jax
import jax.numpy as jnp
from jax import lax
from jax.experimental import pallas as pl
from jax.experimental.pallas import tpu as pltpu
from jax.sharding import PartitionSpec as P

F32 = jnp.float32
BF16 = jnp.bfloat16
LANES = 128
GROUP = 4
POWER = 17
LOG2_E = 1.4426950408889634
CODE_TOP = 128.0
STEP_LANES = 24
MESH = pl.DeviceIdType.MESH
VMEM_BYTES = 56 * 1024 * 1024


def split(value):
    high = value.astype(BF16)
    return high, (value - high.astype(F32)).astype(BF16)


def dot(a, b):
    return lax.dot_general(a, b, (((1,), (0,)), ((), ())), preferred_element_type=F32)


def rows_iota(shape):
    return lax.broadcasted_iota(jnp.int32, shape, 0)


def lanes_iota(shape):
    return lax.broadcasted_iota(jnp.int32, shape, 1)


def spread(columns, pair, head_size):
    first, second = columns[:, 2 * pair : 2 * pair + 1], columns[:, 2 * pair + 1 : 2 * pair + 2]
    shape = (columns.shape[0], LANES)
    return jnp.where(lanes_iota(shape) < head_size, first, second)


def params(semantics=("arbitrary",)):
    return pltpu.CompilerParams(vmem_limit_bytes=VMEM_BYTES, dimension_semantics=semantics)


def encode(scaled):
    square = scaled * scaled
    fourth = square * square
    eighth = fourth * fourth
    return (eighth * eighth * scaled).astype(BF16)


def decode(coded):
    coded = coded.astype(F32)
    size = jnp.exp2(jnp.log2(jnp.abs(coded)) * (1.0 / POWER))
    return jnp.where(coded < 0.0, -size, size)


def code_scale(largest):
    scale = jnp.maximum(largest, 1e-30).astype(BF16)
    return scale, CODE_TOP / scale.astype(F32)


def column_groups(first, second):
    low = rows_iota(first.shape) < GROUP
    even = jnp.where(low, first, pltpu.roll(second, GROUP, 0))
    odd = jnp.where(low, pltpu.roll(first, GROUP, 0), second)
    return even, odd


def earlier_mask(size, column_rows):
    shape = (size, size)
    t, s = rows_iota(shape), lanes_iota(shape)
    if column_rows:

        def place(index):
            return size - 1 - (lax.rem(index, GROUP) * column_rows + index // GROUP)

        t, s = place(t), place(s)
    return s <= t


def running_logs(steps, rate, earlier):
    logs = -steps * rate
    high, rest = split(logs)
    middle = logs - high.astype(F32)
    middle, low = split(middle)
    before = jnp.where(earlier, 1.0, 0.0).astype(BF16)
    running = dot(before, high) + dot(before, middle) + dot(before, low)
    return running, jnp.sum(logs, axis=0, keepdims=True)


def advance(memory, keys_t, weighted, decay):
    keys_high, keys_low = keys_t
    high, low = split(weighted)
    both = dot(keys_high, jnp.concatenate([high, low], axis=1))
    added = both[:, :LANES] + both[:, LANES:] + dot(keys_low, high)
    return memory * decay + added


def fold_chunk(values, keys, steps, rate, earlier, head_size, memory_ref, total_ref):
    keys_t = split(jnp.transpose(keys))
    running, total = running_logs(steps, rate, earlier)
    coefficient = steps * jnp.exp(jnp.minimum(total - running, 0.0))
    decay = jnp.exp(total)
    for pair in range(memory_ref.shape[1] // LANES):
        lanes = pl.ds(pair * LANES, LANES)
        weighted = values(pair) * spread(coefficient, pair, head_size)
        memory_ref[:, lanes] = advance(
            memory_ref[:, lanes], keys_t, weighted, spread(decay, pair, head_size)
        )
    total_ref[...] = total_ref[...] + total


def in_order(ref, depth):
    parts = []
    for row in range(16):
        where, part, core = row // 4, (row // 2) % 2, row % 2
        parts.append(ref[pl.ds((core * 8 + part * 4 + where) * depth, depth), :])
    return jnp.concatenate(parts, axis=0)


def gate_kernel(depth, tokens_ref, weight_ref, gate_ref):
    width = weight_ref.shape[2]
    for quarter in range(0, 4, 2):
        weight = jnp.concatenate(
            [in_order(weight_ref.at[quarter + k], depth) for k in range(2)], axis=1
        )
        gate_ref[:, pl.ds(quarter * width, 2 * width)] = dot(tokens_ref[...], weight)


def gate_rows_of(tokens, weight, depth):
    total, model = tokens.shape
    inner = 4 * weight.shape[2]
    tile = total // 5
    return pl.pallas_call(
        functools.partial(gate_kernel, depth),
        grid=(5,),
        in_specs=[pl.BlockSpec((tile, model), lambda m: (m, 0)), whole(weight.shape)],
        out_specs=pl.BlockSpec((tile, inner), lambda m: (m, 0)),
        out_shape=jax.ShapeDtypeStruct((total, inner), F32),
        cost_estimate=pl.CostEstimate(
            flops=2 * total * model * inner, bytes_accessed=20 << 20, transcendentals=0
        ),
        compiler_params=params(),
    )(tokens, weight)


def project_kernel(
    geometry,
    tokens_ref,
    state_ref,
    bias_ref,
    rate_ref,
    xz_ref,
    values_ref,
    keys_ref,
    columns_ref,
    memory_ref,
    total_ref,
    gate_ref,
    weight,
    gate_weight,
    product,
    middle,
    tokens,
    own_sem,
    x_send,
    x_recv,
    y_send,
    y_recv,
    core_send,
    core_recv,
    move_send,
    move_recv,
    move_own,
    out_sem,
    gate_send,
    gate_recv,
    gate_out,
):
    row_part, col_total, inner, depth, blocks, head_size = geometry
    half = depth // 2
    frame, place, part = lax.axis_index("frame"), lax.axis_index("spatial"), lax.axis_index("dp")
    core, y = part % 2, (frame % 2) * 2 + part // 2
    right, left, across = (place + 1) % 4, (place + 3) % 4, (place + 2) % 4

    z = frame // 2

    def z_device(other):
        return (other * 2 + frame % 2, place, part)

    def y_device(other):
        return ((frame // 2) * 2 + other // 2, place, (other % 2) * 2 + core)

    x_right, x_left, x_across = (frame, right, part), (frame, left, part), (frame, across, part)
    y_up, y_down = y_device((y + 1) % 4), y_device((y + 3) % 4)
    partner = (frame, place, (part // 2) * 2 + 1 - core)

    barrier = pltpu.get_barrier_semaphore()
    z_up, z_down = z_device((z + 1) % 4), z_device((z + 3) % 4)
    peers = (x_right, x_left, x_across, y_up, y_down, z_up, z_down, partner)
    for peer in peers:
        pl.semaphore_signal(barrier, inc=1, device_id=peer, device_id_type=MESH)
    pl.semaphore_wait(barrier, len(peers))

    def slot(where, other_core, other_part):
        return other_core * 8 + other_part * 4 + where

    same, opposite = part // 2, 1 - part // 2
    sources = (place, left, right, across)

    def rows(index, first, count):
        return pl.ds(pl.multiple_of(index * depth + first, 16), count)

    def view(block, index, first, count):
        return weight.at[block, rows(index, first, count), pl.ds(0, blocks[block][1])]

    def own(block, first, count):
        start, width = blocks[block]
        if block == 0:
            return state_ref.at[pl.ds(first, count), :]
        return xz_ref.at[pl.ds(first, count), pl.ds(inner + start, width)]

    pending = []

    def send(source, target, send_sem, recv_sem, device):
        copy = pltpu.make_async_remote_copy(
            src_ref=source,
            dst_ref=target,
            send_sem=send_sem,
            recv_sem=recv_sem,
            device_id=device,
            device_id_type=MESH,
        )
        copy.start()
        pending.append(copy)

    def arrived(target, send_sem, recv_sem):
        pltpu.make_async_remote_copy(
            src_ref=target,
            dst_ref=target,
            send_sem=send_sem,
            recv_sem=recv_sem,
            device_id=x_right,
            device_id_type=MESH,
        ).wait_recv()

    def send_y(block, which, source_of):
        index = slot(sources[which], core, same)
        for part_at, device in ((0, y_up), (1, y_down)):
            first = part_at * half
            send(
                source_of(first),
                view(block, index, first, half),
                y_send.at[block, which, part_at],
                y_recv.at[block, which, part_at],
                device,
            )

    def send_core(block, at, index, source):
        send(
            source,
            view(block, index, 0, depth),
            core_send.at[block, at],
            core_recv.at[block, at],
            partner,
        )

    def send_own(block):
        index = slot(place, core, same)
        target = view(block, index, 0, depth)
        source = own(block, 0, depth)
        send(source, target, x_send.at[block, 0], x_recv.at[block, 0], x_right)
        send(source, target, x_send.at[block, 1], x_recv.at[block, 1], x_left)
        send_y(block, 0, lambda first: own(block, first, half))
        send_core(block, 0, index, source)
        copy = pltpu.make_async_copy(source, target, own_sem.at[block])
        copy.start()

    def relay(block):
        from_left, from_right = slot(left, core, same), slot(right, core, same)
        for which, index in ((1, from_left), (2, from_right)):
            arrived(
                view(block, index, 0, depth),
                x_send.at[block, which - 1],
                x_recv.at[block, which - 1],
            )
            part_at = which - 1
            send(
                view(block, index, part_at * half, half),
                view(block, index, part_at * half, half),
                x_send.at[block, 2 + part_at],
                x_recv.at[block, 2 + part_at],
                (x_right, x_left)[part_at],
            )
            send_y(block, which, lambda first: view(block, index, first, half))
            send_core(block, which, index, view(block, index, 0, depth))
    def relay_far(block):
        far = slot(across, core, same)
        for part_at in (0, 1):
            arrived(
                view(block, far, part_at * half, half),
                x_send.at[block, 2 + part_at],
                x_recv.at[block, 2 + part_at],
            )
        send_y(block, 3, lambda first: view(block, far, first, half))
        send_core(block, 3, far, view(block, far, 0, depth))

    def pass_on(block):
        for which in range(4):
            index = slot(sources[which], core, opposite)
            for part_at in (0, 1):
                arrived(
                    view(block, index, part_at * half, half),
                    y_send.at[block, which, part_at],
                    y_recv.at[block, which, part_at],
                )
            send_core(block, 4 + which, index, view(block, index, 0, depth))

    def gathered(block):
        for at in range(8):
            index = slot(sources[at % 4], 1 - core, same if at < 4 else opposite)
            arrived(
                view(block, index, 0, depth), core_send.at[block, at], core_recv.at[block, at]
            )
        index = slot(place, core, same)
        target = view(block, index, 0, depth)
        pltpu.make_async_copy(own(block, 0, depth), target, own_sem.at[block]).wait()


    quarter_width = gate_weight.shape[2]
    many, core_rows = 4 * depth, 8 * depth

    def gate_view(quarter, first, rows_count):
        return gate_weight.at[quarter, pl.ds(pl.multiple_of(first, 16), rows_count), :]

    def gate_copy(source, at, device):
        send(source, source, gate_send.at[at], gate_recv.at[at], device)

    def gate_arrived(target, at):
        arrived(target, gate_send.at[at], gate_recv.at[at])

    def gate_own():
        first = pl.multiple_of(z * quarter_width, LANES)
        return xz_ref.at[:, pl.ds(first, quarter_width)]

    def gate_start():
        target = gate_view(z, slot(place, core, same) * depth, depth)
        send(gate_own(), target, gate_send.at[0], gate_recv.at[0], x_right)
        send(gate_own(), target, gate_send.at[1], gate_recv.at[1], x_left)
        pltpu.make_async_copy(gate_own(), target, own_sem.at[len(blocks)]).start()

    def gate_x():
        for at, index in ((0, slot(left, core, same)), (1, slot(right, core, same))):
            gate_arrived(gate_view(z, index * depth, depth), at)
            gate_copy(gate_view(z, index * depth + at * half, half), 2 + at, (x_right, x_left)[at])

    def gate_y():
        far = slot(across, core, same) * depth
        for at in (0, 1):
            gate_arrived(gate_view(z, far + at * half, half), 2 + at)
        target = gate_view(z, slot(place, core, same) * depth, depth)
        pltpu.make_async_copy(gate_own(), target, own_sem.at[len(blocks)]).wait()
        first = slot(0, core, same) * depth
        for at, device in ((0, y_up), (1, y_down)):
            gate_copy(gate_view(z, first + at * (many // 2), many // 2), 4 + at, device)

    def gate_z():
        first = slot(0, core, opposite) * depth
        for at in (0, 1):
            gate_arrived(gate_view(z, first + at * (many // 2), many // 2), 4 + at)
        mine = gate_view(z, core * core_rows, core_rows)
        gate_copy(mine, 6, z_up)
        gate_copy(mine, 7, z_down)
        gate_copy(mine, 10, partner)

    def gate_pass():
        for at, quarter in ((0, (z + 3) % 4), (1, (z + 1) % 4)):
            mine = gate_view(quarter, core * core_rows, core_rows)
            gate_arrived(mine, 6 + at)
            part_rows = gate_view(quarter, core * core_rows + at * many, many)
            gate_copy(part_rows, 8 + at, (z_up, z_down)[at])
            gate_copy(mine, 11 + at, partner)

    def gate_end():
        quarter = (z + 2) % 4
        for at in (0, 1):
            gate_arrived(gate_view(quarter, core * core_rows + at * many, many), 8 + at)
        gate_copy(gate_view(quarter, core * core_rows, core_rows), 13, partner)
        for at, quarter in enumerate((z, (z + 3) % 4, (z + 1) % 4, (z + 2) % 4)):
            gate_arrived(gate_view(quarter, (1 - core) * core_rows, core_rows), 10 + at)

    tile = row_part * col_total // 5
    groups = col_total // GROUP // 4
    piece_rows = groups * row_part * GROUP
    outs = {}

    def compute(block):
        start, width = blocks[block]
        lanes = pl.ds(0, width)
        buffer = block

        def one_tile(i, largest):
            at = pl.ds(pl.multiple_of(i * tile, tile), tile)
            result = dot(tokens[at, :], in_order(weight.at[block, :, lanes], depth))
            if block == 0:
                raw = result[:, width - LANES :] + bias_ref[...]
                steps = jnp.maximum(raw, 0.0) + jnp.log1p(jnp.exp(-jnp.abs(raw)))
                result = jnp.concatenate([result[:, : width - LANES], steps], axis=1)
            product[buffer, at, lanes] = result
            return jnp.maximum(largest, jnp.max(jnp.abs(result), axis=0, keepdims=True))

        largest = lax.fori_loop(0, 5, one_tile, jnp.zeros((1, width), F32))
        if block == 0:
            out = keys_ref
        else:
            out = values_ref.at[:, pl.ds(start, width)]
        copy = pltpu.make_async_copy(product.at[buffer, :, lanes], out, out_sem.at[block])
        copy.start()
        outs[block] = copy

        scale, factor = code_scale(largest)

        def code(value):
            coded = encode(value * factor)
            if block == 0:
                exact = value[:, width - LANES :]
                high = exact.astype(BF16)
                rest = exact - high.astype(F32)
                second = rest.astype(BF16)
                third = (rest - second.astype(F32)).astype(BF16)
                lane = lanes_iota(exact.shape)
                heads = STEP_LANES
                parts = jnp.where(
                    lane < heads,
                    high.astype(F32),
                    jnp.where(lane < 2 * heads, second.astype(F32), third.astype(F32)),
                )
                coded = jnp.concatenate([coded[:, : width - LANES], parts.astype(BF16)], axis=1)
            return coded

        for quad in range(row_part // 4):

            def one_group(at, carry):
                both = []
                for pair in (2 * quad, 2 * quad + 1):
                    first = product[buffer, pl.ds(pl.multiple_of(2 * pair * col_total + 8 * at, 8), 8), lanes]
                    second = product[
                        buffer, pl.ds(pl.multiple_of((2 * pair + 1) * col_total + 8 * at, 8), 8), lanes
                    ]
                    both.append(column_groups(first, second))
                for odd in (0, 1):
                    group = 2 * at + odd
                    piece = group // groups
                    row = pl.multiple_of((group % groups) * row_part * GROUP + 16 * quad, 16)
                    value = jnp.concatenate([both[0][odd], both[1][odd]], axis=0)
                    middle[block, piece, pl.ds(row, 16), lanes] = code(value)
                return carry

            lax.fori_loop(0, col_total // 8, one_group, 0)
        for piece in range(4):
            middle[block, piece, pl.ds(piece_rows, 16), lanes] = jnp.broadcast_to(scale, (16, width))
        into = columns_ref.at[place, :, pl.ds(inner if block == 0 else start, width)]
        for at, (where, device) in enumerate(((right, x_right), (left, x_left), (across, x_across))):
            send(
                middle.at[block, where, :, lanes],
                into,
                move_send.at[block, at],
                move_recv.at[block, at],
                device,
            )
        pltpu.make_async_copy(middle.at[block, place, :, lanes], into, move_own.at[block]).start()

    count = len(blocks)
    for block in range(count):
        send_own(block)
    gate_start()
    tokens_copy = pltpu.make_async_copy(tokens_ref, tokens, own_sem.at[count + 1])
    tokens_copy.start()
    relay(0)
    relay(1)
    gate_x()
    relay_far(0)
    for block in range(count):
        if block + 2 < count:
            relay(block + 2)
        if block + 1 < count:
            relay_far(block + 1)
        if block < 2:
            (gate_y, gate_z)[block]()
        pass_on(block)
        gathered(block)
        if block == 0:
            tokens_copy.wait()
        compute(block)

    gate_pass()

    memory_ref[...] = jnp.zeros_like(memory_ref)
    total_ref[...] = jnp.zeros_like(total_ref)

    def fold_rows(step, carry):
        at = pl.ds(pl.multiple_of(step * tile, 16), tile)
        block_pairs = blocks[1][1] // LANES

        def values(pair):
            return product[1 + pair // block_pairs, at, pl.ds(pair % block_pairs * LANES, LANES)]

        fold_chunk(
            values,
            product[0, at, pl.ds(0, LANES)],
            product[0, at, pl.ds(2 * LANES, LANES)],
            rate_ref[...],
            earlier_mask(tile, 0),
            head_size,
            memory_ref,
            total_ref,
        )
        return carry

    lax.fori_loop(0, 5, fold_rows, 0)
    gate_end()
    gate_copies = [
        pltpu.make_async_copy(gate_weight.at[quarter], gate_ref.at[quarter], gate_out.at[quarter])
        for quarter in range(4)
    ]
    for copy in gate_copies:
        copy.start()
    for block in range(count):
        start, width = blocks[block]
        lanes = pl.ds(0, width)
        for at, where in enumerate((left, right, across)):
            into = columns_ref.at[where, :, pl.ds(inner if block == 0 else start, width)]
            arrived(into, move_send.at[block, at], move_recv.at[block, at])
        into = columns_ref.at[place, :, pl.ds(inner if block == 0 else start, width)]
        pltpu.make_async_copy(middle.at[block, place, :, lanes], into, move_own.at[block]).wait()
    for copy in list(outs.values()) + gate_copies:
        copy.wait()
    for copy in pending:
        copy.wait_send()


def project(tokens, state_weight, bias, rate, xz_weight, row_part, col_total, inner, head_size, block_width):
    depth, state_width = state_weight.shape
    count = inner // block_width + 1
    blocks = ((0, state_width),) + tuple((k * block_width, block_width) for k in range(count - 1))
    width = max(block_width, state_width)
    total = tokens.shape[0]
    piece_rows = total // 4 + 16
    vmem, hbm = pl.BlockSpec(memory_space=pltpu.VMEM), pl.BlockSpec(memory_space=pl.ANY)
    dma = pltpu.SemaphoreType.DMA
    return pl.pallas_call(
        functools.partial(project_kernel, (row_part, col_total, inner, depth, blocks, head_size)),
        in_specs=[hbm, vmem, vmem, vmem, hbm],
        out_specs=[hbm, hbm, hbm, vmem, vmem, hbm],
        out_shape=[
            jax.ShapeDtypeStruct((total, inner), F32),
            jax.ShapeDtypeStruct((total, state_width), F32),
            jax.ShapeDtypeStruct((4, piece_rows, inner + state_width), BF16),
            jax.ShapeDtypeStruct((LANES, inner), F32),
            jax.ShapeDtypeStruct((8, LANES), F32),
            jax.ShapeDtypeStruct((4, tokens.shape[1], inner // 4), BF16),
        ],
        scratch_shapes=[
            pltpu.VMEM((count, tokens.shape[1], width), BF16),
            pltpu.VMEM((4, tokens.shape[1], inner // 4), BF16),
            pltpu.VMEM((count, total, width), F32),
            pltpu.VMEM((count, 4, piece_rows, width), BF16),
            pltpu.VMEM(tokens.shape, BF16),
            dma((count + 2,)),
            dma((count, 4)),
            dma((count, 4)),
            dma((count, 4, 2)),
            dma((count, 4, 2)),
            dma((count, 8)),
            dma((count, 8)),
            dma((count, 3)),
            dma((count, 3)),
            dma((count,)),
            dma((count,)),
            dma((14,)),
            dma((14,)),
            dma((4,)),
        ],
        compiler_params=pltpu.CompilerParams(
            collective_id=0, has_side_effects=True, vmem_limit_bytes=VMEM_BYTES
        ),
    )(tokens, state_weight, bias, rate, xz_weight)


class Chunk:
    def __init__(self, column_rows, values_ref, keys_ref, steps_ref, scale_ref):
        self.size = values_ref.shape[0] * values_ref.shape[1]
        self.inner = values_ref.shape[2]
        self.pairs = self.inner // LANES
        self.column_rows, self.values_ref, self.scale_ref = column_rows, values_ref, scale_ref
        self.keys_ref, self.steps_ref = keys_ref, steps_ref
        if column_rows:
            self.scales = [scale_ref[k, pl.ds(0, 16), :].astype(F32)[0:1] for k in range(4)]

    def read(self, ref, lanes, scale_lane):
        block = ref[:, :, lanes]
        if not self.column_rows:
            return block.reshape(self.size, LANES)
        block = decode(block)
        parts = [
            block[k] * (self.scales[k][:, scale_lane : scale_lane + LANES] * (1.0 / CODE_TOP))
            for k in range(4)
        ]
        return jnp.concatenate(parts, axis=0)

    def values(self, pair):
        return self.read(self.values_ref, pl.ds(pair * LANES, LANES), pair * LANES)

    def keys(self):
        return self.read(self.keys_ref, pl.ds(0, LANES), self.inner)

    def queries(self, ref):
        return self.read(ref, pl.ds(0, LANES), self.inner + LANES)

    def steps(self):
        block = self.steps_ref[...].reshape(self.size, LANES)
        if not self.column_rows:
            return block
        shape = (LANES, LANES)
        part, head = rows_iota(shape), lanes_iota(shape)
        fold = (lax.rem(part, STEP_LANES) == head) & (part < 3 * STEP_LANES)
        return dot(block, jnp.where(fold, 1.0, 0.0).astype(BF16))

    def earlier(self):
        return earlier_mask(self.size, self.column_rows)


def output_chunk(chunk, values_of, queries, rate, memory_ref, head_size, emit):
    size = chunk.size
    steps = chunk.steps()
    keys_t = split(jnp.transpose(chunk.keys()))
    queries_high, queries_low = queries
    earlier = chunk.earlier()
    running, total = running_logs(steps, rate, earlier)
    running_bits = running * LOG2_E
    across = jnp.transpose(running_bits)
    scores = dot(queries_high, keys_t[0]) + dot(queries_high, keys_t[1]) + dot(queries_low, keys_t[0])
    scores = jnp.where(earlier, scores, 0.0)
    arrived = jnp.exp(running)
    leaving = jnp.exp(jnp.minimum(total - running, 0.0))
    decay = jnp.exp(total)
    first_half = lanes_iota((size, LANES)) < head_size
    for pair in range(chunk.pairs):
        lanes = pl.ds(pair * LANES, LANES)
        values = values_of(pair)
        scaled = values * spread(steps, pair, head_size)
        high, low = split(scaled)
        both = jnp.concatenate([high, low], axis=1)
        halves = []
        for head in (2 * pair, 2 * pair + 1):
            between = running_bits[:, head : head + 1] - across[head : head + 1, :]
            kernel_high, kernel_low = split(jnp.exp2(jnp.minimum(between, 0.0)) * scores)
            part = dot(kernel_high, both)
            halves.append(part[:, :LANES] + part[:, LANES:] + dot(kernel_low, high))
        memory = memory_ref[:, lanes]
        result = jnp.where(first_half, halves[0], halves[1])
        result = result + carried(queries, memory) * spread(arrived, pair, head_size)
        emit(pair, result, values)
        weighted = scaled * spread(leaving, pair, head_size)
        memory_ref[:, lanes] = advance(memory, keys_t, weighted, spread(decay, pair, head_size))
    return running, total


def carried(queries, memory):
    queries_high, queries_low = queries
    memory_high, memory_low = split(memory)
    part = dot(queries_high, jnp.concatenate([memory_high, memory_low], axis=1))
    return part[:, :LANES] + part[:, LANES:] + dot(queries_low, memory_high)


def output_kernel(
    head_size, values_ref, keys_ref, steps_ref, queries_ref, rate_ref, entering_ref, skip_ref, out_ref, memory_ref
):
    chunk = Chunk(0, values_ref, keys_ref, steps_ref, None)

    @pl.when(pl.program_id(0) == 0)
    def _():
        memory_ref[...] = entering_ref[...]

    def emit(pair, result, values):
        lanes = pl.ds(pair * LANES, LANES)
        result = result + values * skip_ref[:, lanes]
        out_ref[:, :, lanes] = result.reshape(1, chunk.size, LANES)

    queries = split(chunk.queries(queries_ref))
    output_chunk(chunk, chunk.values, queries, rate_ref[...], memory_ref, head_size, emit)


def whole(shape):
    return pl.BlockSpec(shape, lambda j: (0,) * len(shape))


def estimate(tokens, inner, passes, transfers):
    return pl.CostEstimate(
        flops=2 * tokens * inner * 192 * passes, bytes_accessed=transfers, transcendentals=0
    )


def row_output(values, keys, rate, entering, skip, inner, size, head_size):
    count = values.shape[1] // size

    def spec(lane_count, lane_block):
        return pl.BlockSpec((1, size, lane_count), lambda j: (0, j, lane_block))

    return pl.pallas_call(
        functools.partial(output_kernel, head_size),
        grid=(count,),
        in_specs=[
            spec(inner, 0),
            spec(LANES, 0),
            spec(LANES, 2),
            spec(LANES, 1),
            whole((1, LANES)),
            whole((LANES, inner)),
            whole((1, inner)),
        ],
        out_specs=spec(inner, 0),
        out_shape=jax.ShapeDtypeStruct(values.shape, F32),
        scratch_shapes=[pltpu.VMEM((LANES, inner), F32)],
        cost_estimate=estimate(count * size, inner, 30, 32 << 20),
        compiler_params=params(),
    )(values, keys, keys, keys, rate, entering, skip)


def states_kernel(
    geometry,
    columns_ref,
    rate_ref,
    forward_ref,
    forward_total_ref,
    entering_forward_ref,
    out_ref,
    entering_backward_ref,
    outputs,
    logs,
    before,
    scales_ref,
    local_memory,
    memory,
    total,
    sent,
    received,
    found,
    out_send,
    out_recv,
    back_send,
    back_recv,
    own_sem,
):
    inner, size, column_rows, head_size, count, spatial = geometry
    slices = count // 2
    rows, wide = LANES // slices, inner // 2
    pairs = wide // LANES
    frame, place, part = lax.axis_index("frame"), lax.axis_index("spatial"), lax.axis_index("dp")
    me = frame * spatial + place

    def device(index):
        return (index // spatial, index % spatial, part)

    barrier = pltpu.get_barrier_semaphore()

    def greet(k, carry):
        peer = device((me + k) % count)
        pl.semaphore_signal(barrier, inc=1, device_id=peer, device_id_type=MESH)
        return carry

    lax.fori_loop(1, count, greet, 0)
    pl.semaphore_wait(barrier, count - 1)

    def send_slices(way, memory_ref, total_ref):
        totals = total_ref[...]
        shifted = pltpu.roll(totals, LANES - 2 * pairs, 1)
        for index in range(count):
            first, lane = rows * (index // 2), wide * (index % 2)
            sent[way, index, :, pl.ds(0, wide)] = memory_ref[pl.ds(first, rows), pl.ds(lane, wide)]
            sent[way, index, :, pl.ds(wide, LANES)] = shifted if index % 2 else totals

        def one(k, carry):
            to = (me + k) % count
            pltpu.make_async_remote_copy(
                src_ref=sent.at[way, to],
                dst_ref=received.at[way, me],
                send_sem=out_send.at[way, k],
                recv_sem=out_recv.at[way, k],
                device_id=device(to),
                device_id_type=MESH,
            ).start()
            return carry

        lax.fori_loop(1, count, one, 0)
        received[way, me] = sent[way, me]

    def scan(way, reverse, entering_ref):
        def arrive(k, carry):
            source = (me + count - k) % count
            pltpu.make_async_remote_copy(
                src_ref=received.at[way, source],
                dst_ref=received.at[way, source],
                send_sem=out_send.at[way, k],
                recv_sem=out_recv.at[way, k],
                device_id=device(source),
                device_id_type=MESH,
            ).wait_recv()
            return carry

        lax.fori_loop(1, count, arrive, 0)
        entering = jnp.zeros((rows, wide), F32)
        for k in range(count):
            at = count - 1 - k if reverse else k
            found[way, at] = entering
            decay = jnp.exp(received[way, at, :, pl.ds(wide, LANES)])
            spreads = [spread(decay, pair, head_size) for pair in range(pairs)]
            decay = jnp.concatenate(spreads, axis=1)
            entering = entering * decay + received[way, at, :, pl.ds(0, wide)]

        def one(k, carry):
            to = (me + k) % count
            pltpu.make_async_remote_copy(
                src_ref=found.at[way, to],
                dst_ref=place_of(entering_ref, me),
                send_sem=back_send.at[way, k],
                recv_sem=back_recv.at[way, k],
                device_id=device(to),
                device_id_type=MESH,
            ).start()
            return carry

        lax.fori_loop(1, count, one, 0)
        copy = pltpu.make_async_copy(found.at[way, me], place_of(entering_ref, me), own_sem.at[way])
        copy.start()

    def place_of(entering_ref, index):
        first = pl.multiple_of(rows * (index // 2), rows)
        lane = pl.multiple_of(wide * (index % 2), LANES)
        return entering_ref.at[pl.ds(first, rows), pl.ds(lane, wide)]

    def finish_way(way, entering_ref):
        def arrive(k, carry):
            source = (me + count - k) % count
            to = (me + k) % count
            pltpu.make_async_remote_copy(
                src_ref=found.at[way, source],
                dst_ref=place_of(entering_ref, source),
                send_sem=back_send.at[way, k],
                recv_sem=back_recv.at[way, k],
                device_id=device(to),
                device_id_type=MESH,
            ).wait()
            pltpu.make_async_remote_copy(
                src_ref=sent.at[way, to],
                dst_ref=received.at[way, me],
                send_sem=out_send.at[way, k],
                recv_sem=out_recv.at[way, k],
                device_id=device(to),
                device_id_type=MESH,
            ).wait_send()
            return carry

        lax.fori_loop(1, count, arrive, 0)
        pltpu.make_async_copy(
            found.at[way, me], place_of(entering_ref, me), own_sem.at[way]
        ).wait()

    send_slices(0, forward_ref, forward_total_ref)
    memory[...] = jnp.zeros_like(memory)
    total[...] = jnp.zeros_like(total)
    chunks = (columns_ref.shape[1] - 16) // (size // 4)
    last = columns_ref.shape[1] - 16

    part_rows = size // 4

    def chunk_at(step):
        at = pl.ds(pl.multiple_of((chunks - 1 - step) * part_rows, 16), part_rows)
        chunk = Chunk(
            column_rows,
            columns_ref.at[:, at, pl.ds(0, inner)],
            columns_ref.at[:, at, pl.ds(inner, LANES)],
            columns_ref.at[:, at, pl.ds(inner + 2 * LANES, LANES)],
            columns_ref.at[:, pl.ds(last, 16), :],
        )
        return chunk, split(chunk.queries(columns_ref.at[:, at, pl.ds(inner + LANES, LANES)]))

    def fold_columns(step, carry):
        chunk, _ = chunk_at(step)

        def keep_values(pair):
            values = chunk.values(pair)
            outputs[step, :, pl.ds(pair * LANES, LANES)] = values
            return values

        fold_chunk(
            keep_values,
            chunk.keys(),
            chunk.steps(),
            rate_ref[...],
            chunk.earlier(),
            head_size,
            memory,
            total,
        )
        return carry

    def output_columns(step, carry):
        chunk, queries = chunk_at(step)

        def emit(pair, result, values):
            outputs[step, :, pl.ds(pair * LANES, LANES)] = result

        def kept_values(pair):
            return outputs[step, :, pl.ds(pair * LANES, LANES)]

        running, chunk_total = output_chunk(
            chunk, kept_values, queries, rate_ref[...], local_memory, head_size, emit
        )
        logs[step] = before[0:1] + running
        before[...] = before[...] + chunk_total

        @pl.when(step == 2)
        def _():
            scan(1, True, entering_backward_ref)

        @pl.when(step == 3)
        def _():
            scan(0, False, entering_forward_ref)

        return carry

    def correct(step, carry):
        _, queries = chunk_at(step)
        arrived = jnp.exp(logs[step])
        first = pl.multiple_of((chunks - 1 - step) * part_rows, 16)
        here = rows_iota((16, LANES)) == chunks - 1 - step
        for pair in range(inner // LANES):
            lanes = pl.ds(pair * LANES, LANES)
            added = carried(queries, memory[:, lanes]) * spread(arrived, pair, head_size)
            result = outputs[step, :, lanes] + added
            scale, factor = code_scale(jnp.max(jnp.abs(result), axis=0, keepdims=True))
            out_ref[:, pl.ds(first, part_rows), lanes] = encode(result * factor).reshape(
                4, part_rows, LANES
            )
            scales_ref[:, lanes] = jnp.where(here, scale.astype(F32), scales_ref[:, lanes])
        return carry

    lax.fori_loop(0, chunks, fold_columns, 0)
    send_slices(1, memory, total)
    local_memory[...] = jnp.zeros_like(local_memory)
    before[...] = jnp.zeros_like(before)
    scales_ref[...] = jnp.zeros_like(scales_ref)
    lax.fori_loop(0, chunks, output_columns, 0)
    finish_way(1, entering_backward_ref)
    memory[...] = entering_backward_ref[...]
    lax.fori_loop(0, chunks, correct, 0)
    for k in range(4):
        out_ref[k, pl.ds(last, 16), :] = scales_ref[...].astype(BF16)
    finish_way(0, entering_forward_ref)


def column_output(columns, rate, memory, total, inner, size, column_rows, head_size):
    spatial = lax.axis_size("spatial")
    count = lax.axis_size("frame") * spatial
    rows, wide = LANES * 2 // count, inner // 2
    chunks = (columns.shape[1] - 16) * 4 // size
    vmem, hbm = pl.BlockSpec(memory_space=pltpu.VMEM), pl.BlockSpec(memory_space=pl.ANY)
    dma = pltpu.SemaphoreType.DMA
    geometry = (inner, size, column_rows, head_size, count, spatial)
    return pl.pallas_call(
        functools.partial(states_kernel, geometry),
        in_specs=[vmem] * 4,
        out_specs=[hbm, vmem],
        out_shape=[
            jax.ShapeDtypeStruct((LANES, inner), F32),
            jax.ShapeDtypeStruct(columns.shape[:2] + (inner,), BF16),
        ],
        scratch_shapes=[
            pltpu.VMEM((LANES, inner), F32),
            pltpu.VMEM((chunks, size, inner), F32),
            pltpu.VMEM((chunks, size, LANES), F32),
            pltpu.VMEM((8, LANES), F32),
            pltpu.VMEM((16, inner), F32),
            pltpu.VMEM((LANES, inner), F32),
            pltpu.VMEM((LANES, inner), F32),
            pltpu.VMEM((8, LANES), F32),
            pltpu.VMEM((2, count, rows, wide + LANES), F32),
            pltpu.VMEM((2, count, rows, wide + LANES), F32),
            pltpu.VMEM((2, count, rows, wide), F32),
            dma((2, count)),
            dma((2, count)),
            dma((2, count)),
            dma((2, count)),
            dma((2,)),
        ],
        compiler_params=pltpu.CompilerParams(
            collective_id=1, has_side_effects=True, vmem_limit_bytes=VMEM_BYTES
        ),
    )(columns, rate, memory, total)


def finish_kernel(head_size, groups, part, forward_ref, backward_ref, gate_ref, gain_ref, out_ref, moved_ref):
    col_total = forward_ref.shape[0] // 4
    quad = pl.program_id(0)
    last = backward_ref.shape[1] - 16
    scales = [backward_ref[k, pl.ds(last, 16), :].astype(F32) * (1.0 / CODE_TOP) for k in range(4)]

    def group_rows(group):
        piece, within = group // groups, group % groups
        first = pl.multiple_of(within * part + 16 * quad, 16)
        coded = backward_ref[piece, pl.ds(first, 16), :]
        return decode(coded) * scales[piece][within : within + 1, :]

    for at in range(col_total // 8):
        even, odd = group_rows(2 * at), group_rows(2 * at + 1)
        for k in (0, 1):
            low_half, high_half = even[8 * k : 8 * k + 8], odd[8 * k : 8 * k + 8]
            first, second = column_groups(low_half, high_half)
            moved_ref[pl.ds(2 * k * col_total + 8 * at, 8), :] = first
            moved_ref[pl.ds((2 * k + 1) * col_total + 8 * at, 8), :] = second
    wide = 2 * LANES
    same = rows_iota((wide, wide)) // head_size == lanes_iota((wide, wide)) // head_size
    ones = jnp.where(same, 1.0, 0.0).astype(BF16)
    for block in range(forward_ref.shape[1] // wide):
        lanes = pl.ds(block * wide, wide)
        gate = gate_ref[:, lanes]
        combined = forward_ref[:, lanes] + moved_ref[:, lanes]
        gated = combined * (gate / (1.0 + jnp.exp(-gate)))
        high, low = split(gated * gated)
        mean = (dot(high, ones) + dot(low, ones)) * (1.0 / head_size)
        normed = gated * lax.rsqrt(mean + 1e-5) * gain_ref[:, lanes]
        out_ref[:, lanes] = normed.astype(out_ref.dtype)


def finish(forward, backward, gate, gain, row_part, col_total, head_size):
    tokens, inner = forward.shape
    groups = col_total // GROUP // 4
    block = 4 * col_total
    flat = pl.BlockSpec((block, inner), lambda m: (m, 0))
    return pl.pallas_call(
        functools.partial(finish_kernel, head_size, groups, row_part * GROUP),
        grid=(row_part // 4,),
        in_specs=[flat, whole(backward.shape), flat, whole((1, inner))],
        out_specs=flat,
        out_shape=jax.ShapeDtypeStruct((tokens, inner), BF16),
        scratch_shapes=[pltpu.VMEM((block, inner), F32)],
        compiler_params=params(),
    )(forward, backward, gate, gain)


def pad_lanes(source):
    return jnp.pad(source, ((0, 0), (0, LANES - source.shape[1])))


def local(tokens, xz_weight, state_weight, step_weight, step_bias, decay_rate, skip, norm_gain):
    videos, frame_count, row_part, col_total, width = tokens.shape
    flattened = tokens.reshape(-1, width)
    inner = xz_weight.shape[1] // 2
    heads = step_weight.shape[1]
    head_size = inner // heads
    column_rows = row_part * lax.axis_size("spatial")
    size = column_rows * GROUP
    axes = ("frame", "spatial")

    thrice = pad_lanes(jnp.concatenate([step_weight] * 3, axis=1))
    bias = pad_lanes(jnp.concatenate([step_bias] * 3)[None])
    first_weight = jnp.concatenate([state_weight, thrice], axis=1)
    rates = pad_lanes(decay_rate)
    skips = jnp.repeat(skip[0] + skip[1], head_size)[None]

    values, keys, columns, memory, total, gate_weight = project(
        flattened,
        first_weight,
        bias,
        rates[0:1],
        xz_weight,
        row_part,
        col_total,
        inner,
        head_size,
        512,
    )
    entering, backward = column_output(
        columns, rates[1:2], memory, total, inner, size, column_rows, head_size
    )
    returned = lax.all_to_all(backward, "spatial", 0, 0, tiled=True)
    forward = row_output(
        values[None], keys[None], rates[0:1], entering, skips, inner, size, head_size
    )
    gate_weight, forward = lax.optimization_barrier((gate_weight, forward))
    gate_rows = gate_rows_of(flattened, gate_weight, xz_weight.shape[0])
    normed = finish(
        forward[0], returned, gate_rows, norm_gain[None], row_part, col_total, head_size
    )
    return normed.reshape(videos, frame_count, row_part, col_total, inner)


def solution(mesh):
    in_specs = (
        P("dp", "frame", "spatial", None, None),
        P(("spatial", "dp"), None),
        P(("spatial", "dp"), None),
        P(("spatial", "dp"), None),
        P(),
        P(),
        P(),
        P(),
    )
    out_specs = P("dp", "frame", "spatial", None, None)
    return jax.shard_map(local, mesh=mesh, in_specs=in_specs, out_specs=out_specs, check_vma=False)
```

```python
import functools

import jax
import jax.numpy as jnp
from jax import lax
from jax.experimental import pallas as pl
from jax.experimental.pallas import tpu as pltpu
from jax.sharding import PartitionSpec as P

F32 = jnp.float32
BF16 = jnp.bfloat16
LANES = 128
GROUP = 4
POWER = 17
LOG2_E = 1.4426950408889634
CODE_TOP = 128.0
STEP_LANES = 24
MESH = pl.DeviceIdType.MESH
VMEM_BYTES = 56 * 1024 * 1024


def split(value):
    high = value.astype(BF16)
    return high, (value - high.astype(F32)).astype(BF16)


def dot(a, b):
    return lax.dot_general(a, b, (((1,), (0,)), ((), ())), preferred_element_type=F32)


def rows_iota(shape):
    return lax.broadcasted_iota(jnp.int32, shape, 0)


def lanes_iota(shape):
    return lax.broadcasted_iota(jnp.int32, shape, 1)


def spread(columns, pair, head_size):
    first, second = columns[:, 2 * pair : 2 * pair + 1], columns[:, 2 * pair + 1 : 2 * pair + 2]
    shape = (columns.shape[0], LANES)
    return jnp.where(lanes_iota(shape) < head_size, first, second)


def params(semantics=("arbitrary",)):
    return pltpu.CompilerParams(vmem_limit_bytes=VMEM_BYTES, dimension_semantics=semantics)


def widen(columns, copies):
    heads = columns.shape[1]
    shape = (heads, LANES)
    head, lane = rows_iota(shape), lanes_iota(shape)
    place = (lax.rem(lane, heads) == head) & (lane < copies * heads)
    place = jnp.where(place, 1.0, 0.0).astype(BF16)
    if columns.dtype == BF16:
        return dot(columns, place)
    high = columns.astype(BF16)
    middle, low = split(columns - high.astype(F32))
    return dot(high, place) + dot(middle, place) + dot(low, place)


def encode(scaled):
    square = scaled * scaled
    fourth = square * square
    eighth = fourth * fourth
    return (eighth * eighth * scaled).astype(BF16)


def decode(coded):
    coded = coded.astype(F32)
    size = jnp.exp2(jnp.log2(jnp.abs(coded)) * (1.0 / POWER))
    return jnp.where(coded < 0.0, -size, size)


def code_scale(largest):
    scale = jnp.maximum(largest, 1e-30).astype(BF16)
    return scale, CODE_TOP / scale.astype(F32)


def column_groups(first, second):
    low = rows_iota(first.shape) < GROUP
    even = jnp.where(low, first, pltpu.roll(second, GROUP, 0))
    odd = jnp.where(low, pltpu.roll(first, GROUP, 0), second)
    return even, odd


def earlier_mask(size, column_rows):
    shape = (size, size)
    t, s = rows_iota(shape), lanes_iota(shape)
    if column_rows:

        def place(index):
            return size - 1 - (lax.rem(index, GROUP) * column_rows + index // GROUP)

        t, s = place(t), place(s)
    return s <= t


def running_logs(steps, rate, earlier):
    logs = -steps * rate
    high, rest = split(logs)
    middle = logs - high.astype(F32)
    middle, low = split(middle)
    before = jnp.where(earlier, 1.0, 0.0).astype(BF16)
    running = dot(before, high) + dot(before, middle) + dot(before, low)
    return running, jnp.sum(logs, axis=0, keepdims=True)


def advance(memory, keys_t, weighted, decay):
    keys_high, keys_low = keys_t
    high, low = split(weighted)
    both = dot(keys_high, jnp.concatenate([high, low], axis=1))
    added = both[:, :LANES] + both[:, LANES:] + dot(keys_low, high)
    return memory * decay + added


def fold_chunk(values, keys, steps, rate, earlier, head_size, memory_ref, total_ref):
    keys_t = split(jnp.transpose(keys))
    running, total = running_logs(steps, rate, earlier)
    coefficient = steps * jnp.exp(jnp.minimum(total - running, 0.0))
    decay = jnp.exp(total)
    for pair in range(memory_ref.shape[1] // LANES):
        lanes = pl.ds(pair * LANES, LANES)
        weighted = values(pair) * spread(coefficient, pair, head_size)
        memory_ref[:, lanes] = advance(
            memory_ref[:, lanes], keys_t, weighted, spread(decay, pair, head_size)
        )
    total_ref[...] = total_ref[...] + total
    return running


def in_order(ref, depth):
    parts = []
    for row in range(16):
        where, part, core = row // 4, (row // 2) % 2, row % 2
        parts.append(ref[pl.ds((core * 8 + part * 4 + where) * depth, depth), :])
    return jnp.concatenate(parts, axis=0)


def gate_kernel(depth, tokens_ref, weight_ref, gate_ref):
    width = weight_ref.shape[2]
    for quarter in range(0, 4, 2):
        weight = jnp.concatenate(
            [in_order(weight_ref.at[quarter + k], depth) for k in range(2)], axis=1
        )
        gate_ref[:, pl.ds(quarter * width, 2 * width)] = dot(tokens_ref[...], weight)


def gate_rows_of(tokens, weight, depth):
    total, model = tokens.shape
    inner = 4 * weight.shape[2]
    tile = total // 5
    return pl.pallas_call(
        functools.partial(gate_kernel, depth),
        grid=(5,),
        in_specs=[pl.BlockSpec((tile, model), lambda m: (m, 0)), whole(weight.shape)],
        out_specs=pl.BlockSpec((tile, inner), lambda m: (m, 0)),
        out_shape=jax.ShapeDtypeStruct((total, inner), F32),
        cost_estimate=pl.CostEstimate(
            flops=2 * total * model * inner, bytes_accessed=20 << 20, transcendentals=0
        ),
        compiler_params=params(),
    )(tokens, weight)


def project_kernel(
    geometry,
    tokens_ref,
    state_weight_ref,
    step_weight_ref,
    bias_ref,
    rate_ref,
    xz_ref,
    values_ref,
    keys_ref,
    columns_ref,
    memory_ref,
    total_ref,
    gate_ref,
    weight,
    gate_weight,
    product,
    middle,
    tokens,
    state_ref,
    own_sem,
    x_send,
    x_recv,
    y_send,
    y_recv,
    core_send,
    core_recv,
    move_send,
    move_recv,
    move_own,
    out_sem,
    gate_send,
    gate_recv,
    gate_out,
):
    row_part, col_total, inner, depth, blocks, head_size = geometry
    half = depth // 2
    frame, place, part = lax.axis_index("frame"), lax.axis_index("spatial"), lax.axis_index("dp")
    core, y = part % 2, (frame % 2) * 2 + part // 2
    right, left, across = (place + 1) % 4, (place + 3) % 4, (place + 2) % 4

    z = frame // 2

    def z_device(other):
        return (other * 2 + frame % 2, place, part)

    def y_device(other):
        return ((frame // 2) * 2 + other // 2, place, (other % 2) * 2 + core)

    x_right, x_left, x_across = (frame, right, part), (frame, left, part), (frame, across, part)
    y_up, y_down = y_device((y + 1) % 4), y_device((y + 3) % 4)
    partner = (frame, place, (part // 2) * 2 + 1 - core)

    barrier = pltpu.get_barrier_semaphore()
    z_up, z_down = z_device((z + 1) % 4), z_device((z + 3) % 4)
    peers = (x_right, x_left, x_across, y_up, y_down, z_up, z_down, partner)
    for peer in peers:
        pl.semaphore_signal(barrier, inc=1, device_id=peer, device_id_type=MESH)
    pl.semaphore_wait(barrier, len(peers))

    def slot(where, other_core, other_part):
        return other_core * 8 + other_part * 4 + where

    same, opposite = part // 2, 1 - part // 2
    sources = (place, left, right, across)

    def rows(index, first, count):
        return pl.ds(pl.multiple_of(index * depth + first, 16), count)

    def view(block, index, first, count):
        return weight.at[block, rows(index, first, count), pl.ds(0, blocks[block][1])]

    def own(block, first, count):
        start, width = blocks[block]
        if block == 0:
            return state_ref.at[pl.ds(first, count), :]
        return xz_ref.at[pl.ds(first, count), pl.ds(inner + start, width)]

    pending = []

    def send(source, target, send_sem, recv_sem, device):
        copy = pltpu.make_async_remote_copy(
            src_ref=source,
            dst_ref=target,
            send_sem=send_sem,
            recv_sem=recv_sem,
            device_id=device,
            device_id_type=MESH,
        )
        copy.start()
        pending.append(copy)

    def arrived(target, send_sem, recv_sem):
        pltpu.make_async_remote_copy(
            src_ref=target,
            dst_ref=target,
            send_sem=send_sem,
            recv_sem=recv_sem,
            device_id=x_right,
            device_id_type=MESH,
        ).wait_recv()

    def send_y(block, which, source_of):
        index = slot(sources[which], core, same)
        for part_at, device in ((0, y_up), (1, y_down)):
            first = part_at * half
            send(
                source_of(first),
                view(block, index, first, half),
                y_send.at[block, which, part_at],
                y_recv.at[block, which, part_at],
                device,
            )

    def send_core(block, at, index, source):
        send(
            source,
            view(block, index, 0, depth),
            core_send.at[block, at],
            core_recv.at[block, at],
            partner,
        )

    def send_own(block):
        index = slot(place, core, same)
        target = view(block, index, 0, depth)
        source = own(block, 0, depth)
        send(source, target, x_send.at[block, 0], x_recv.at[block, 0], x_right)
        send(source, target, x_send.at[block, 1], x_recv.at[block, 1], x_left)
        send_y(block, 0, lambda first: own(block, first, half))
        send_core(block, 0, index, source)
        copy = pltpu.make_async_copy(source, target, own_sem.at[block])
        copy.start()

    def relay(block):
        from_left, from_right = slot(left, core, same), slot(right, core, same)
        for which, index in ((1, from_left), (2, from_right)):
            arrived(
                view(block, index, 0, depth),
                x_send.at[block, which - 1],
                x_recv.at[block, which - 1],
            )
            part_at = which - 1
            send(
                view(block, index, part_at * half, half),
                view(block, index, part_at * half, half),
                x_send.at[block, 2 + part_at],
                x_recv.at[block, 2 + part_at],
                (x_right, x_left)[part_at],
            )
            send_y(block, which, lambda first: view(block, index, first, half))
            send_core(block, which, index, view(block, index, 0, depth))
    def relay_far(block):
        far = slot(across, core, same)
        for part_at in (0, 1):
            arrived(
                view(block, far, part_at * half, half),
                x_send.at[block, 2 + part_at],
                x_recv.at[block, 2 + part_at],
            )
        send_y(block, 3, lambda first: view(block, far, first, half))
        send_core(block, 3, far, view(block, far, 0, depth))

    def pass_on(block):
        for which in range(4):
            index = slot(sources[which], core, opposite)
            for part_at in (0, 1):
                arrived(
                    view(block, index, part_at * half, half),
                    y_send.at[block, which, part_at],
                    y_recv.at[block, which, part_at],
                )
            send_core(block, 4 + which, index, view(block, index, 0, depth))

    def gathered(block):
        for at in range(8):
            index = slot(sources[at % 4], 1 - core, same if at < 4 else opposite)
            arrived(
                view(block, index, 0, depth), core_send.at[block, at], core_recv.at[block, at]
            )
        index = slot(place, core, same)
        target = view(block, index, 0, depth)
        pltpu.make_async_copy(own(block, 0, depth), target, own_sem.at[block]).wait()


    quarter_width = gate_weight.shape[2]
    many, core_rows = 4 * depth, 8 * depth

    def gate_view(quarter, first, rows_count):
        return gate_weight.at[quarter, pl.ds(pl.multiple_of(first, 16), rows_count), :]

    def gate_copy(source, at, device):
        send(source, source, gate_send.at[at], gate_recv.at[at], device)

    def gate_arrived(target, at):
        arrived(target, gate_send.at[at], gate_recv.at[at])

    def gate_own():
        first = pl.multiple_of(z * quarter_width, LANES)
        return xz_ref.at[:, pl.ds(first, quarter_width)]

    def gate_start():
        target = gate_view(z, slot(place, core, same) * depth, depth)
        send(gate_own(), target, gate_send.at[0], gate_recv.at[0], x_right)
        send(gate_own(), target, gate_send.at[1], gate_recv.at[1], x_left)
        pltpu.make_async_copy(gate_own(), target, own_sem.at[len(blocks)]).start()

    def gate_x():
        for at, index in ((0, slot(left, core, same)), (1, slot(right, core, same))):
            gate_arrived(gate_view(z, index * depth, depth), at)
            gate_copy(gate_view(z, index * depth + at * half, half), 2 + at, (x_right, x_left)[at])

    def gate_y():
        far = slot(across, core, same) * depth
        for at in (0, 1):
            gate_arrived(gate_view(z, far + at * half, half), 2 + at)
        target = gate_view(z, slot(place, core, same) * depth, depth)
        pltpu.make_async_copy(gate_own(), target, own_sem.at[len(blocks)]).wait()
        first = slot(0, core, same) * depth
        for at, device in ((0, y_up), (1, y_down)):
            gate_copy(gate_view(z, first + at * (many // 2), many // 2), 4 + at, device)

    def gate_z():
        first = slot(0, core, opposite) * depth
        for at in (0, 1):
            gate_arrived(gate_view(z, first + at * (many // 2), many // 2), 4 + at)
        mine = gate_view(z, core * core_rows, core_rows)
        gate_copy(mine, 6, z_up)
        gate_copy(mine, 7, z_down)
        gate_copy(mine, 10, partner)

    def gate_pass():
        for at, quarter in ((0, (z + 3) % 4), (1, (z + 1) % 4)):
            mine = gate_view(quarter, core * core_rows, core_rows)
            gate_arrived(mine, 6 + at)
            part_rows = gate_view(quarter, core * core_rows + at * many, many)
            gate_copy(part_rows, 8 + at, (z_up, z_down)[at])
            gate_copy(mine, 11 + at, partner)

    def gate_end():
        quarter = (z + 2) % 4
        for at in (0, 1):
            gate_arrived(gate_view(quarter, core * core_rows + at * many, many), 8 + at)
        gate_copy(gate_view(quarter, core * core_rows, core_rows), 13, partner)
        for at, quarter in enumerate((z, (z + 3) % 4, (z + 1) % 4, (z + 2) % 4)):
            gate_arrived(gate_view(quarter, (1 - core) * core_rows, core_rows), 10 + at)

    tile = row_part * col_total // 5
    groups = col_total // GROUP // 4
    piece_rows = groups * row_part * GROUP
    outs = {}

    def compute(block):
        start, width = blocks[block]
        lanes = pl.ds(0, width)
        buffer = block

        def one_tile(i, largest):
            at = pl.ds(pl.multiple_of(i * tile, tile), tile)
            result = dot(tokens[at, :], in_order(weight.at[block, :, lanes], depth))
            if block == 0:
                raw = result[:, width - LANES :] + widen(bias_ref[...], 3)
                steps = jnp.maximum(raw, 0.0) + jnp.log1p(jnp.exp(-jnp.abs(raw)))
                result = jnp.concatenate([result[:, : width - LANES], steps], axis=1)
            product[buffer, at, lanes] = result
            return jnp.maximum(largest, jnp.max(jnp.abs(result), axis=0, keepdims=True))

        largest = lax.fori_loop(0, 5, one_tile, jnp.zeros((1, width), F32))
        if block == 0:
            out = keys_ref
        else:
            out = values_ref.at[:, pl.ds(start, width)]
        copy = pltpu.make_async_copy(product.at[buffer, :, lanes], out, out_sem.at[block])
        copy.start()
        outs[block] = copy

        scale, factor = code_scale(largest)

        def code(value):
            coded = encode(value * factor)
            if block == 0:
                exact = value[:, width - LANES :]
                high = exact.astype(BF16)
                rest = exact - high.astype(F32)
                second = rest.astype(BF16)
                third = (rest - second.astype(F32)).astype(BF16)
                lane = lanes_iota(exact.shape)
                heads = STEP_LANES
                parts = jnp.where(
                    lane < heads,
                    high.astype(F32),
                    jnp.where(lane < 2 * heads, second.astype(F32), third.astype(F32)),
                )
                coded = jnp.concatenate([coded[:, : width - LANES], parts.astype(BF16)], axis=1)
            return coded

        for quad in range(row_part // 4):

            def one_group(at, carry):
                both = []
                for pair in (2 * quad, 2 * quad + 1):
                    first = product[buffer, pl.ds(pl.multiple_of(2 * pair * col_total + 8 * at, 8), 8), lanes]
                    second = product[
                        buffer, pl.ds(pl.multiple_of((2 * pair + 1) * col_total + 8 * at, 8), 8), lanes
                    ]
                    both.append(column_groups(first, second))
                for odd in (0, 1):
                    group = 2 * at + odd
                    piece = group // groups
                    row = pl.multiple_of((group % groups) * row_part * GROUP + 16 * quad, 16)
                    value = jnp.concatenate([both[0][odd], both[1][odd]], axis=0)
                    middle[block, piece, pl.ds(row, 16), lanes] = code(value)
                return carry

            lax.fori_loop(0, col_total // 8, one_group, 0)
        for piece in range(4):
            middle[block, piece, pl.ds(piece_rows, 16), lanes] = jnp.broadcast_to(scale, (16, width))
        into = columns_ref.at[place, :, pl.ds(inner if block == 0 else start, width)]
        for at, (where, device) in enumerate(((right, x_right), (left, x_left), (across, x_across))):
            send(
                middle.at[block, where, :, lanes],
                into,
                move_send.at[block, at],
                move_recv.at[block, at],
                device,
            )
        pltpu.make_async_copy(middle.at[block, place, :, lanes], into, move_own.at[block]).start()

    count = len(blocks)
    state_columns = state_weight_ref.shape[1]
    state_ref[:, pl.ds(0, state_columns)] = state_weight_ref[...]
    state_ref[:, pl.ds(state_columns, LANES)] = widen(step_weight_ref[...], 3).astype(BF16)
    for block in range(count):
        send_own(block)
    gate_start()
    tokens_copy = pltpu.make_async_copy(tokens_ref, tokens, own_sem.at[count + 1])
    tokens_copy.start()
    relay(0)
    relay(1)
    gate_x()
    relay_far(0)
    for block in range(count):
        if block + 2 < count:
            relay(block + 2)
        if block + 1 < count:
            relay_far(block + 1)
        if block < 2:
            (gate_y, gate_z)[block]()
        pass_on(block)
        gathered(block)
        if block == 0:
            tokens_copy.wait()
        compute(block)

    gate_pass()

    memory_ref[...] = jnp.zeros_like(memory_ref)
    total_ref[...] = jnp.zeros_like(total_ref)

    rate = widen(rate_ref[...], 1)[0:1]

    def fold_rows(step, carry):
        at = pl.ds(pl.multiple_of(step * tile, 16), tile)
        block_pairs = blocks[1][1] // LANES

        def values(pair):
            return product[1 + pair // block_pairs, at, pl.ds(pair % block_pairs * LANES, LANES)]

        fold_chunk(
            values,
            product[0, at, pl.ds(0, LANES)],
            product[0, at, pl.ds(2 * LANES, LANES)],
            rate,
            earlier_mask(tile, 0),
            head_size,
            memory_ref,
            total_ref,
        )
        return carry

    lax.fori_loop(0, 5, fold_rows, 0)
    gate_end()
    gate_copies = [
        pltpu.make_async_copy(gate_weight.at[quarter], gate_ref.at[quarter], gate_out.at[quarter])
        for quarter in range(4)
    ]
    for copy in gate_copies:
        copy.start()
    for block in range(count):
        start, width = blocks[block]
        lanes = pl.ds(0, width)
        for at, where in enumerate((left, right, across)):
            into = columns_ref.at[where, :, pl.ds(inner if block == 0 else start, width)]
            arrived(into, move_send.at[block, at], move_recv.at[block, at])
        into = columns_ref.at[place, :, pl.ds(inner if block == 0 else start, width)]
        pltpu.make_async_copy(middle.at[block, place, :, lanes], into, move_own.at[block]).wait()
    for copy in list(outs.values()) + gate_copies:
        copy.wait()
    for copy in pending:
        copy.wait_send()


def project(
    tokens, state_weight, step_weight, bias, rate, xz_weight, row_part, col_total, inner, head_size, block_width
):
    depth = state_weight.shape[0]
    state_width = state_weight.shape[1] + LANES
    count = inner // block_width + 1
    blocks = ((0, state_width),) + tuple((k * block_width, block_width) for k in range(count - 1))
    width = max(block_width, state_width)
    total = tokens.shape[0]
    piece_rows = total // 4 + 16
    vmem, hbm = pl.BlockSpec(memory_space=pltpu.VMEM), pl.BlockSpec(memory_space=pl.ANY)
    dma = pltpu.SemaphoreType.DMA
    return pl.pallas_call(
        functools.partial(project_kernel, (row_part, col_total, inner, depth, blocks, head_size)),
        in_specs=[hbm, vmem, vmem, vmem, vmem, hbm],
        out_specs=[hbm, hbm, hbm, vmem, vmem, hbm],
        out_shape=[
            jax.ShapeDtypeStruct((total, inner), F32),
            jax.ShapeDtypeStruct((total, state_width), F32),
            jax.ShapeDtypeStruct((4, piece_rows, inner + state_width), BF16),
            jax.ShapeDtypeStruct((LANES, inner), F32),
            jax.ShapeDtypeStruct((8, LANES), F32),
            jax.ShapeDtypeStruct((4, tokens.shape[1], inner // 4), BF16),
        ],
        scratch_shapes=[
            pltpu.VMEM((count, tokens.shape[1], width), BF16),
            pltpu.VMEM((4, tokens.shape[1], inner // 4), BF16),
            pltpu.VMEM((count, total, width), F32),
            pltpu.VMEM((count, 4, piece_rows, width), BF16),
            pltpu.VMEM(tokens.shape, BF16),
            pltpu.VMEM((depth, state_width), BF16),
            dma((count + 2,)),
            dma((count, 4)),
            dma((count, 4)),
            dma((count, 4, 2)),
            dma((count, 4, 2)),
            dma((count, 8)),
            dma((count, 8)),
            dma((count, 3)),
            dma((count, 3)),
            dma((count,)),
            dma((count,)),
            dma((14,)),
            dma((14,)),
            dma((4,)),
        ],
        compiler_params=pltpu.CompilerParams(
            collective_id=0, has_side_effects=True, vmem_limit_bytes=VMEM_BYTES
        ),
    )(tokens, state_weight, step_weight, bias, rate, xz_weight)


class Chunk:
    def __init__(self, column_rows, values_ref, keys_ref, steps_ref, scale_ref):
        self.size = values_ref.shape[0] * values_ref.shape[1]
        self.inner = values_ref.shape[2]
        self.pairs = self.inner // LANES
        self.column_rows, self.values_ref, self.scale_ref = column_rows, values_ref, scale_ref
        self.keys_ref, self.steps_ref = keys_ref, steps_ref
        if column_rows:
            self.scales = [scale_ref[k, pl.ds(0, 16), :].astype(F32)[0:1] for k in range(4)]

    def read(self, ref, lanes, scale_lane):
        block = ref[:, :, lanes]
        if not self.column_rows:
            return block.reshape(self.size, LANES)
        block = decode(block)
        parts = [
            block[k] * (self.scales[k][:, scale_lane : scale_lane + LANES] * (1.0 / CODE_TOP))
            for k in range(4)
        ]
        return jnp.concatenate(parts, axis=0)

    def values(self, pair):
        return self.read(self.values_ref, pl.ds(pair * LANES, LANES), pair * LANES)

    def keys(self):
        return self.read(self.keys_ref, pl.ds(0, LANES), self.inner)

    def queries(self, ref):
        return self.read(ref, pl.ds(0, LANES), self.inner + LANES)

    def steps(self):
        block = self.steps_ref[...].reshape(self.size, LANES)
        if not self.column_rows:
            return block
        shape = (LANES, LANES)
        part, head = rows_iota(shape), lanes_iota(shape)
        fold = (lax.rem(part, STEP_LANES) == head) & (part < 3 * STEP_LANES)
        return dot(block, jnp.where(fold, 1.0, 0.0).astype(BF16))

    def earlier(self):
        return earlier_mask(self.size, self.column_rows)


def score_matrix(queries, keys_t, earlier):
    queries_high, queries_low = queries
    scores = dot(queries_high, keys_t[0]) + dot(queries_high, keys_t[1]) + dot(queries_low, keys_t[0])
    return jnp.where(earlier, scores, 0.0)


def within_pair(pair, scaled, running_bits, across, scores, head_size):
    high, low = scaled
    both = jnp.concatenate([high, low], axis=1)
    halves = []
    for head in (2 * pair, 2 * pair + 1):
        between = running_bits[:, head : head + 1] - across[head : head + 1, :]
        kernel_high, kernel_low = split(jnp.exp2(jnp.minimum(between, 0.0)) * scores)
        part = dot(kernel_high, both)
        halves.append(part[:, :LANES] + part[:, LANES:] + dot(kernel_low, high))
    return jnp.where(lanes_iota(halves[0].shape) < head_size, halves[0], halves[1])


def output_chunk(chunk, queries, rate, memory_ref, head_size, emit):
    steps = chunk.steps()
    keys_t = split(jnp.transpose(chunk.keys()))
    earlier = chunk.earlier()
    running, total = running_logs(steps, rate, earlier)
    running_bits = running * LOG2_E
    across = jnp.transpose(running_bits)
    scores = score_matrix(queries, keys_t, earlier)
    arrived = jnp.exp(running)
    leaving = jnp.exp(jnp.minimum(total - running, 0.0))
    decay = jnp.exp(total)
    for pair in range(chunk.pairs):
        lanes = pl.ds(pair * LANES, LANES)
        values = chunk.values(pair)
        scaled = values * spread(steps, pair, head_size)
        result = within_pair(pair, split(scaled), running_bits, across, scores, head_size)
        memory = memory_ref[:, lanes]
        result = result + carried(queries, memory) * spread(arrived, pair, head_size)
        emit(pair, result, values)
        weighted = scaled * spread(leaving, pair, head_size)
        memory_ref[:, lanes] = advance(memory, keys_t, weighted, spread(decay, pair, head_size))


def carried(queries, memory):
    queries_high, queries_low = queries
    memory_high, memory_low = split(memory)
    part = dot(queries_high, jnp.concatenate([memory_high, memory_low], axis=1))
    return part[:, :LANES] + part[:, LANES:] + dot(queries_low, memory_high)


def output_kernel(
    head_size, values_ref, keys_ref, steps_ref, queries_ref, rate_ref, entering_ref, skip_ref, out_ref, memory_ref
):
    chunk = Chunk(0, values_ref, keys_ref, steps_ref, None)

    @pl.when(pl.program_id(0) == 0)
    def _():
        memory_ref[...] = entering_ref[...]

    def emit(pair, result, values):
        lanes = pl.ds(pair * LANES, LANES)
        result = result + values * skip_ref[:, lanes]
        out_ref[:, :, lanes] = result.reshape(1, chunk.size, LANES)

    queries = split(chunk.queries(queries_ref))
    output_chunk(chunk, queries, widen(rate_ref[...], 1)[0:1], memory_ref, head_size, emit)


def whole(shape):
    return pl.BlockSpec(shape, lambda j: (0,) * len(shape))


def estimate(tokens, inner, passes, transfers):
    return pl.CostEstimate(
        flops=2 * tokens * inner * 192 * passes, bytes_accessed=transfers, transcendentals=0
    )


def row_output(values, keys, rate, entering, skip, inner, size, head_size):
    count = values.shape[1] // size

    def spec(lane_count, lane_block):
        return pl.BlockSpec((1, size, lane_count), lambda j: (0, j, lane_block))

    return pl.pallas_call(
        functools.partial(output_kernel, head_size),
        grid=(count,),
        in_specs=[
            spec(inner, 0),
            spec(LANES, 0),
            spec(LANES, 2),
            spec(LANES, 1),
            whole(rate.shape),
            whole((LANES, inner)),
            whole((1, inner)),
        ],
        out_specs=spec(inner, 0),
        out_shape=jax.ShapeDtypeStruct(values.shape, F32),
        scratch_shapes=[pltpu.VMEM((LANES, inner), F32)],
        cost_estimate=estimate(count * size, inner, 30, 32 << 20),
        compiler_params=params(),
    )(values, keys, keys, keys, rate, entering, skip)


def states_kernel(
    geometry,
    columns_ref,
    rate_ref,
    forward_ref,
    forward_total_ref,
    entering_forward_ref,
    out_ref,
    entering_backward_ref,
    outputs,
    logs,
    before,
    scales_ref,
    kept_memory,
    kept_steps,
    memory,
    total,
    sent,
    received,
    found,
    returned,
    out_send,
    out_recv,
    back_send,
    back_recv,
):
    inner, size, column_rows, head_size, count, spatial = geometry
    rows, wide = LANES * 4 // count, inner // 4
    pairs = wide // LANES
    frame, place, part = lax.axis_index("frame"), lax.axis_index("spatial"), lax.axis_index("dp")
    me = frame * spatial + place

    def device(index):
        return (index // spatial, index % spatial, part)

    barrier = pltpu.get_barrier_semaphore()

    def greet(k, carry):
        peer = device((me + k) % count)
        pl.semaphore_signal(barrier, inc=1, device_id=peer, device_id_type=MESH)
        return carry

    lax.fori_loop(1, count, greet, 0)
    pl.semaphore_wait(barrier, count - 1)

    def place_of(index):
        return pl.ds(rows * (index // 4), rows), pl.ds(wide * (index % 4), wide)

    def put(ref, way, index, block, extra):
        scale, factor = code_scale(jnp.max(jnp.abs(block), axis=0, keepdims=True))
        ref[way, index, :, pl.ds(0, wide)] = encode(block * factor)
        scale = scale.astype(F32)
        beside = [scale[:, k * LANES : (k + 1) * LANES] for k in range(pairs)] + extra
        row = rows_iota((rows, LANES))
        filled = jnp.zeros((rows, LANES), F32)
        for k, line in enumerate(beside):
            filled = jnp.where(row == k, line, filled)
        ref[way, index, :, pl.ds(wide, LANES)] = filled.astype(BF16)

    def take(ref, way, index):
        beside = ref[way, index, :, pl.ds(wide, LANES)].astype(F32)
        scale = jnp.concatenate([beside[k : k + 1] for k in range(pairs)], axis=1)
        block = decode(ref[way, index, :, pl.ds(0, wide)]) * (scale * (1.0 / CODE_TOP))
        return block, beside

    def send_slices(way, memory_ref, total_ref):
        totals = total_ref[...]
        parts = []
        for quarter in range(4):
            shift = (LANES - 2 * pairs * quarter) % LANES
            turned = (pltpu.roll(totals, shift, 1) if shift else totals)[0:1]
            high = turned.astype(BF16).astype(F32)
            middle = (turned - high).astype(BF16).astype(F32)
            parts.append([high, middle, turned - high - middle])
        for index in range(count):
            where_rows, where_lanes = place_of(index)
            put(sent, way, index, memory_ref[where_rows, where_lanes], parts[index % 4])

        def one(k, carry):
            to = (me + k) % count
            pltpu.make_async_remote_copy(
                src_ref=sent.at[way, to],
                dst_ref=received.at[way, me],
                send_sem=out_send.at[way, k],
                recv_sem=out_recv.at[way, k],
                device_id=device(to),
                device_id_type=MESH,
            ).start()
            return carry

        lax.fori_loop(1, count, one, 0)
        received[way, me] = sent[way, me]

    def scan(way, reverse):
        def arrive(k, carry):
            source = (me + count - k) % count
            pltpu.make_async_remote_copy(
                src_ref=received.at[way, source],
                dst_ref=received.at[way, source],
                send_sem=out_send.at[way, k],
                recv_sem=out_recv.at[way, k],
                device_id=device(source),
                device_id_type=MESH,
            ).wait_recv()
            return carry

        lax.fori_loop(1, count, arrive, 0)
        entering = jnp.zeros((rows, wide), F32)
        for k in range(count):
            at = count - 1 - k if reverse else k
            put(found, way, at, entering, [])
            block, beside = take(received, way, at)
            total_at = beside[pairs : pairs + 1] + beside[pairs + 1 : pairs + 2]
            decay = jnp.exp(total_at + beside[pairs + 2 : pairs + 3])
            spreads = [spread(decay, pair, head_size) for pair in range(pairs)]
            entering = entering * jnp.concatenate(spreads, axis=1) + block

        def one(k, carry):
            to = (me + k) % count
            pltpu.make_async_remote_copy(
                src_ref=found.at[way, to],
                dst_ref=returned.at[way, me],
                send_sem=back_send.at[way, k],
                recv_sem=back_recv.at[way, k],
                device_id=device(to),
                device_id_type=MESH,
            ).start()
            return carry

        lax.fori_loop(1, count, one, 0)
        returned[way, me] = found[way, me]

    def finish_way(way, entering_ref):
        def arrive(k, carry):
            source = (me + count - k) % count
            to = (me + k) % count
            pltpu.make_async_remote_copy(
                src_ref=found.at[way, to],
                dst_ref=returned.at[way, source],
                send_sem=back_send.at[way, k],
                recv_sem=back_recv.at[way, k],
                device_id=device(to),
                device_id_type=MESH,
            ).wait()
            pltpu.make_async_remote_copy(
                src_ref=sent.at[way, to],
                dst_ref=received.at[way, me],
                send_sem=out_send.at[way, k],
                recv_sem=out_recv.at[way, k],
                device_id=device(to),
                device_id_type=MESH,
            ).wait_send()
            return carry

        lax.fori_loop(1, count, arrive, 0)
        for index in range(count):
            where_rows, where_lanes = place_of(index)
            entering_ref[where_rows, where_lanes] = take(returned, way, index)[0]

    rate = widen(rate_ref[...], 1)[1:2]
    send_slices(0, forward_ref, forward_total_ref)
    memory[...] = jnp.zeros_like(memory)
    total[...] = jnp.zeros_like(total)
    chunks = (columns_ref.shape[1] - 16) // (size // 4)
    last = columns_ref.shape[1] - 16

    part_rows = size // 4

    def chunk_at(step):
        at = pl.ds(pl.multiple_of((chunks - 1 - step) * part_rows, 16), part_rows)
        chunk = Chunk(
            column_rows,
            columns_ref.at[:, at, pl.ds(0, inner)],
            columns_ref.at[:, at, pl.ds(inner, LANES)],
            columns_ref.at[:, at, pl.ds(inner + 2 * LANES, LANES)],
            columns_ref.at[:, pl.ds(last, 16), :],
        )
        return chunk, split(chunk.queries(columns_ref.at[:, at, pl.ds(inner + LANES, LANES)]))

    def fold_columns(step, carry):
        chunk, _ = chunk_at(step)
        steps = chunk.steps()
        kept_memory[step] = memory[...]
        before[step] = total[...]
        kept_steps[step] = steps

        def keep_values(pair):
            values = chunk.values(pair)
            outputs[step, :, pl.ds(pair * LANES, LANES)] = values
            return values

        logs[step] = fold_chunk(
            keep_values, chunk.keys(), steps, rate, chunk.earlier(), head_size, memory, total
        )
        return carry

    def output_columns(step, carry):
        chunk, queries = chunk_at(step)
        running_bits = logs[step] * LOG2_E
        across = jnp.transpose(running_bits)
        scores = score_matrix(queries, split(jnp.transpose(chunk.keys())), chunk.earlier())
        steps = kept_steps[step]
        for pair in range(chunk.pairs):
            lanes = pl.ds(pair * LANES, LANES)
            scaled = split(outputs[step, :, lanes] * spread(steps, pair, head_size))
            outputs[step, :, lanes] = within_pair(
                pair, scaled, running_bits, across, scores, head_size
            )

        @pl.when(step == 2)
        def _():
            scan(1, True)

        @pl.when(step == 3)
        def _():
            scan(0, False)

        return carry

    def correct(step, carry):
        _, queries = chunk_at(step)
        arrived = jnp.exp(logs[step])
        decayed = jnp.exp(before[step][0:1])
        first = pl.multiple_of((chunks - 1 - step) * part_rows, 16)
        here = rows_iota((16, LANES)) == chunks - 1 - step
        for pair in range(inner // LANES):
            lanes = pl.ds(pair * LANES, LANES)
            entering = entering_backward_ref[:, lanes] * spread(decayed, pair, head_size)
            added = carried(queries, kept_memory[step, :, lanes] + entering)
            result = outputs[step, :, lanes] + added * spread(arrived, pair, head_size)
            scale, factor = code_scale(jnp.max(jnp.abs(result), axis=0, keepdims=True))
            out_ref[:, pl.ds(first, part_rows), lanes] = encode(result * factor).reshape(
                4, part_rows, LANES
            )
            scales_ref[:, lanes] = jnp.where(here, scale.astype(F32), scales_ref[:, lanes])
        return carry

    lax.fori_loop(0, chunks, fold_columns, 0)
    send_slices(1, memory, total)
    scales_ref[...] = jnp.zeros_like(scales_ref)
    lax.fori_loop(0, chunks, output_columns, 0)
    finish_way(1, entering_backward_ref)
    lax.fori_loop(0, chunks, correct, 0)
    for k in range(4):
        out_ref[k, pl.ds(last, 16), :] = scales_ref[...].astype(BF16)
    finish_way(0, entering_forward_ref)


def column_output(columns, rate, memory, total, inner, size, column_rows, head_size):
    spatial = lax.axis_size("spatial")
    count = lax.axis_size("frame") * spatial
    slices = (2, count, LANES * 4 // count, inner // 4 + LANES)
    chunks = (columns.shape[1] - 16) * 4 // size
    vmem = pl.BlockSpec(memory_space=pltpu.VMEM)
    dma = pltpu.SemaphoreType.DMA
    geometry = (inner, size, column_rows, head_size, count, spatial)
    return pl.pallas_call(
        functools.partial(states_kernel, geometry),
        in_specs=[vmem] * 4,
        out_specs=[vmem, vmem],
        out_shape=[
            jax.ShapeDtypeStruct((LANES, inner), F32),
            jax.ShapeDtypeStruct(columns.shape[:2] + (inner,), BF16),
        ],
        scratch_shapes=[
            pltpu.VMEM((LANES, inner), F32),
            pltpu.VMEM((chunks, size, inner), F32),
            pltpu.VMEM((chunks, size, LANES), F32),
            pltpu.VMEM((chunks, 8, LANES), F32),
            pltpu.VMEM((16, inner), F32),
            pltpu.VMEM((chunks, LANES, inner), F32),
            pltpu.VMEM((chunks, size, LANES), F32),
            pltpu.VMEM((LANES, inner), F32),
            pltpu.VMEM((8, LANES), F32),
            pltpu.VMEM(slices, BF16),
            pltpu.VMEM(slices, BF16),
            pltpu.VMEM(slices, BF16),
            pltpu.VMEM(slices, BF16),
            dma((2, count)),
            dma((2, count)),
            dma((2, count)),
            dma((2, count)),
        ],
        compiler_params=pltpu.CompilerParams(
            collective_id=1, has_side_effects=True, vmem_limit_bytes=VMEM_BYTES
        ),
    )(columns, rate, memory, total)


def finish_kernel(head_size, groups, part, forward_ref, backward_ref, gate_ref, gain_ref, out_ref, moved_ref):
    col_total = forward_ref.shape[0] // 4
    quad = pl.program_id(0)
    last = backward_ref.shape[1] - 16
    scales = [backward_ref[k, pl.ds(last, 16), :].astype(F32) * (1.0 / CODE_TOP) for k in range(4)]

    def group_rows(group):
        piece, within = group // groups, group % groups
        first = pl.multiple_of(within * part + 16 * quad, 16)
        coded = backward_ref[piece, pl.ds(first, 16), :]
        return decode(coded) * scales[piece][within : within + 1, :]

    for at in range(col_total // 8):
        even, odd = group_rows(2 * at), group_rows(2 * at + 1)
        for k in (0, 1):
            low_half, high_half = even[8 * k : 8 * k + 8], odd[8 * k : 8 * k + 8]
            first, second = column_groups(low_half, high_half)
            moved_ref[pl.ds(2 * k * col_total + 8 * at, 8), :] = first
            moved_ref[pl.ds((2 * k + 1) * col_total + 8 * at, 8), :] = second
    wide = 2 * LANES
    same = rows_iota((wide, wide)) // head_size == lanes_iota((wide, wide)) // head_size
    ones = jnp.where(same, 1.0, 0.0).astype(BF16)
    for block in range(forward_ref.shape[1] // wide):
        lanes = pl.ds(block * wide, wide)
        gate = gate_ref[:, lanes]
        combined = forward_ref[:, lanes] + moved_ref[:, lanes]
        gated = combined * (gate / (1.0 + jnp.exp(-gate)))
        high, low = split(gated * gated)
        mean = (dot(high, ones) + dot(low, ones)) * (1.0 / head_size)
        normed = gated * lax.rsqrt(mean + 1e-5) * gain_ref[:, lanes]
        out_ref[:, lanes] = normed.astype(out_ref.dtype)


def finish(forward, backward, gate, gain, row_part, col_total, head_size):
    tokens, inner = forward.shape
    groups = col_total // GROUP // 4
    block = 4 * col_total
    flat = pl.BlockSpec((block, inner), lambda m: (m, 0))
    return pl.pallas_call(
        functools.partial(finish_kernel, head_size, groups, row_part * GROUP),
        grid=(row_part // 4,),
        in_specs=[flat, whole(backward.shape), flat, whole((1, inner))],
        out_specs=flat,
        out_shape=jax.ShapeDtypeStruct((tokens, inner), BF16),
        scratch_shapes=[pltpu.VMEM((block, inner), F32)],
        compiler_params=params(),
    )(forward, backward, gate, gain)


def local(tokens, xz_weight, state_weight, step_weight, step_bias, decay_rate, skip, norm_gain):
    videos, frame_count, row_part, col_total, width = tokens.shape
    flattened = tokens.reshape(-1, width)
    inner = xz_weight.shape[1] // 2
    heads = step_weight.shape[1]
    head_size = inner // heads
    column_rows = row_part * lax.axis_size("spatial")
    size = column_rows * GROUP
    axes = ("frame", "spatial")

    skips = jnp.repeat(skip[0] + skip[1], head_size)[None]

    values, keys, columns, memory, total, gate_weight = project(
        flattened,
        state_weight,
        step_weight,
        step_bias[None],
        decay_rate,
        xz_weight,
        row_part,
        col_total,
        inner,
        head_size,
        512,
    )
    entering, backward = column_output(
        columns, decay_rate, memory, total, inner, size, column_rows, head_size
    )
    returned = lax.all_to_all(backward, "spatial", 0, 0, tiled=True)
    forward = row_output(
        values[None], keys[None], decay_rate, entering, skips, inner, size, head_size
    )
    gate_weight, forward = lax.optimization_barrier((gate_weight, forward))
    gate_rows = gate_rows_of(flattened, gate_weight, xz_weight.shape[0])
    normed = finish(
        forward[0], returned, gate_rows, norm_gain[None], row_part, col_total, head_size
    )
    return normed.reshape(videos, frame_count, row_part, col_total, inner)


def solution(mesh):
    in_specs = (
        P("dp", "frame", "spatial", None, None),
        P(("spatial", "dp"), None),
        P(("spatial", "dp"), None),
        P(("spatial", "dp"), None),
        P(),
        P(),
        P(),
        P(),
    )
    out_specs = P("dp", "frame", "spatial", None, None)
    return jax.shard_map(local, mesh=mesh, in_specs=in_specs, out_specs=out_specs, check_vma=False)
```

```python
import functools

import jax
import jax.numpy as jnp
from jax import lax
from jax.experimental import pallas as pl
from jax.experimental.pallas import tpu as pltpu
from jax.sharding import PartitionSpec as P

F32 = jnp.float32
BF16 = jnp.bfloat16
LANES = 128
GROUP = 4
POWER = 17
LOG2_E = 1.4426950408889634
CODE_TOP = 128.0
STEP_LANES = 24
MESH = pl.DeviceIdType.MESH
VMEM_BYTES = 56 * 1024 * 1024


def split(value):
    high = value.astype(BF16)
    return high, (value - high.astype(F32)).astype(BF16)


def dot(a, b):
    return lax.dot_general(a, b, (((1,), (0,)), ((), ())), preferred_element_type=F32)


def rows_iota(shape):
    return lax.broadcasted_iota(jnp.int32, shape, 0)


def lanes_iota(shape):
    return lax.broadcasted_iota(jnp.int32, shape, 1)


def spread(columns, pair, head_size):
    first, second = columns[:, 2 * pair : 2 * pair + 1], columns[:, 2 * pair + 1 : 2 * pair + 2]
    shape = (columns.shape[0], LANES)
    return jnp.where(lanes_iota(shape) < head_size, first, second)


def params(semantics=("arbitrary",)):
    return pltpu.CompilerParams(vmem_limit_bytes=VMEM_BYTES, dimension_semantics=semantics)


def widen(columns, copies):
    heads = columns.shape[1]
    shape = (heads, LANES)
    head, lane = rows_iota(shape), lanes_iota(shape)
    place = (lax.rem(lane, heads) == head) & (lane < copies * heads)
    place = jnp.where(place, 1.0, 0.0).astype(BF16)
    if columns.dtype == BF16:
        return dot(columns, place)
    high = columns.astype(BF16)
    middle, low = split(columns - high.astype(F32))
    return dot(high, place) + dot(middle, place) + dot(low, place)


def encode(scaled):
    square = scaled * scaled
    fourth = square * square
    eighth = fourth * fourth
    return (eighth * eighth * scaled).astype(BF16)


def decode(coded):
    coded = coded.astype(F32)
    size = jnp.exp2(jnp.log2(jnp.abs(coded)) * (1.0 / POWER))
    return jnp.where(coded < 0.0, -size, size)


def code_scale(largest):
    scale = jnp.maximum(largest, 1e-30).astype(BF16)
    return scale, CODE_TOP / scale.astype(F32)


def column_groups(first, second):
    low = rows_iota(first.shape) < GROUP
    even = jnp.where(low, first, pltpu.roll(second, GROUP, 0))
    odd = jnp.where(low, pltpu.roll(first, GROUP, 0), second)
    return even, odd


def earlier_mask(size, column_rows):
    shape = (size, size)
    t, s = rows_iota(shape), lanes_iota(shape)
    if column_rows:

        def place(index):
            return size - 1 - (lax.rem(index, GROUP) * column_rows + index // GROUP)

        t, s = place(t), place(s)
    return s <= t


def running_logs(steps, rate, earlier):
    logs = -steps * rate
    high, rest = split(logs)
    middle = logs - high.astype(F32)
    middle, low = split(middle)
    before = jnp.where(earlier, 1.0, 0.0).astype(BF16)
    running = dot(before, high) + dot(before, middle) + dot(before, low)
    return running, jnp.sum(logs, axis=0, keepdims=True)


def advance(memory, keys_t, weighted, decay):
    keys_high, keys_low = keys_t
    high, low = split(weighted)
    both = dot(keys_high, jnp.concatenate([high, low], axis=1))
    added = both[:, :LANES] + both[:, LANES:] + dot(keys_low, high)
    return memory * decay + added


def fold_chunk(values, keys, steps, rate, earlier, head_size, memory_ref, total_ref):
    keys_t = split(jnp.transpose(keys))
    running, total = running_logs(steps, rate, earlier)
    coefficient = steps * jnp.exp(jnp.minimum(total - running, 0.0))
    decay = jnp.exp(total)
    for pair in range(memory_ref.shape[1] // LANES):
        lanes = pl.ds(pair * LANES, LANES)
        weighted = values(pair) * spread(coefficient, pair, head_size)
        memory_ref[:, lanes] = advance(
            memory_ref[:, lanes], keys_t, weighted, spread(decay, pair, head_size)
        )
    total_ref[...] = total_ref[...] + total
    return running


def in_order(ref, depth):
    parts = []
    for row in range(16):
        where, part, core = row // 4, (row // 2) % 2, row % 2
        parts.append(ref[pl.ds((core * 8 + part * 4 + where) * depth, depth), :])
    return jnp.concatenate(parts, axis=0)


def gate_kernel(depth, tokens_ref, weight_ref, gate_ref):
    width = weight_ref.shape[2]
    for quarter in range(0, 4, 2):
        weight = jnp.concatenate(
            [in_order(weight_ref.at[quarter + k], depth) for k in range(2)], axis=1
        )
        gate_ref[:, pl.ds(quarter * width, 2 * width)] = dot(tokens_ref[...], weight)


def gate_rows_of(tokens, weight, depth):
    total, model = tokens.shape
    inner = 4 * weight.shape[2]
    tile = total // 2
    return pl.pallas_call(
        functools.partial(gate_kernel, depth),
        grid=(2,),
        in_specs=[pl.BlockSpec((tile, model), lambda m: (m, 0)), whole(weight.shape)],
        out_specs=pl.BlockSpec((tile, inner), lambda m: (m, 0)),
        out_shape=jax.ShapeDtypeStruct((total, inner), F32),
        cost_estimate=pl.CostEstimate(
            flops=2 * total * model * inner, bytes_accessed=20 << 20, transcendentals=0
        ),
        compiler_params=params(),
    )(tokens, weight)


def project_kernel(
    geometry,
    tokens_ref,
    state_weight_ref,
    step_weight_ref,
    bias_ref,
    rate_ref,
    xz_ref,
    values_ref,
    keys_ref,
    columns_ref,
    memory_ref,
    total_ref,
    gate_ref,
    kept_ref,
    before_ref,
    weight,
    gate_weight,
    product,
    middle,
    tokens,
    state_ref,
    kept,
    own_sem,
    x_send,
    x_recv,
    y_send,
    y_recv,
    core_send,
    core_recv,
    move_send,
    move_recv,
    move_own,
    out_sem,
    gate_send,
    gate_recv,
    gate_out,
    kept_sem,
):
    row_part, col_total, inner, depth, blocks, head_size = geometry
    half = depth // 2
    frame, place, part = lax.axis_index("frame"), lax.axis_index("spatial"), lax.axis_index("dp")
    core, y = part % 2, (frame % 2) * 2 + part // 2
    right, left, across = (place + 1) % 4, (place + 3) % 4, (place + 2) % 4

    z = frame // 2

    def z_device(other):
        return (other * 2 + frame % 2, place, part)

    def y_device(other):
        return ((frame // 2) * 2 + other // 2, place, (other % 2) * 2 + core)

    x_right, x_left, x_across = (frame, right, part), (frame, left, part), (frame, across, part)
    y_up, y_down = y_device((y + 1) % 4), y_device((y + 3) % 4)
    partner = (frame, place, (part // 2) * 2 + 1 - core)

    barrier = pltpu.get_barrier_semaphore()
    z_up, z_down = z_device((z + 1) % 4), z_device((z + 3) % 4)
    peers = (x_right, x_left, x_across, y_up, y_down, z_up, z_down, partner)
    for peer in peers:
        pl.semaphore_signal(barrier, inc=1, device_id=peer, device_id_type=MESH)
    pl.semaphore_wait(barrier, len(peers))

    def slot(where, other_core, other_part):
        return other_core * 8 + other_part * 4 + where

    same, opposite = part // 2, 1 - part // 2
    sources = (place, left, right, across)

    def rows(index, first, count):
        return pl.ds(pl.multiple_of(index * depth + first, 16), count)

    def view(block, index, first, count):
        return weight.at[block, rows(index, first, count), pl.ds(0, blocks[block][1])]

    def own(block, first, count):
        start, width = blocks[block]
        if block == 0:
            return state_ref.at[pl.ds(first, count), :]
        return xz_ref.at[pl.ds(first, count), pl.ds(inner + start, width)]

    pending = []

    def send(source, target, send_sem, recv_sem, device):
        copy = pltpu.make_async_remote_copy(
            src_ref=source,
            dst_ref=target,
            send_sem=send_sem,
            recv_sem=recv_sem,
            device_id=device,
            device_id_type=MESH,
        )
        copy.start()
        pending.append(copy)

    def arrived(target, send_sem, recv_sem):
        pltpu.make_async_remote_copy(
            src_ref=target,
            dst_ref=target,
            send_sem=send_sem,
            recv_sem=recv_sem,
            device_id=x_right,
            device_id_type=MESH,
        ).wait_recv()

    def send_y(block, which, source_of):
        index = slot(sources[which], core, same)
        for part_at, device in ((0, y_up), (1, y_down)):
            first = part_at * half
            send(
                source_of(first),
                view(block, index, first, half),
                y_send.at[block, which, part_at],
                y_recv.at[block, which, part_at],
                device,
            )

    def send_core(block, at, index, source):
        send(
            source,
            view(block, index, 0, depth),
            core_send.at[block, at],
            core_recv.at[block, at],
            partner,
        )

    def send_own(block):
        index = slot(place, core, same)
        target = view(block, index, 0, depth)
        source = own(block, 0, depth)
        send(source, target, x_send.at[block, 0], x_recv.at[block, 0], x_right)
        send(source, target, x_send.at[block, 1], x_recv.at[block, 1], x_left)
        send_y(block, 0, lambda first: own(block, first, half))
        send_core(block, 0, index, source)
        copy = pltpu.make_async_copy(source, target, own_sem.at[block])
        copy.start()

    def relay(block):
        from_left, from_right = slot(left, core, same), slot(right, core, same)
        for which, index in ((1, from_left), (2, from_right)):
            arrived(
                view(block, index, 0, depth),
                x_send.at[block, which - 1],
                x_recv.at[block, which - 1],
            )
            part_at = which - 1
            send(
                view(block, index, part_at * half, half),
                view(block, index, part_at * half, half),
                x_send.at[block, 2 + part_at],
                x_recv.at[block, 2 + part_at],
                (x_right, x_left)[part_at],
            )
            send_y(block, which, lambda first: view(block, index, first, half))
            send_core(block, which, index, view(block, index, 0, depth))
    def relay_far(block):
        far = slot(across, core, same)
        for part_at in (0, 1):
            arrived(
                view(block, far, part_at * half, half),
                x_send.at[block, 2 + part_at],
                x_recv.at[block, 2 + part_at],
            )
        send_y(block, 3, lambda first: view(block, far, first, half))
        send_core(block, 3, far, view(block, far, 0, depth))

    def pass_on(block):
        for which in range(4):
            index = slot(sources[which], core, opposite)
            for part_at in (0, 1):
                arrived(
                    view(block, index, part_at * half, half),
                    y_send.at[block, which, part_at],
                    y_recv.at[block, which, part_at],
                )
            send_core(block, 4 + which, index, view(block, index, 0, depth))

    def gathered(block):
        for at in range(8):
            index = slot(sources[at % 4], 1 - core, same if at < 4 else opposite)
            arrived(
                view(block, index, 0, depth), core_send.at[block, at], core_recv.at[block, at]
            )
        index = slot(place, core, same)
        target = view(block, index, 0, depth)
        pltpu.make_async_copy(own(block, 0, depth), target, own_sem.at[block]).wait()


    quarter_width = gate_weight.shape[2]
    many, core_rows = 4 * depth, 8 * depth

    def gate_view(quarter, first, rows_count):
        return gate_weight.at[quarter, pl.ds(pl.multiple_of(first, 16), rows_count), :]

    def gate_copy(source, at, device):
        send(source, source, gate_send.at[at], gate_recv.at[at], device)

    def gate_arrived(target, at):
        arrived(target, gate_send.at[at], gate_recv.at[at])

    def gate_own():
        first = pl.multiple_of(z * quarter_width, LANES)
        return xz_ref.at[:, pl.ds(first, quarter_width)]

    def gate_start():
        target = gate_view(z, slot(place, core, same) * depth, depth)
        send(gate_own(), target, gate_send.at[0], gate_recv.at[0], x_right)
        send(gate_own(), target, gate_send.at[1], gate_recv.at[1], x_left)
        pltpu.make_async_copy(gate_own(), target, own_sem.at[len(blocks)]).start()

    def gate_x():
        for at, index in ((0, slot(left, core, same)), (1, slot(right, core, same))):
            gate_arrived(gate_view(z, index * depth, depth), at)
            gate_copy(gate_view(z, index * depth + at * half, half), 2 + at, (x_right, x_left)[at])

    def gate_y():
        far = slot(across, core, same) * depth
        for at in (0, 1):
            gate_arrived(gate_view(z, far + at * half, half), 2 + at)
        target = gate_view(z, slot(place, core, same) * depth, depth)
        pltpu.make_async_copy(gate_own(), target, own_sem.at[len(blocks)]).wait()
        first = slot(0, core, same) * depth
        for at, device in ((0, y_up), (1, y_down)):
            gate_copy(gate_view(z, first + at * (many // 2), many // 2), 4 + at, device)

    def gate_z():
        first = slot(0, core, opposite) * depth
        for at in (0, 1):
            gate_arrived(gate_view(z, first + at * (many // 2), many // 2), 4 + at)
        mine = gate_view(z, core * core_rows, core_rows)
        gate_copy(mine, 6, z_up)
        gate_copy(mine, 7, z_down)
        gate_copy(mine, 10, partner)

    def gate_pass():
        for at, quarter in ((0, (z + 3) % 4), (1, (z + 1) % 4)):
            mine = gate_view(quarter, core * core_rows, core_rows)
            gate_arrived(mine, 6 + at)
            part_rows = gate_view(quarter, core * core_rows + at * many, many)
            gate_copy(part_rows, 8 + at, (z_up, z_down)[at])
            gate_copy(mine, 11 + at, partner)

    def gate_end():
        quarter = (z + 2) % 4
        for at in (0, 1):
            gate_arrived(gate_view(quarter, core * core_rows + at * many, many), 8 + at)
        gate_copy(gate_view(quarter, core * core_rows, core_rows), 13, partner)
        for at, quarter in enumerate((z, (z + 3) % 4, (z + 1) % 4, (z + 2) % 4)):
            gate_arrived(gate_view(quarter, (1 - core) * core_rows, core_rows), 10 + at)

    tile = row_part * col_total // 5
    groups = col_total // GROUP // 4
    piece_rows = groups * row_part * GROUP
    outs = {}

    def compute(block):
        start, width = blocks[block]
        lanes = pl.ds(0, width)
        buffer = block

        def one_tile(i, largest):
            at = pl.ds(pl.multiple_of(i * tile, tile), tile)
            result = dot(tokens[at, :], in_order(weight.at[block, :, lanes], depth))
            if block == 0:
                raw = result[:, width - LANES :] + widen(bias_ref[...], 3)
                steps = jnp.maximum(raw, 0.0) + jnp.log1p(jnp.exp(-jnp.abs(raw)))
                result = jnp.concatenate([result[:, : width - LANES], steps], axis=1)
            product[buffer, at, lanes] = result
            return jnp.maximum(largest, jnp.max(jnp.abs(result), axis=0, keepdims=True))

        largest = lax.fori_loop(0, 5, one_tile, jnp.zeros((1, width), F32))
        if block == 0:
            out = keys_ref
        else:
            out = values_ref.at[:, pl.ds(start, width)]
        copy = pltpu.make_async_copy(product.at[buffer, :, lanes], out, out_sem.at[block])
        copy.start()
        outs[block] = copy

        scale, factor = code_scale(largest)

        def code(value):
            coded = encode(value * factor)
            if block == 0:
                exact = value[:, width - LANES :]
                high = exact.astype(BF16)
                rest = exact - high.astype(F32)
                second = rest.astype(BF16)
                third = (rest - second.astype(F32)).astype(BF16)
                lane = lanes_iota(exact.shape)
                heads = STEP_LANES
                parts = jnp.where(
                    lane < heads,
                    high.astype(F32),
                    jnp.where(lane < 2 * heads, second.astype(F32), third.astype(F32)),
                )
                coded = jnp.concatenate([coded[:, : width - LANES], parts.astype(BF16)], axis=1)
            return coded

        for quad in range(row_part // 4):

            def one_group(at, carry):
                both = []
                for pair in (2 * quad, 2 * quad + 1):
                    first = product[buffer, pl.ds(pl.multiple_of(2 * pair * col_total + 8 * at, 8), 8), lanes]
                    second = product[
                        buffer, pl.ds(pl.multiple_of((2 * pair + 1) * col_total + 8 * at, 8), 8), lanes
                    ]
                    both.append(column_groups(first, second))
                for odd in (0, 1):
                    group = 2 * at + odd
                    piece = group // groups
                    row = pl.multiple_of((group % groups) * row_part * GROUP + 16 * quad, 16)
                    value = jnp.concatenate([both[0][odd], both[1][odd]], axis=0)
                    middle[block, piece, pl.ds(row, 16), lanes] = code(value)
                return carry

            lax.fori_loop(0, col_total // 8, one_group, 0)
        for piece in range(4):
            middle[block, piece, pl.ds(piece_rows, 16), lanes] = jnp.broadcast_to(scale, (16, width))
        into = columns_ref.at[place, :, pl.ds(inner if block == 0 else start, width)]
        for at, (where, device) in enumerate(((right, x_right), (left, x_left), (across, x_across))):
            send(
                middle.at[block, where, :, lanes],
                into,
                move_send.at[block, at],
                move_recv.at[block, at],
                device,
            )
        pltpu.make_async_copy(middle.at[block, place, :, lanes], into, move_own.at[block]).start()

    count = len(blocks)
    state_columns = state_weight_ref.shape[1]
    state_ref[:, pl.ds(0, state_columns)] = state_weight_ref[...]
    state_ref[:, pl.ds(state_columns, LANES)] = widen(step_weight_ref[...], 3).astype(BF16)
    for block in range(count):
        send_own(block)
    gate_start()
    tokens_copy = pltpu.make_async_copy(tokens_ref, tokens, own_sem.at[count + 1])
    tokens_copy.start()
    relay(0)
    relay(1)
    gate_x()
    relay_far(0)
    for block in range(count):
        if block + 2 < count:
            relay(block + 2)
        if block + 1 < count:
            relay_far(block + 1)
        if block < 2:
            (gate_y, gate_z)[block]()
        pass_on(block)
        gathered(block)
        if block == 0:
            tokens_copy.wait()
        compute(block)

    gate_pass()

    memory_ref[...] = jnp.zeros_like(memory_ref)
    total_ref[...] = jnp.zeros_like(total_ref)

    rate = widen(rate_ref[...], 1)[0:1]

    def fold_rows(step, carry):
        at = pl.ds(pl.multiple_of(step * tile, 16), tile)
        kept[step] = memory_ref[...]
        before_ref[step] = total_ref[...]
        block_pairs = blocks[1][1] // LANES

        def values(pair):
            return product[1 + pair // block_pairs, at, pl.ds(pair % block_pairs * LANES, LANES)]

        fold_chunk(
            values,
            product[0, at, pl.ds(0, LANES)],
            product[0, at, pl.ds(2 * LANES, LANES)],
            rate,
            earlier_mask(tile, 0),
            head_size,
            memory_ref,
            total_ref,
        )
        return carry

    lax.fori_loop(0, 5, fold_rows, 0)
    kept_copy = pltpu.make_async_copy(kept, kept_ref, kept_sem.at[0])
    kept_copy.start()
    gate_end()
    gate_copies = [
        pltpu.make_async_copy(gate_weight.at[quarter], gate_ref.at[quarter], gate_out.at[quarter])
        for quarter in range(4)
    ]
    for copy in gate_copies:
        copy.start()
    for block in range(count):
        start, width = blocks[block]
        lanes = pl.ds(0, width)
        for at, where in enumerate((left, right, across)):
            into = columns_ref.at[where, :, pl.ds(inner if block == 0 else start, width)]
            arrived(into, move_send.at[block, at], move_recv.at[block, at])
        into = columns_ref.at[place, :, pl.ds(inner if block == 0 else start, width)]
        pltpu.make_async_copy(middle.at[block, place, :, lanes], into, move_own.at[block]).wait()
    for copy in list(outs.values()) + gate_copies + [kept_copy]:
        copy.wait()
    for copy in pending:
        copy.wait_send()


def project(
    tokens, state_weight, step_weight, bias, rate, xz_weight, row_part, col_total, inner, head_size, block_width
):
    depth = state_weight.shape[0]
    state_width = state_weight.shape[1] + LANES
    count = inner // block_width + 1
    blocks = ((0, state_width),) + tuple((k * block_width, block_width) for k in range(count - 1))
    width = max(block_width, state_width)
    total = tokens.shape[0]
    piece_rows = total // 4 + 16
    vmem, hbm = pl.BlockSpec(memory_space=pltpu.VMEM), pl.BlockSpec(memory_space=pl.ANY)
    dma = pltpu.SemaphoreType.DMA
    return pl.pallas_call(
        functools.partial(project_kernel, (row_part, col_total, inner, depth, blocks, head_size)),
        in_specs=[hbm, vmem, vmem, vmem, vmem, hbm],
        out_specs=[hbm, hbm, hbm, vmem, vmem, hbm, hbm, vmem],
        out_shape=[
            jax.ShapeDtypeStruct((total, inner), F32),
            jax.ShapeDtypeStruct((total, state_width), F32),
            jax.ShapeDtypeStruct((4, piece_rows, inner + state_width), BF16),
            jax.ShapeDtypeStruct((LANES, inner), F32),
            jax.ShapeDtypeStruct((8, LANES), F32),
            jax.ShapeDtypeStruct((4, tokens.shape[1], inner // 4), BF16),
            jax.ShapeDtypeStruct((5, LANES, inner), F32),
            jax.ShapeDtypeStruct((5, 8, LANES), F32),
        ],
        scratch_shapes=[
            pltpu.VMEM((count, tokens.shape[1], width), BF16),
            pltpu.VMEM((4, tokens.shape[1], inner // 4), BF16),
            pltpu.VMEM((count, total, width), F32),
            pltpu.VMEM((count, 4, piece_rows, width), BF16),
            pltpu.VMEM(tokens.shape, BF16),
            pltpu.VMEM((depth, state_width), BF16),
            pltpu.VMEM((5, LANES, inner), F32),
            dma((count + 2,)),
            dma((count, 4)),
            dma((count, 4)),
            dma((count, 4, 2)),
            dma((count, 4, 2)),
            dma((count, 8)),
            dma((count, 8)),
            dma((count, 3)),
            dma((count, 3)),
            dma((count,)),
            dma((count,)),
            dma((14,)),
            dma((14,)),
            dma((4,)),
            dma((1,)),
        ],
        compiler_params=pltpu.CompilerParams(
            collective_id=0, has_side_effects=True, vmem_limit_bytes=VMEM_BYTES
        ),
    )(tokens, state_weight, step_weight, bias, rate, xz_weight)


class Chunk:
    def __init__(self, column_rows, values_ref, keys_ref, steps_ref, scale_ref):
        self.size = values_ref.shape[0] * values_ref.shape[1]
        self.inner = values_ref.shape[2]
        self.pairs = self.inner // LANES
        self.column_rows, self.values_ref, self.scale_ref = column_rows, values_ref, scale_ref
        self.keys_ref, self.steps_ref = keys_ref, steps_ref
        if column_rows:
            self.scales = [scale_ref[k, pl.ds(0, 16), :].astype(F32)[0:1] for k in range(4)]

    def read(self, ref, lanes, scale_lane):
        block = ref[:, :, lanes]
        if not self.column_rows:
            return block.reshape(self.size, LANES)
        block = decode(block)
        parts = [
            block[k] * (self.scales[k][:, scale_lane : scale_lane + LANES] * (1.0 / CODE_TOP))
            for k in range(4)
        ]
        return jnp.concatenate(parts, axis=0)

    def values(self, pair):
        return self.read(self.values_ref, pl.ds(pair * LANES, LANES), pair * LANES)

    def keys(self):
        return self.read(self.keys_ref, pl.ds(0, LANES), self.inner)

    def queries(self, ref):
        return self.read(ref, pl.ds(0, LANES), self.inner + LANES)

    def steps(self):
        block = self.steps_ref[...].reshape(self.size, LANES)
        if not self.column_rows:
            return block
        shape = (LANES, LANES)
        part, head = rows_iota(shape), lanes_iota(shape)
        fold = (lax.rem(part, STEP_LANES) == head) & (part < 3 * STEP_LANES)
        return dot(block, jnp.where(fold, 1.0, 0.0).astype(BF16))

    def earlier(self):
        return earlier_mask(self.size, self.column_rows)


def score_matrix(queries, keys_t, earlier):
    queries_high, queries_low = queries
    scores = dot(queries_high, keys_t[0]) + dot(queries_high, keys_t[1]) + dot(queries_low, keys_t[0])
    return jnp.where(earlier, scores, 0.0)


def within_pair(pair, scaled, running_bits, across, scores, head_size):
    high, low = scaled
    both = jnp.concatenate([high, low], axis=1)
    halves = []
    for head in (2 * pair, 2 * pair + 1):
        between = running_bits[:, head : head + 1] - across[head : head + 1, :]
        kernel_high, kernel_low = split(jnp.exp2(jnp.minimum(between, 0.0)) * scores)
        part = dot(kernel_high, both)
        halves.append(part[:, :LANES] + part[:, LANES:] + dot(kernel_low, high))
    return jnp.where(lanes_iota(halves[0].shape) < head_size, halves[0], halves[1])


def carried(queries, memory):
    queries_high, queries_low = queries
    memory_high, memory_low = split(memory)
    part = dot(queries_high, jnp.concatenate([memory_high, memory_low], axis=1))
    return part[:, :LANES] + part[:, LANES:] + dot(queries_low, memory_high)


def output_kernel(
    head_size,
    values_ref,
    keys_ref,
    steps_ref,
    queries_ref,
    kept_ref,
    before_ref,
    rate_ref,
    entering_ref,
    skip_ref,
    out_ref,
):
    chunk = Chunk(0, values_ref, keys_ref, steps_ref, None)
    queries = split(chunk.queries(queries_ref))
    steps, earlier = chunk.steps(), chunk.earlier()
    running, _ = running_logs(steps, widen(rate_ref[...], 1)[0:1], earlier)
    running_bits = running * LOG2_E
    across = jnp.transpose(running_bits)
    scores = score_matrix(queries, split(jnp.transpose(chunk.keys())), earlier)
    arrived, decayed = jnp.exp(running), jnp.exp(before_ref[0, 0:1])
    for pair in range(chunk.pairs):
        lanes = pl.ds(pair * LANES, LANES)
        values = chunk.values(pair)
        scaled = split(values * spread(steps, pair, head_size))
        result = within_pair(pair, scaled, running_bits, across, scores, head_size)
        memory = kept_ref[0, :, lanes] + entering_ref[:, lanes] * spread(decayed, pair, head_size)
        result = result + carried(queries, memory) * spread(arrived, pair, head_size)
        result = result + values * skip_ref[:, lanes]
        out_ref[:, :, lanes] = result.reshape(1, chunk.size, LANES)


def whole(shape):
    return pl.BlockSpec(shape, lambda j: (0,) * len(shape))


def estimate(tokens, inner, passes, transfers):
    return pl.CostEstimate(
        flops=2 * tokens * inner * 192 * passes, bytes_accessed=transfers, transcendentals=0
    )


def row_output(values, keys, kept, before, rate, entering, skip, inner, size, head_size):
    count = values.shape[1] // size

    def spec(lane_count, lane_block):
        return pl.BlockSpec((1, size, lane_count), lambda j: (0, j, lane_block))

    return pl.pallas_call(
        functools.partial(output_kernel, head_size),
        grid=(count,),
        in_specs=[
            spec(inner, 0),
            spec(LANES, 0),
            spec(LANES, 2),
            spec(LANES, 1),
            pl.BlockSpec((1, LANES, inner), lambda j: (j, 0, 0)),
            pl.BlockSpec((1, 8, LANES), lambda j: (j, 0, 0)),
            whole(rate.shape),
            whole((LANES, inner)),
            whole((1, inner)),
        ],
        out_specs=spec(inner, 0),
        out_shape=jax.ShapeDtypeStruct(values.shape, F32),
        cost_estimate=estimate(count * size, inner, 30, 32 << 20),
        compiler_params=params(),
    )(values, keys, keys, keys, kept, before, rate, entering, skip)


def states_kernel(
    geometry,
    columns_ref,
    rate_ref,
    forward_ref,
    forward_total_ref,
    entering_forward_ref,
    out_ref,
    entering_backward_ref,
    outputs,
    logs,
    before,
    scales_ref,
    kept_memory,
    kept_steps,
    memory,
    total,
    sent,
    received,
    found,
    returned,
    out_send,
    out_recv,
    back_send,
    back_recv,
):
    inner, size, column_rows, head_size, count, spatial = geometry
    rows, wide = LANES * 4 // count, inner // 4
    pairs = wide // LANES
    frame, place, part = lax.axis_index("frame"), lax.axis_index("spatial"), lax.axis_index("dp")
    me = frame * spatial + place

    def device(index):
        return (index // spatial, index % spatial, part)

    barrier = pltpu.get_barrier_semaphore()

    def greet(k, carry):
        peer = device((me + k) % count)
        pl.semaphore_signal(barrier, inc=1, device_id=peer, device_id_type=MESH)
        return carry

    lax.fori_loop(1, count, greet, 0)
    pl.semaphore_wait(barrier, count - 1)

    def place_of(index):
        return pl.ds(rows * (index // 4), rows), pl.ds(wide * (index % 4), wide)

    def put(ref, way, index, block, extra):
        scale, factor = code_scale(jnp.max(jnp.abs(block), axis=0, keepdims=True))
        ref[way, index, :, pl.ds(0, wide)] = encode(block * factor)
        scale = scale.astype(F32)
        beside = [scale[:, k * LANES : (k + 1) * LANES] for k in range(pairs)] + extra
        row = rows_iota((rows, LANES))
        filled = jnp.zeros((rows, LANES), F32)
        for k, line in enumerate(beside):
            filled = jnp.where(row == k, line, filled)
        ref[way, index, :, pl.ds(wide, LANES)] = filled.astype(BF16)

    def take(ref, way, index):
        beside = ref[way, index, :, pl.ds(wide, LANES)].astype(F32)
        scale = jnp.concatenate([beside[k : k + 1] for k in range(pairs)], axis=1)
        block = decode(ref[way, index, :, pl.ds(0, wide)]) * (scale * (1.0 / CODE_TOP))
        return block, beside

    def send_slices(way, memory_ref, total_ref):
        totals = total_ref[...]
        parts = []
        for quarter in range(4):
            shift = (LANES - 2 * pairs * quarter) % LANES
            turned = (pltpu.roll(totals, shift, 1) if shift else totals)[0:1]
            high = turned.astype(BF16).astype(F32)
            middle = (turned - high).astype(BF16).astype(F32)
            parts.append([high, middle, turned - high - middle])
        for index in range(count):
            where_rows, where_lanes = place_of(index)
            put(sent, way, index, memory_ref[where_rows, where_lanes], parts[index % 4])

        def one(k, carry):
            to = (me + k) % count
            pltpu.make_async_remote_copy(
                src_ref=sent.at[way, to],
                dst_ref=received.at[way, me],
                send_sem=out_send.at[way, k],
                recv_sem=out_recv.at[way, k],
                device_id=device(to),
                device_id_type=MESH,
            ).start()
            return carry

        lax.fori_loop(1, count, one, 0)
        received[way, me] = sent[way, me]

    def scan(way, reverse):
        def arrive(k, carry):
            source = (me + count - k) % count
            pltpu.make_async_remote_copy(
                src_ref=received.at[way, source],
                dst_ref=received.at[way, source],
                send_sem=out_send.at[way, k],
                recv_sem=out_recv.at[way, k],
                device_id=device(source),
                device_id_type=MESH,
            ).wait_recv()
            return carry

        lax.fori_loop(1, count, arrive, 0)
        entering = jnp.zeros((rows, wide), F32)
        for k in range(count):
            at = count - 1 - k if reverse else k
            put(found, way, at, entering, [])
            block, beside = take(received, way, at)
            total_at = beside[pairs : pairs + 1] + beside[pairs + 1 : pairs + 2]
            decay = jnp.exp(total_at + beside[pairs + 2 : pairs + 3])
            spreads = [spread(decay, pair, head_size) for pair in range(pairs)]
            entering = entering * jnp.concatenate(spreads, axis=1) + block

        def one(k, carry):
            to = (me + k) % count
            pltpu.make_async_remote_copy(
                src_ref=found.at[way, to],
                dst_ref=returned.at[way, me],
                send_sem=back_send.at[way, k],
                recv_sem=back_recv.at[way, k],
                device_id=device(to),
                device_id_type=MESH,
            ).start()
            return carry

        lax.fori_loop(1, count, one, 0)
        returned[way, me] = found[way, me]

    def finish_way(way, entering_ref):
        def arrive(k, carry):
            source = (me + count - k) % count
            to = (me + k) % count
            pltpu.make_async_remote_copy(
                src_ref=found.at[way, to],
                dst_ref=returned.at[way, source],
                send_sem=back_send.at[way, k],
                recv_sem=back_recv.at[way, k],
                device_id=device(to),
                device_id_type=MESH,
            ).wait()
            pltpu.make_async_remote_copy(
                src_ref=sent.at[way, to],
                dst_ref=received.at[way, me],
                send_sem=out_send.at[way, k],
                recv_sem=out_recv.at[way, k],
                device_id=device(to),
                device_id_type=MESH,
            ).wait_send()
            return carry

        lax.fori_loop(1, count, arrive, 0)
        for index in range(count):
            where_rows, where_lanes = place_of(index)
            entering_ref[where_rows, where_lanes] = take(returned, way, index)[0]

    rate = widen(rate_ref[...], 1)[1:2]
    send_slices(0, forward_ref, forward_total_ref)
    memory[...] = jnp.zeros_like(memory)
    total[...] = jnp.zeros_like(total)
    chunks = (columns_ref.shape[1] - 16) // (size // 4)
    last = columns_ref.shape[1] - 16

    part_rows = size // 4

    def chunk_at(step):
        at = pl.ds(pl.multiple_of((chunks - 1 - step) * part_rows, 16), part_rows)
        chunk = Chunk(
            column_rows,
            columns_ref.at[:, at, pl.ds(0, inner)],
            columns_ref.at[:, at, pl.ds(inner, LANES)],
            columns_ref.at[:, at, pl.ds(inner + 2 * LANES, LANES)],
            columns_ref.at[:, pl.ds(last, 16), :],
        )
        return chunk, split(chunk.queries(columns_ref.at[:, at, pl.ds(inner + LANES, LANES)]))

    def fold_columns(step, carry):
        chunk, _ = chunk_at(step)
        steps = chunk.steps()
        kept_memory[step] = memory[...]
        before[step] = total[...]
        kept_steps[step] = steps

        def keep_values(pair):
            values = chunk.values(pair)
            outputs[step, :, pl.ds(pair * LANES, LANES)] = values
            return values

        logs[step] = fold_chunk(
            keep_values, chunk.keys(), steps, rate, chunk.earlier(), head_size, memory, total
        )
        return carry

    def output_columns(step, carry):
        chunk, queries = chunk_at(step)
        running_bits = logs[step] * LOG2_E
        across = jnp.transpose(running_bits)
        scores = score_matrix(queries, split(jnp.transpose(chunk.keys())), chunk.earlier())
        steps = kept_steps[step]
        for pair in range(chunk.pairs):
            lanes = pl.ds(pair * LANES, LANES)
            scaled = split(outputs[step, :, lanes] * spread(steps, pair, head_size))
            outputs[step, :, lanes] = within_pair(
                pair, scaled, running_bits, across, scores, head_size
            )

        @pl.when(step == 2)
        def _():
            scan(1, True)

        @pl.when(step == 3)
        def _():
            scan(0, False)

        return carry

    def correct(step, carry):
        _, queries = chunk_at(step)
        arrived = jnp.exp(logs[step])
        decayed = jnp.exp(before[step][0:1])
        first = pl.multiple_of((chunks - 1 - step) * part_rows, 16)
        here = rows_iota((16, LANES)) == chunks - 1 - step
        for pair in range(inner // LANES):
            lanes = pl.ds(pair * LANES, LANES)
            entering = entering_backward_ref[:, lanes] * spread(decayed, pair, head_size)
            added = carried(queries, kept_memory[step, :, lanes] + entering)
            result = outputs[step, :, lanes] + added * spread(arrived, pair, head_size)
            scale, factor = code_scale(jnp.max(jnp.abs(result), axis=0, keepdims=True))
            out_ref[:, pl.ds(first, part_rows), lanes] = encode(result * factor).reshape(
                4, part_rows, LANES
            )
            scales_ref[:, lanes] = jnp.where(here, scale.astype(F32), scales_ref[:, lanes])
        return carry

    lax.fori_loop(0, chunks, fold_columns, 0)
    send_slices(1, memory, total)
    scales_ref[...] = jnp.zeros_like(scales_ref)
    lax.fori_loop(0, chunks, output_columns, 0)
    finish_way(1, entering_backward_ref)
    lax.fori_loop(0, chunks, correct, 0)
    for k in range(4):
        out_ref[k, pl.ds(last, 16), :] = scales_ref[...].astype(BF16)
    finish_way(0, entering_forward_ref)


def column_output(columns, rate, memory, total, inner, size, column_rows, head_size):
    spatial = lax.axis_size("spatial")
    count = lax.axis_size("frame") * spatial
    slices = (2, count, LANES * 4 // count, inner // 4 + LANES)
    chunks = (columns.shape[1] - 16) * 4 // size
    vmem = pl.BlockSpec(memory_space=pltpu.VMEM)
    dma = pltpu.SemaphoreType.DMA
    geometry = (inner, size, column_rows, head_size, count, spatial)
    return pl.pallas_call(
        functools.partial(states_kernel, geometry),
        in_specs=[vmem] * 4,
        out_specs=[vmem, vmem],
        out_shape=[
            jax.ShapeDtypeStruct((LANES, inner), F32),
            jax.ShapeDtypeStruct(columns.shape[:2] + (inner,), BF16),
        ],
        scratch_shapes=[
            pltpu.VMEM((LANES, inner), F32),
            pltpu.VMEM((chunks, size, inner), F32),
            pltpu.VMEM((chunks, size, LANES), F32),
            pltpu.VMEM((chunks, 8, LANES), F32),
            pltpu.VMEM((16, inner), F32),
            pltpu.VMEM((chunks, LANES, inner), F32),
            pltpu.VMEM((chunks, size, LANES), F32),
            pltpu.VMEM((LANES, inner), F32),
            pltpu.VMEM((8, LANES), F32),
            pltpu.VMEM(slices, BF16),
            pltpu.VMEM(slices, BF16),
            pltpu.VMEM(slices, BF16),
            pltpu.VMEM(slices, BF16),
            dma((2, count)),
            dma((2, count)),
            dma((2, count)),
            dma((2, count)),
        ],
        compiler_params=pltpu.CompilerParams(
            collective_id=1, has_side_effects=True, vmem_limit_bytes=VMEM_BYTES
        ),
    )(columns, rate, memory, total)


def finish_kernel(head_size, groups, part, forward_ref, backward_ref, gate_ref, gain_ref, out_ref, moved_ref):
    col_total = forward_ref.shape[0] // 4
    quad = pl.program_id(0)
    last = backward_ref.shape[1] - 16
    scales = [backward_ref[k, pl.ds(last, 16), :].astype(F32) * (1.0 / CODE_TOP) for k in range(4)]

    def group_rows(group):
        piece, within = group // groups, group % groups
        first = pl.multiple_of(within * part + 16 * quad, 16)
        coded = backward_ref[piece, pl.ds(first, 16), :]
        return decode(coded) * scales[piece][within : within + 1, :]

    for at in range(col_total // 8):
        even, odd = group_rows(2 * at), group_rows(2 * at + 1)
        for k in (0, 1):
            low_half, high_half = even[8 * k : 8 * k + 8], odd[8 * k : 8 * k + 8]
            first, second = column_groups(low_half, high_half)
            moved_ref[pl.ds(2 * k * col_total + 8 * at, 8), :] = first
            moved_ref[pl.ds((2 * k + 1) * col_total + 8 * at, 8), :] = second
    wide = 2 * LANES
    same = rows_iota((wide, wide)) // head_size == lanes_iota((wide, wide)) // head_size
    ones = jnp.where(same, 1.0, 0.0).astype(BF16)
    for block in range(forward_ref.shape[1] // wide):
        lanes = pl.ds(block * wide, wide)
        gate = gate_ref[:, lanes]
        combined = forward_ref[:, lanes] + moved_ref[:, lanes]
        gated = combined * (gate / (1.0 + jnp.exp(-gate)))
        high, low = split(gated * gated)
        mean = (dot(high, ones) + dot(low, ones)) * (1.0 / head_size)
        normed = gated * lax.rsqrt(mean + 1e-5) * gain_ref[:, lanes]
        out_ref[:, lanes] = normed.astype(out_ref.dtype)


def finish(forward, backward, gate, gain, row_part, col_total, head_size):
    tokens, inner = forward.shape
    groups = col_total // GROUP // 4
    block = 4 * col_total
    flat = pl.BlockSpec((block, inner), lambda m: (m, 0))
    return pl.pallas_call(
        functools.partial(finish_kernel, head_size, groups, row_part * GROUP),
        grid=(row_part // 4,),
        in_specs=[flat, whole(backward.shape), flat, whole((1, inner))],
        out_specs=flat,
        out_shape=jax.ShapeDtypeStruct((tokens, inner), BF16),
        scratch_shapes=[pltpu.VMEM((block, inner), F32)],
        compiler_params=params(),
    )(forward, backward, gate, gain)


def local(tokens, xz_weight, state_weight, step_weight, step_bias, decay_rate, skip, norm_gain):
    videos, frame_count, row_part, col_total, width = tokens.shape
    flattened = tokens.reshape(-1, width)
    inner = xz_weight.shape[1] // 2
    heads = step_weight.shape[1]
    head_size = inner // heads
    column_rows = row_part * lax.axis_size("spatial")
    size = column_rows * GROUP
    axes = ("frame", "spatial")

    skips = jnp.repeat(skip[0] + skip[1], head_size)[None]

    values, keys, columns, memory, total, gate_weight, kept, before = project(
        flattened,
        state_weight,
        step_weight,
        step_bias[None],
        decay_rate,
        xz_weight,
        row_part,
        col_total,
        inner,
        head_size,
        512,
    )
    entering, backward = column_output(
        columns, decay_rate, memory, total, inner, size, column_rows, head_size
    )
    returned = lax.all_to_all(backward, "spatial", 0, 0, tiled=True)
    forward = row_output(
        values[None], keys[None], kept, before, decay_rate, entering, skips, inner, size, head_size
    )
    gate_weight, forward = lax.optimization_barrier((gate_weight, forward))
    gate_rows = gate_rows_of(flattened, gate_weight, xz_weight.shape[0])
    normed = finish(
        forward[0], returned, gate_rows, norm_gain[None], row_part, col_total, head_size
    )
    return normed.reshape(videos, frame_count, row_part, col_total, inner)


def solution(mesh):
    in_specs = (
        P("dp", "frame", "spatial", None, None),
        P(("spatial", "dp"), None),
        P(("spatial", "dp"), None),
        P(("spatial", "dp"), None),
        P(),
        P(),
        P(),
        P(),
    )
    out_specs = P("dp", "frame", "spatial", None, None)
    return jax.shard_map(local, mesh=mesh, in_specs=in_specs, out_specs=out_specs, check_vma=False)
```
